32 devices in a mesh: dp: 4 (over y, x), seq: 4 (over z), tensor: 2 (over core).
Axes of the slice: x: 2, y: 2, z: 4, core: 2. Of those that a mesh axis runs over, the one named last changes fastest.
Arguments:
- inputs: bfloat16 [2048, 3584], P(('dp', 'seq'), 'tensor'), parts along dimension 0, may hold values from -6 to 6
- cotangent: bfloat16 [2048, 3584], P(('dp', 'seq'), 'tensor'), parts along dimension 0, may hold values from -6 to 6
- norm_gain: float32 [2, 3584], replicated, may hold values from 0.25 to 1.75
- head_gain: float32 [2, 2, 128], replicated, may hold values from 0.5 to 2.5
- query_weight: bfloat16 [2, 3584, 2048], P(None, None, 'tensor'), may hold values from -0.09375 to 0.09375
- key_weight: bfloat16 [2, 3584, 1024], P(None, None, 'tensor'), may hold values from -0.09375 to 0.09375
- output_weight: bfloat16 [2, 2048, 3584], P(None, 'tensor'), may hold values from -0.375 to 0.375
- modality: int32 [2048], P(('dp', 'seq')), parts along dimension 0, may hold values 0 or 1
- segments: int32 [2048], P('dp'), parts along dimension 0, may hold values from 0 to 63, never falling along the last dimension, each value on 1 to 256 neighbouring positions
- block_order: int32 [16], P('dp'), parts along dimension 0, may hold values from 0 to 3, each once
Outputs:
- attention_out: bfloat16 [2048, 3584], P(('dp', 'seq'), 'tensor'), parts along dimension 0
- grad_input: bfloat16 [2048, 3584], P(('dp', 'seq'), 'tensor'), parts along dimension 0
The draws below stay inside these ranges and needn't reach their ends.
There are 4 independent parts, one for each index of `dp`. The reference program is written for one: setup_inputs(seed, part) draws one part's arguments, and reference() takes and returns one part's arrays. A program takes and returns all parts, laid end to end along the dimension named above; an argument that names none is the same for every part. Nothing has to cross between parts.
Inputs may be any that keep to these rules, and one draw needn't show every extreme that they name: `modality`: 1 marks an image token, 0 a text token. `segments`: never falls along the sequence; each segment covers 1 to 256 positions and one covers exactly 256. `block_order`: each block appears once.
All inputs are finite; a program needn't handle non-finite values. No bound on the sum of `modality` on one device may be relied on, other than what follows from the above.
Results may differ from the reference program's by a relative error of at most 0.022.
Values may be sent and summed in bfloat16 or wider, within the bound.
No kernel may reach another device: no remote copies, remote signals or barrier semaphores. Data moves between devices by JAX's collectives and lax.ppermute only.
A program may use at most 128 MiB of HBM per device.

```python
import math
import jax
import jax.numpy as jnp
import numpy as np
from jax import lax

D = 3584
HEADS = 16
KV_HEADS = 4
HEAD_DIM = 128
GROUP = 4
TOK_DEV = 128
TOKENS = 512
BLOCKS = 4
SEGS = 64
SEG_MOST = 256


def place_ends(drawn, own_key, low, largest):
    extent = drawn.shape
    place = [jax.random.randint(jax.random.fold_in(own_key, axis), (), 0, extent[axis]) for axis in range(len(extent))]
    drawn = drawn.at[tuple(place)].set(low)
    longest = extent.index(max(extent))
    place[longest] = (place[longest] + 1) % extent[longest]
    return drawn.at[tuple(place)].set(largest)


def block_scale(rng, shape, pieces, low, largest):
    factor_of, own = 1.0, jax.random.fold_in(rng, 6)
    for position, parts in pieces:
        steps = jnp.exp(jax.random.uniform(jax.random.fold_in(own, position), (parts,), jnp.float32, low / len(pieces), largest / len(pieces)))
        factor_of = factor_of * jnp.repeat(steps, shape[position] // parts).reshape([-1 if axis == position else 1 for axis in range(len(shape))])
    return factor_of


def length_profile(number_of, total, most, slope):
    portions = [(1 << 20) // math.isqrt(rank ** slope) + 1 for rank in range(2, number_of + 1)]
    spare, given = total - most - (number_of - 1), [1] * (number_of - 1)
    while spare > 0:
        candidates = [i for i in range(number_of - 1) if given[i] < most]
        pool, left = sum([portions[i] for i in candidates]), spare
        for i in candidates:
            more = min(most - given[i], max(1, left * portions[i] // pool), spare)
            given[i] = given[i] + more
            spare = spare - more
    return np.array([most] + given)


def uneven(stream_key, number_of, total, most, lean):
    if number_of == 2:
        one = jax.random.randint(stream_key, (), max(1, total - most), min(most, total - 1) + 1)
        return jnp.stack([one, total - one])
    sizes = jnp.asarray(length_profile(number_of, total, most, lean), jnp.int32)
    pairs = (number_of - 1) // 2
    donor, receiver = sizes[1:1 + 2 * pairs:2], sizes[2:2 + 2 * pairs:2]
    margin = jnp.minimum(donor - 1, most - receiver)
    passed = jax.random.randint(jax.random.fold_in(stream_key, 1), (pairs,), 0, 1 << 20) % (margin + 1)
    sizes = sizes.at[1:1 + 2 * pairs:2].set(donor - passed).at[2:2 + 2 * pairs:2].set(receiver + passed)
    return sizes[jax.random.permutation(jax.random.fold_in(stream_key, 2), number_of)]


def centred(stream_key, shape, width, most, split=(), kind=jnp.bfloat16):
    drawn = jax.random.normal(stream_key, shape, jnp.float32) * width
    if len(split) > 0:
        drawn = block_scale(stream_key, shape, split, -0.22, 0.18) * drawn
    return jnp.clip(drawn, min=-most, max=most).astype(kind)


def setup_inputs(seed: int = 0, part: int = 0) -> dict:
    key_of = jax.random.split(jax.random.key(seed), 11)
    part_splits = jax.random.split(jax.random.fold_in(key_of[10], part), 11)
    return {
        "inputs": centred(part_splits[0], (TOKENS, D), 1.0, 6.0, ((0, 4), (1, 2))),
        "cotangent": centred(part_splits[1], (TOKENS, D), 1.0, 6.0, ((0, 4), (1, 2))),
        "norm_gain": jnp.clip(1.0 + 0.15 * jax.random.normal(key_of[2], (2, D), jnp.float32), 0.25, 1.75),
        "head_gain": jnp.clip(jnp.exp(jax.random.uniform(key_of[3], (2, 2, HEAD_DIM), jnp.float32, math.log(0.5), math.log(2.5))), 0.5, 2.5),
        "query_weight": centred(key_of[4], (2, D, HEADS * HEAD_DIM), D ** -0.5, 0.09375, ((2, 2),)),
        "key_weight": centred(key_of[5], (2, D, 2 * KV_HEADS * HEAD_DIM), D ** -0.5, 0.09375, ((2, 2),)),
        "output_weight": centred(key_of[6], (2, HEADS * HEAD_DIM, D), (HEADS * HEAD_DIM // 8) ** -0.5, 0.375, ((1, 2),)),
        "modality": place_ends((jax.random.randint(part_splits[7], (TOKENS,), 0, 2) < 1).astype(jnp.int32), jax.random.fold_in(part_splits[7], 1), 0, 1),
        "segments": jnp.searchsorted(jnp.cumsum(uneven(part_splits[8], SEGS, TOKENS, SEG_MOST, 2)), jnp.arange(TOKENS), side="right").astype(jnp.int32),
        "block_order": jax.random.permutation(part_splits[9], BLOCKS).astype(jnp.int32),
    }


epsilon = 1e-06

def row_norm(values, scaling):
    factor = lax.rsqrt(lax.optimization_barrier(jnp.mean(values * values, axis=-1, keepdims=True)) + epsilon)
    return (values * factor * scaling, factor)

def norm_back(values, factor, scaling, upstream):
    unit_rows = values * factor
    inner_mean = lax.optimization_barrier(jnp.mean(scaling * upstream * unit_rows, axis=-1, keepdims=True))
    return factor * (scaling * upstream - unit_rows * inner_mean)

def expert_pick(is_image, weights, operand):
    text_part = jnp.dot(operand, weights[0], preferred_element_type=jnp.float32)
    image_part = jnp.dot(operand, weights[1], preferred_element_type=jnp.float32)
    return jnp.where(is_image, image_part, text_part)

def expert_back(is_image, weights, operand):
    text_part = jnp.dot(operand, weights[0].T, preferred_element_type=jnp.float32)
    image_part = jnp.dot(operand, weights[1].T, preferred_element_type=jnp.float32)
    return jnp.where(is_image, image_part, text_part)

def reference(inputs, cotangent, norm_gain, head_gain, query_weight, key_weight, output_weight, modality, segments, block_order):
    total_rows = inputs.shape[0]
    score_scale = 1.0 / math.sqrt(HEAD_DIM)
    positions = jnp.arange(total_rows, dtype=jnp.int32)
    anchor = block_order[positions // TOK_DEV] * TOK_DEV + positions % TOK_DEV
    row_segments = segments[anchor]
    visible = row_segments[None, :] <= row_segments[:, None]
    is_image = (modality == 1)[:, None]
    head_image = is_image[:, :, None]
    rows_float = inputs.astype(jnp.float32)
    row_scaling = jnp.where(is_image, norm_gain[1][None, :], norm_gain[0][None, :])
    normed, row_factor = row_norm(rows_float, row_scaling)
    normed = normed.astype(jnp.bfloat16)
    query_raw = expert_pick(is_image, query_weight, normed).reshape(total_rows, HEADS, HEAD_DIM)
    query_scaling = jnp.where(head_image, head_gain[1, 0], head_gain[0, 0])
    query_normed, query_factor = row_norm(query_raw, query_scaling)
    query_normed = query_normed.astype(jnp.bfloat16)
    pair_raw = expert_pick(is_image, key_weight, normed).reshape(total_rows, KV_HEADS, 2, HEAD_DIM)
    key_raw = pair_raw[:, :, 0]
    value_rows = pair_raw[:, :, 1].astype(jnp.bfloat16)
    key_scaling = jnp.where(head_image, head_gain[1, 1], head_gain[0, 1])
    key_normed, key_factor = row_norm(key_raw, key_scaling)
    key_normed = key_normed.astype(jnp.bfloat16)
    head_keys = jnp.repeat(key_normed, GROUP, axis=1).transpose(1, 0, 2)
    head_values = jnp.repeat(value_rows, GROUP, axis=1).transpose(1, 0, 2)
    head_queries = query_normed.transpose(1, 0, 2)

    def weights_of(query_head, key_head):
        scores = jnp.dot(query_head, key_head.T, preferred_element_type=jnp.float32) * score_scale
        return jnp.where(visible, jnp.exp(scores), 0.0).astype(jnp.bfloat16)

    def forward_head(operands):
        query_head, key_head, value_head = operands
        weights = weights_of(query_head, key_head)
        denominator = lax.optimization_barrier(jnp.sum(weights.astype(jnp.float32), axis=1))
        numerator = jnp.dot(weights, value_head, preferred_element_type=jnp.float32)
        return ((numerator / denominator[:, None]).astype(jnp.bfloat16), denominator)
    attended, denominator = lax.map(forward_head, (head_queries, head_keys, head_values))
    attended_rows = attended.transpose(1, 0, 2).reshape(total_rows, HEADS * HEAD_DIM)
    attention_out = expert_pick(is_image, output_weight, attended_rows).astype(jnp.bfloat16)
    back_attended = expert_back(is_image, output_weight, cotangent).astype(jnp.bfloat16)
    head_backs = back_attended.reshape(total_rows, HEADS, HEAD_DIM).transpose(1, 0, 2)
    offset = lax.optimization_barrier(jnp.sum(head_backs.astype(jnp.float32) * attended.astype(jnp.float32), axis=2))

    def backward_head(operands):
        query_head, key_head, value_head, back_head, total_head, offset_head = operands
        weights = weights_of(query_head, key_head)
        probability = (weights.astype(jnp.float32) / total_head[:, None]).astype(jnp.bfloat16)
        back_prob = jnp.dot(back_head, value_head.T, preferred_element_type=jnp.float32)
        back_score = (probability.astype(jnp.float32) * (back_prob - offset_head[:, None])).astype(jnp.bfloat16)
        back_query = jnp.dot(back_score, key_head, preferred_element_type=jnp.float32) * score_scale
        back_key = jnp.dot(back_score.T, query_head, preferred_element_type=jnp.float32) * score_scale
        back_value = jnp.dot(probability.T, back_head, preferred_element_type=jnp.float32)
        return (back_query, back_key, back_value)
    back_query, back_key, back_value = lax.map(backward_head, (head_queries, head_keys, head_values, head_backs, denominator, offset))
    back_key = back_key.reshape(KV_HEADS, GROUP, total_rows, HEAD_DIM).sum(axis=1).transpose(1, 0, 2)
    back_value = back_value.reshape(KV_HEADS, GROUP, total_rows, HEAD_DIM).sum(axis=1).transpose(1, 0, 2)
    query_back = norm_back(query_raw, query_factor, query_scaling, back_query.transpose(1, 0, 2)).astype(jnp.bfloat16)
    key_back = norm_back(key_raw, key_factor, key_scaling, back_key).astype(jnp.bfloat16)
    pair_back = jnp.stack([key_back, back_value.astype(jnp.bfloat16)], axis=2).reshape(total_rows, 2 * KV_HEADS * HEAD_DIM)
    back_normed = expert_back(is_image, query_weight, query_back.reshape(total_rows, HEADS * HEAD_DIM)) + expert_back(is_image, key_weight, pair_back)
    grad_input = norm_back(rows_float, row_factor, row_scaling, back_normed).astype(jnp.bfloat16)
    return (attention_out, grad_input)
```

```python
import functools
import math

import jax
import jax.numpy as jnp
from jax import lax
from jax.experimental import pallas as pl
from jax.experimental.pallas import tpu as pltpu
from jax.sharding import PartitionSpec as P

KV_HEADS = 4
HEAD_DIM = 128

epsilon = 1e-06
bf16 = jnp.bfloat16
f32 = jnp.float32


def inverse_norm(values):
    return lax.rsqrt(jnp.mean(values * values, axis=-1, keepdims=True) + epsilon)


def norm_back(values, factor, scaling, upstream):
    unit_rows = values * factor
    inner_mean = jnp.mean(scaling * upstream * unit_rows, axis=-1, keepdims=True)
    return factor * (scaling * upstream - unit_rows * inner_mean)


def seq_pairs(step, count):
    if count & (count - 1) == 0:
        return [(i, i ^ step) for i in range(count)]
    return [(i, (i + step) % count) for i in range(count)]


def seq_source(rank, step, count):
    if count & (count - 1) == 0:
        return rank ^ step
    return (rank - step) % count


def inverted(pairs):
    return [(b, a) for a, b in pairs]


def expert_pick(is_image, weights, operand):
    zero = jnp.zeros_like(operand)
    masked = jnp.concatenate(
        [jnp.where(is_image, zero, operand), jnp.where(is_image, operand, zero)], axis=1
    )
    flat = weights.reshape(-1, weights.shape[2])
    return jnp.dot(masked, flat, preferred_element_type=f32)


def expert_back(is_image, weights, operand):
    text_part = lax.dot_general(
        operand, weights[0], (((1,), (1,)), ((), ())), preferred_element_type=f32
    )
    image_part = lax.dot_general(
        operand, weights[1], (((1,), (1,)), ((), ())), preferred_element_type=f32
    )
    return jnp.where(is_image, image_part, text_part)


def dot_nt(a, b):
    return lax.dot_general(a, b, (((1,), (1,)), ((), ())), preferred_element_type=f32)


def dot_tn(a, b):
    return lax.dot_general(a, b, (((0,), (0,)), ((), ())), preferred_element_type=f32)


def attention_kernel(blocks, per_group, *refs):
    source_ref, segments_ref, query_ref, back_ref = refs[:4]
    memory_refs = refs[4 : 4 + blocks]
    attended_ref, back_query_ref = refs[4 + blocks : 6 + blocks]
    grad_refs = refs[6 + blocks :]
    rows = query_ref.shape[0]
    scale = 1.0 / math.sqrt(HEAD_DIM)

    def heads(ref):
        return jnp.concatenate(
            [ref[:, h * HEAD_DIM : (h + 1) * HEAD_DIM] for h in range(per_group)], axis=0
        )

    query, back = heads(query_ref), heads(back_ref)
    key = jnp.concatenate([m[:, :HEAD_DIM] for m in memory_refs], axis=0)
    value = jnp.concatenate([m[:, HEAD_DIM:] for m in memory_refs], axis=0)
    key_segments = jnp.concatenate(
        [segments_ref[pl.ds(source_ref[b], 1), :] for b in range(blocks)], axis=1
    )
    own = segments_ref[pl.ds(source_ref[0], 1), :]
    query_segments = jnp.broadcast_to(own.astype(f32), (rows, rows)).T[:, :1]
    visible = key_segments.astype(f32) <= query_segments
    visible = jnp.where(visible, 1.0, 0.0)
    visible = jnp.concatenate([visible] * per_group, axis=0)
    scores = dot_nt(query, key) * scale
    weights = jnp.where(visible > 0.0, jnp.exp(scores), 0.0).astype(bf16)
    weights32 = weights.astype(f32)
    denominator = jnp.sum(weights32, axis=1, keepdims=True)
    numerator = jnp.dot(weights, value, preferred_element_type=f32)
    attended = (numerator / denominator).astype(bf16)
    offset = jnp.sum(back.astype(f32) * attended.astype(f32), axis=1, keepdims=True)
    probability = (weights32 / denominator).astype(bf16)
    back_prob = dot_nt(back, value)
    back_score = (probability.astype(f32) * (back_prob - offset)).astype(bf16)
    back_query = jnp.dot(back_score, key, preferred_element_type=f32) * scale
    back_key = dot_tn(back_score, query) * scale
    back_value = dot_tn(probability, back)
    for h in range(per_group):
        part = slice(h * rows, (h + 1) * rows)
        columns = slice(h * HEAD_DIM, (h + 1) * HEAD_DIM)
        attended_ref[:, columns] = attended[part]
        back_query_ref[:, columns] = back_query[part]
    for b in range(blocks):
        part = slice(b * rows, (b + 1) * rows)
        grad_refs[b][:, :HEAD_DIM] = back_key[part].astype(grad_refs[b].dtype)
        grad_refs[b][:, HEAD_DIM:] = back_value[part].astype(grad_refs[b].dtype)


def attention(sources, segments, query, back, memories):
    rows, width = query.shape
    blocks = len(memories)
    pairs = memories[0].shape[1] // (2 * HEAD_DIM)
    per_group = width // HEAD_DIM // pairs
    wide = pl.BlockSpec((rows, per_group * HEAD_DIM), lambda g: (0, g))
    narrow = pl.BlockSpec((rows, 2 * HEAD_DIM), lambda g: (0, g))
    outs = [
        jax.ShapeDtypeStruct((rows, width), bf16),
        jax.ShapeDtypeStruct((rows, width), f32),
    ] + [
        jax.ShapeDtypeStruct((rows, pairs * 2 * HEAD_DIM), f32 if b == 0 else bf16)
        for b in range(blocks)
    ]
    return pl.pallas_call(
        functools.partial(attention_kernel, blocks, per_group),
        grid=(pairs,),
        out_shape=outs,
        in_specs=[
            pl.BlockSpec(memory_space=pltpu.SMEM),
            pl.BlockSpec(segments.shape, lambda g: (0, 0)),
            wide,
            wide,
        ]
        + [narrow] * blocks,
        out_specs=[wide, wide] + [narrow] * blocks,
        compiler_params=pltpu.CompilerParams(vmem_limit_bytes=40 * 1024 * 1024),
        cost_estimate=pl.CostEstimate(
            flops=12 * rows * rows * blocks * width,
            bytes_accessed=rows * width * 10,
            transcendentals=rows * rows * blocks * width // HEAD_DIM,
        ),
        name="attention",
    )(sources, segments, query, back, *memories)


def local(
    inputs,
    cotangent,
    norm_gain,
    head_gain,
    query_weight,
    key_weight,
    output_weight,
    modality,
    segments,
    block_order,
):
    tensor_rank = lax.axis_index("tensor")
    block_rank = lax.axis_index("seq")
    tensor_count = lax.axis_size("tensor")
    block_count = lax.axis_size("seq")
    local_rows = inputs.shape[0]
    local_width = inputs.shape[1]
    full_width = local_width * tensor_count
    swap = [(0, 1), (1, 0)]

    def spread(part):
        if tensor_count != 2:
            return lax.all_gather(part, "tensor", axis=1, tiled=True)
        other = lax.ppermute(part, "tensor", swap)
        first = tensor_rank == 0
        return jnp.concatenate(
            [jnp.where(first, part, other), jnp.where(first, other, part)], axis=1
        )

    def reduce_columns(part):
        if tensor_count != 2:
            return lax.psum_scatter(
                part.astype(bf16), "tensor", scatter_dimension=1, tiled=True
            ).astype(f32)
        first = tensor_rank == 0
        low, high = part[:, :local_width], part[:, local_width:]
        other = lax.ppermute(jnp.where(first, high, low).astype(bf16), "tensor", swap)
        return jnp.where(first, low, high) + other.astype(f32)

    whole_rows = lax.all_gather(inputs, "tensor", axis=1, tiled=True)
    is_image = (modality == 1)[:, None]
    head_image = is_image[:, :, None]
    row_scaling = jnp.where(is_image, norm_gain[1][None, :], norm_gain[0][None, :])
    rows_float = whole_rows.astype(f32)
    row_factor = inverse_norm(rows_float)
    normed = (rows_float * row_factor * row_scaling).astype(bf16)

    slice_blocks = key_weight.shape[2] // HEAD_DIM
    key_raw = expert_pick(is_image, key_weight, normed).reshape(local_rows, slice_blocks, HEAD_DIM)
    block_index = tensor_rank * slice_blocks + jnp.arange(slice_blocks, dtype=jnp.int32)
    is_key = (block_index % 2 == 0)[None, :, None]
    key_scaling = jnp.where(head_image, head_gain[1, 1], head_gain[0, 1])
    key_factor = inverse_norm(key_raw)
    slice_out = jnp.where(is_key, key_raw * key_factor * key_scaling, key_raw).astype(bf16)
    slice_out = slice_out.reshape(local_rows, slice_blocks * HEAD_DIM)
    shared = tensor_count > KV_HEADS
    is_even = tensor_rank % 2 == 0
    if shared:
        pair_swap = [(i, i ^ 1) for i in range(tensor_count)]
        partner = lax.ppermute(slice_out, "tensor", pair_swap)
        memory = jnp.where(
            is_even,
            jnp.concatenate([slice_out, partner], 1),
            jnp.concatenate([partner, slice_out], 1),
        )
    else:
        memory = slice_out
    memories, order = [memory], [block_rank]
    for step in range(1, block_count):
        memories.append(lax.ppermute(memory, "seq", seq_pairs(step, block_count)))
        order.append(seq_source(block_rank, step, block_count))
    sources = block_order[jnp.stack(order)]

    query_heads = query_weight.shape[2] // HEAD_DIM
    query_raw = expert_pick(is_image, query_weight, normed).reshape(
        local_rows, query_heads, HEAD_DIM
    )
    query_scaling = jnp.where(head_image, head_gain[1, 0], head_gain[0, 0])
    query_factor = inverse_norm(query_raw)
    query_normed = (query_raw * query_factor * query_scaling).astype(bf16)
    query_normed = query_normed.reshape(local_rows, query_heads * HEAD_DIM)

    back_attended = expert_back(is_image, output_weight, spread(cotangent)).astype(bf16)

    attended, back_query, own_grad, *grads = attention(
        sources,
        segments.reshape(block_count, local_rows),
        query_normed,
        back_attended,
        memories,
    )
    incoming = [
        lax.ppermute(grad, "seq", inverted(seq_pairs(step, block_count)))
        for step, grad in enumerate(grads, 1)
    ]

    output_part = expert_pick(is_image, output_weight, attended)
    attention_out = reduce_columns(output_part).astype(bf16)

    query_back = norm_back(
        query_raw,
        query_factor,
        query_scaling,
        back_query.reshape(local_rows, query_heads, HEAD_DIM),
    ).astype(bf16)
    inner_query = jnp.sum(query_back.astype(f32) * query_raw, axis=(1, 2))
    gradient_part = expert_back(
        is_image, query_weight, query_back.reshape(local_rows, query_heads * HEAD_DIM)
    )

    memory_sum = own_grad + sum(grad.astype(f32) for grad in incoming)
    if shared:
        low, high = memory_sum[:, :HEAD_DIM], memory_sum[:, HEAD_DIM:]
        outgoing = jnp.where(is_even, high, low).astype(bf16)
        slice_grad = jnp.where(is_even, low, high) + lax.ppermute(
            outgoing, "tensor", pair_swap
        ).astype(f32)
    else:
        slice_grad = memory_sum
    slice_grad = slice_grad.reshape(local_rows, slice_blocks, HEAD_DIM)
    slice_back = jnp.where(
        is_key, norm_back(key_raw, key_factor, key_scaling, slice_grad), slice_grad
    ).astype(bf16)
    inner = inner_query + jnp.sum(slice_back.astype(f32) * key_raw, axis=(1, 2))
    if tensor_count == 2:
        inner_total = inner + lax.ppermute(inner, "tensor", swap)
    else:
        inner_total = lax.psum(inner, "tensor")
    gradient_part = gradient_part + expert_back(
        is_image, key_weight, slice_back.reshape(local_rows, slice_blocks * HEAD_DIM)
    )
    back_normed = reduce_columns(gradient_part)
    local_scaling = lax.dynamic_slice_in_dim(
        row_scaling, tensor_rank * local_width, local_width, 1
    )
    unit_rows = inputs.astype(f32) * row_factor
    grad_input = (
        row_factor * (local_scaling * back_normed - unit_rows * (inner_total / full_width)[:, None])
    ).astype(bf16)
    return (attention_out, grad_input)


def solution(mesh):
    return jax.shard_map(
        local,
        mesh=mesh,
        in_specs=(
            P(("dp", "seq"), "tensor"),
            P(("dp", "seq"), "tensor"),
            P(),
            P(),
            P(None, None, "tensor"),
            P(None, None, "tensor"),
            P(None, "tensor", None),
            P(("dp", "seq")),
            P("dp"),
            P("dp"),
        ),
        out_specs=(P(("dp", "seq"), "tensor"), P(("dp", "seq"), "tensor")),
        check_vma=False,
    )
```

```python
import functools
import math

import jax
import jax.numpy as jnp
from jax import lax
from jax.experimental import pallas as pl
from jax.experimental.pallas import tpu as pltpu
from jax.sharding import PartitionSpec as P

KV_HEADS = 4
HEAD_DIM = 128
MIB = 1024 * 1024

epsilon = 1e-06
bf16 = jnp.bfloat16
f32 = jnp.float32
SMEM = pl.BlockSpec(memory_space=pltpu.SMEM)


def seq_pairs(step, count):
    if count & (count - 1) == 0:
        return [(i, i ^ step) for i in range(count)]
    return [(i, (i + step) % count) for i in range(count)]


def seq_source(rank, step, count):
    if count & (count - 1) == 0:
        return rank ^ step
    return (rank - step) % count


def inverted(pairs):
    return [(b, a) for a, b in pairs]


def tile_of(extent, most):
    best = HEAD_DIM
    for size in range(HEAD_DIM, min(extent, most) + 1, HEAD_DIM):
        if extent % size == 0:
            best = size
    return best


def dot_nt(a, b):
    return lax.dot_general(a, b, (((1,), (1,)), ((), ())), preferred_element_type=f32)


def dot_tn(a, b):
    return lax.dot_general(a, b, (((0,), (0,)), ((), ())), preferred_element_type=f32)


def column(row):
    count = row.shape[1]
    return jnp.broadcast_to(row.astype(f32), (count, count)).T[:, :1]


def row_of(col):
    count = col.shape[0]
    return jnp.broadcast_to(col, (count, count)).T[:1, :]


def inverse_norm(values):
    return lax.rsqrt(jnp.mean(values * values, axis=-1, keepdims=True) + epsilon)


def norm_back(values, factor, scaling, upstream):
    unit_rows = values * factor
    inner_mean = jnp.mean(scaling * upstream * unit_rows, axis=-1, keepdims=True)
    return factor * (scaling * upstream - unit_rows * inner_mean)


def whole(shape):
    return pl.BlockSpec(shape, lambda *_: (0,) * len(shape))


def params(mib):
    return pltpu.CompilerParams(vmem_limit_bytes=mib * MIB)


def cost(micros):
    return pl.CostEstimate(
        flops=int(micros * 1e9), bytes_accessed=int(micros * 2e6), transcendentals=0
    )


def in_order(rank, part_refs):
    if len(part_refs) == 1:
        return part_refs[0][...]
    own, other = part_refs[0][...], part_refs[1][...]
    first = rank == 0
    return jnp.concatenate([jnp.where(first, own, other), jnp.where(first, other, own)], axis=1)


def both_experts(image, rows, weights):
    zero = jnp.zeros_like(rows)
    masked = jnp.concatenate([jnp.where(image, zero, rows), jnp.where(image, rows, zero)], axis=1)
    flat = weights.reshape(2 * weights.shape[1], weights.shape[2])
    return jnp.dot(masked, flat, preferred_element_type=f32)


def both_back(image, rows, weights):
    return jnp.where(image, dot_nt(rows, weights[1]), dot_nt(rows, weights[0]))


def key_kernel(count, chunk, *refs):
    rank_ref, modality_ref, gain_ref, head_ref, weight_ref = refs[:5]
    part_refs = refs[5 : 5 + count]
    memory_ref, raw_ref, normed_ref, factor_ref, total = refs[5 + count :]
    step = pl.program_id(0)
    image = column(modality_ref[...]) > 0.0

    @pl.when(step == 0)
    def _():
        rows = in_order(rank_ref[0], part_refs).astype(f32)
        factor = inverse_norm(rows)
        scaling = jnp.where(image, gain_ref[1:2, :], gain_ref[0:1, :])
        normed_ref[...] = (rows * factor * scaling).astype(bf16)
        factor_ref[...] = row_of(factor)
        total[...] = jnp.zeros_like(total)

    columns = pl.ds(pl.multiple_of(step * chunk, HEAD_DIM), chunk)
    total[...] += both_experts(image, normed_ref[:, columns], weight_ref[...])

    @pl.when(step == pl.num_programs(0) - 1)
    def _():
        blocks = total.shape[1] // HEAD_DIM
        scaling = jnp.where(image, head_ref[1, 1:2, :], head_ref[0, 1:2, :])
        raw_ref[...] = total[...]
        for b in range(blocks):
            part = slice(b * HEAD_DIM, (b + 1) * HEAD_DIM)
            raw = total[:, part]
            normed = raw * inverse_norm(raw) * scaling
            is_key = (rank_ref[0] * blocks + b) % 2 == 0
            memory_ref[:, part] = jnp.where(is_key, normed, raw).astype(bf16)


def key_stage(rank, modality, norm_gain, head_gain, weights, parts):
    _, depth, width = weights.shape
    rows = parts[0].shape[0]
    chunk = tile_of(depth, 1792)
    return pl.pallas_call(
        functools.partial(key_kernel, len(parts), chunk),
        grid=(depth // chunk,),
        out_shape=[
            jax.ShapeDtypeStruct((rows, width), bf16),
            jax.ShapeDtypeStruct((rows, width), f32),
            jax.ShapeDtypeStruct((rows, depth), bf16),
            jax.ShapeDtypeStruct((1, rows), f32),
        ],
        in_specs=[
            SMEM,
            whole(modality.shape),
            whole(norm_gain.shape),
            whole(head_gain.shape),
            pl.BlockSpec((2, chunk, width), lambda i: (0, i, 0)),
        ]
        + [whole(p.shape) for p in parts],
        out_specs=[
            whole((rows, width)),
            whole((rows, width)),
            whole((rows, depth)),
            whole((1, rows)),
        ],
        scratch_shapes=[pltpu.VMEM((rows, width), f32)],
        compiler_params=params(20),
        cost_estimate=cost(3),
        name="key_stage",
    )(rank, modality, norm_gain, head_gain, weights, *parts)


def query_kernel(chunk, modality_ref, head_ref, weight_ref, normed_ref, query_ref, raw_ref):
    step = pl.program_id(0)
    image = column(modality_ref[...]) > 0.0
    columns = pl.ds(pl.multiple_of(step * chunk, HEAD_DIM), chunk)
    product = both_experts(image, normed_ref[:, columns], weight_ref[...])

    @pl.when(step == 0)
    def _():
        raw_ref[...] = product

    @pl.when(step > 0)
    def _():
        raw_ref[...] += product

    @pl.when(step == pl.num_programs(0) - 1)
    def _():
        scaling = jnp.where(image, head_ref[1, 0:1, :], head_ref[0, 0:1, :])
        for h in range(raw_ref.shape[1] // HEAD_DIM):
            part = slice(h * HEAD_DIM, (h + 1) * HEAD_DIM)
            raw = raw_ref[:, part]
            query_ref[:, part] = (raw * inverse_norm(raw) * scaling).astype(bf16)


def query_stage(modality, head_gain, weights, normed):
    _, depth, width = weights.shape
    rows = normed.shape[0]
    chunk = tile_of(depth, 896)
    return pl.pallas_call(
        functools.partial(query_kernel, chunk),
        grid=(depth // chunk,),
        out_shape=[
            jax.ShapeDtypeStruct((rows, width), bf16),
            jax.ShapeDtypeStruct((rows, width), f32),
        ],
        in_specs=[
            whole(modality.shape),
            whole(head_gain.shape),
            pl.BlockSpec((2, chunk, width), lambda i: (0, i, 0)),
            whole(normed.shape),
        ],
        out_specs=[whole((rows, width)), whole((rows, width))],
        compiler_params=params(20),
        cost_estimate=cost(5),
        name="query_stage",
    )(modality, head_gain, weights, normed)


def cotangent_kernel(count, *refs):
    rank_ref, modality_ref, weight_ref = refs[:3]
    part_refs = refs[3 : 3 + count]
    back_ref, held = refs[3 + count :]
    image = column(modality_ref[...]) > 0.0

    @pl.when(pl.program_id(0) == 0)
    def _():
        held[...] = in_order(rank_ref[0], part_refs)

    back_ref[...] = both_back(image, held[...], weight_ref[...]).astype(bf16)


def cotangent_stage(rank, modality, weights, parts):
    _, width, depth = weights.shape
    rows = parts[0].shape[0]
    tile = tile_of(width, 256)
    return pl.pallas_call(
        functools.partial(cotangent_kernel, len(parts)),
        grid=(width // tile,),
        out_shape=jax.ShapeDtypeStruct((rows, width), bf16),
        in_specs=[
            SMEM,
            whole(modality.shape),
            pl.BlockSpec((2, tile, depth), lambda i: (0, i, 0)),
        ]
        + [whole(p.shape) for p in parts],
        out_specs=pl.BlockSpec((rows, tile), lambda i: (0, i)),
        scratch_shapes=[pltpu.VMEM((rows, depth), bf16)],
        compiler_params=params(20),
        cost_estimate=cost(7),
        name="cotangent_stage",
    )(rank, modality, weights, *parts)


def attention_kernel(blocks, per_group, *refs):
    source_ref, segments_ref, modality_ref, head_ref, query_ref, raw_ref, back_ref = refs[:7]
    memory_refs = refs[7 : 7 + blocks]
    attended_ref, query_back_ref, inner_ref = refs[7 + blocks : 10 + blocks]
    grad_refs = refs[10 + blocks :]
    rows = query_ref.shape[0]
    scale = 1.0 / math.sqrt(HEAD_DIM)

    def heads(ref):
        return jnp.concatenate(
            [ref[:, h * HEAD_DIM : (h + 1) * HEAD_DIM] for h in range(per_group)], axis=0
        )

    query, back = heads(query_ref), heads(back_ref)
    key = jnp.concatenate([m[:, :HEAD_DIM] for m in memory_refs], axis=0)
    value = jnp.concatenate([m[:, HEAD_DIM:] for m in memory_refs], axis=0)
    key_segments = jnp.concatenate(
        [segments_ref[pl.ds(source_ref[b], 1), :] for b in range(blocks)], axis=1
    )
    query_segments = column(segments_ref[pl.ds(source_ref[0], 1), :])
    visible = jnp.where(key_segments.astype(f32) <= query_segments, 1.0, 0.0)
    visible = jnp.concatenate([visible] * per_group, axis=0)
    scores = dot_nt(query, key) * scale
    weights = jnp.where(visible > 0.0, jnp.exp(scores), 0.0).astype(bf16)
    weights32 = weights.astype(f32)
    denominator = jnp.sum(weights32, axis=1, keepdims=True)
    numerator = jnp.dot(weights, value, preferred_element_type=f32)
    attended = (numerator / denominator).astype(bf16)
    offset = jnp.sum(back.astype(f32) * attended.astype(f32), axis=1, keepdims=True)
    probability = (weights32 / denominator).astype(bf16)
    back_prob = dot_nt(back, value)
    back_score = (probability.astype(f32) * (back_prob - offset)).astype(bf16)
    back_query = jnp.dot(back_score, key, preferred_element_type=f32) * scale
    back_key = dot_tn(back_score, query) * scale
    back_value = dot_tn(probability, back)
    for b in range(blocks):
        part = slice(b * rows, (b + 1) * rows)
        grad_refs[b][:, :HEAD_DIM] = back_key[part].astype(grad_refs[b].dtype)
        grad_refs[b][:, HEAD_DIM:] = back_value[part].astype(grad_refs[b].dtype)
    image = column(modality_ref[...]) > 0.0
    scaling = jnp.where(image, head_ref[1, 0:1, :], head_ref[0, 0:1, :])
    inner = jnp.zeros((rows, 1), f32)
    for h in range(per_group):
        part = slice(h * rows, (h + 1) * rows)
        columns = slice(h * HEAD_DIM, (h + 1) * HEAD_DIM)
        attended_ref[:, columns] = attended[part]
        raw = raw_ref[:, columns]
        query_back = norm_back(raw, inverse_norm(raw), scaling, back_query[part]).astype(bf16)
        query_back_ref[:, columns] = query_back
        inner += jnp.sum(query_back.astype(f32) * raw, axis=1, keepdims=True)
    inner = row_of(inner)

    @pl.when(pl.program_id(0) == 0)
    def _():
        inner_ref[...] = inner

    @pl.when(pl.program_id(0) > 0)
    def _():
        inner_ref[...] += inner


def attention_stage(sources, segments, modality, head_gain, query, raw, back, memories):
    rows, width = query.shape
    blocks = len(memories)
    pairs = memories[0].shape[1] // (2 * HEAD_DIM)
    per_group = width // HEAD_DIM // pairs
    wide = pl.BlockSpec((rows, per_group * HEAD_DIM), lambda g: (0, g))
    narrow = pl.BlockSpec((rows, 2 * HEAD_DIM), lambda g: (0, g))
    outs = [
        jax.ShapeDtypeStruct((rows, width), bf16),
        jax.ShapeDtypeStruct((rows, width), bf16),
        jax.ShapeDtypeStruct((1, rows), f32),
    ] + [
        jax.ShapeDtypeStruct((rows, pairs * 2 * HEAD_DIM), f32 if b == 0 else bf16)
        for b in range(blocks)
    ]
    return pl.pallas_call(
        functools.partial(attention_kernel, blocks, per_group),
        grid=(pairs,),
        out_shape=outs,
        in_specs=[
            SMEM,
            whole(segments.shape),
            whole(modality.shape),
            whole(head_gain.shape),
            wide,
            wide,
            wide,
        ]
        + [narrow] * blocks,
        out_specs=[wide, wide, whole((1, rows))] + [narrow] * blocks,
        compiler_params=params(32),
        cost_estimate=cost(3.5),
        name="attention_stage",
    )(sources, segments, modality, head_gain, query, raw, back, *memories)


def output_kernel(turns, rank_ref, modality_ref, weight_ref, attended_ref, *out_refs):
    image = column(modality_ref[...]) > 0.0
    product = both_experts(image, attended_ref[...], weight_ref[...])
    if len(out_refs) == 1:
        out_refs[0][...] = product.astype(bf16)
        return
    sent_ref, kept_ref = out_refs

    @pl.when(pl.program_id(0) < turns)
    def _():
        sent_ref[...] = product.astype(bf16)

    @pl.when(pl.program_id(0) >= turns)
    def _():
        kept_ref[...] = product


def output_stage(rank, modality, weights, attended, split):
    _, depth, width = weights.shape
    rows = attended.shape[0]
    tile = tile_of(width // 2, 896)
    turns = width // 2 // tile
    if split:
        def place(i, rank_ref):
            half = jnp.where(i < turns, 1 - rank_ref[0], rank_ref[0])
            return half * turns + lax.rem(i, turns)

        outs = [
            jax.ShapeDtypeStruct((rows, width // 2), bf16),
            jax.ShapeDtypeStruct((rows, width // 2), f32),
        ]
        out_specs = [
            pl.BlockSpec((rows, tile), lambda i, r: (0, jnp.minimum(i, turns - 1))),
            pl.BlockSpec((rows, tile), lambda i, r: (0, jnp.maximum(i - turns, 0))),
        ]
    else:
        def place(i, rank_ref):
            return i

        outs = [jax.ShapeDtypeStruct((rows, width), bf16)]
        out_specs = [pl.BlockSpec((rows, tile), lambda i, r: (0, i))]
    return pl.pallas_call(
        functools.partial(output_kernel, turns),
        grid_spec=pltpu.PrefetchScalarGridSpec(
            num_scalar_prefetch=1,
            grid=(2 * turns,),
            in_specs=[
                whole(modality.shape),
                pl.BlockSpec((2, depth, tile), lambda i, r: (0, 0, place(i, r))),
                whole(attended.shape),
            ],
            out_specs=out_specs,
        ),
        out_shape=outs,
        compiler_params=params(20),
        cost_estimate=cost(5),
        name="output_stage",
    )(rank, modality, weights, attended)


def query_back_kernel(modality_ref, weight_ref, back_ref, out_ref):
    image = column(modality_ref[...]) > 0.0
    out_ref[...] = both_back(image, back_ref[...], weight_ref[...])


def query_back_stage(modality, weights, back):
    _, depth, width = weights.shape
    rows = back.shape[0]
    tile = tile_of(depth, 896)
    return pl.pallas_call(
        query_back_kernel,
        grid=(depth // tile,),
        out_shape=jax.ShapeDtypeStruct((rows, depth), f32),
        in_specs=[
            whole(modality.shape),
            pl.BlockSpec((2, tile, width), lambda i: (0, i, 0)),
            whole(back.shape),
        ],
        out_specs=pl.BlockSpec((rows, tile), lambda i: (0, i)),
        compiler_params=params(20),
        cost_estimate=cost(7),
        name="query_back_stage",
    )(modality, weights, back)


def key_back_kernel(
    count, rank_ref, modality_ref, head_ref, raw_ref, inner_in_ref, part_ref, weight_ref, *refs
):
    grad_refs = refs[:count]
    out_ref, back_ref, inner_ref = refs[count:]
    image = column(modality_ref[...]) > 0.0
    blocks = raw_ref.shape[1] // HEAD_DIM

    @pl.when(pl.program_id(0) == 0)
    def _():
        scaling = jnp.where(image, head_ref[1, 1:2, :], head_ref[0, 1:2, :])
        inner = jnp.zeros((raw_ref.shape[0], 1), f32)
        for b in range(blocks):
            part = slice(b * HEAD_DIM, (b + 1) * HEAD_DIM)
            raw = raw_ref[:, part]
            upstream = grad_refs[0][:, part].astype(f32)
            for grad_ref in grad_refs[1:]:
                upstream += grad_ref[:, part].astype(f32)
            is_key = (rank_ref[0] * blocks + b) % 2 == 0
            normed_back = norm_back(raw, inverse_norm(raw), scaling, upstream)
            back = jnp.where(is_key, normed_back, upstream).astype(bf16)
            back_ref[:, part] = back
            inner += jnp.sum(back.astype(f32) * raw, axis=1, keepdims=True)
        inner_ref[...] = inner_in_ref[...] + row_of(inner)

    product = both_back(image, back_ref[...], weight_ref[...])
    out_ref[...] = (product + part_ref[...]).astype(bf16)


def key_back_stage(rank, modality, head_gain, raw, inner, part, weights, grads, split):
    _, depth, width = weights.shape
    rows = raw.shape[0]
    tile = tile_of(depth // 2, 896)
    turns = depth // 2 // tile
    steps = turns if split else 2 * turns

    def place(i, rank_ref):
        return (1 - rank_ref[0]) * turns + i if split else i

    return pl.pallas_call(
        functools.partial(key_back_kernel, len(grads)),
        grid_spec=pltpu.PrefetchScalarGridSpec(
            num_scalar_prefetch=1,
            grid=(steps,),
            in_specs=[
                whole(modality.shape),
                whole(head_gain.shape),
                whole(raw.shape),
                whole(inner.shape),
                pl.BlockSpec((rows, tile), lambda i, r: (0, place(i, r))),
                pl.BlockSpec((2, tile, width), lambda i, r: (0, place(i, r), 0)),
            ]
            + [whole(g.shape) for g in grads],
            out_specs=[
                pl.BlockSpec((rows, tile), lambda i, r: (0, i)),
                whole((rows, width)),
                whole((1, rows)),
            ],
        ),
        out_shape=[
            jax.ShapeDtypeStruct((rows, steps * tile), bf16),
            jax.ShapeDtypeStruct((rows, width), bf16),
            jax.ShapeDtypeStruct((1, rows), f32),
        ],
        compiler_params=params(20),
        cost_estimate=cost(2),
        name="key_back_stage",
    )(rank, modality, head_gain, raw, inner, part, weights, *grads)


def kept_kernel(rank_ref, modality_ref, part_ref, weight_ref, back_ref, out_ref):
    image = column(modality_ref[...]) > 0.0
    out_ref[...] = both_back(image, back_ref[...], weight_ref[...]) + part_ref[...]


def kept_stage(rank, modality, part, weights, back):
    _, depth, width = weights.shape
    rows = back.shape[0]
    tile = tile_of(depth // 2, 896)
    turns = depth // 2 // tile
    return pl.pallas_call(
        kept_kernel,
        grid_spec=pltpu.PrefetchScalarGridSpec(
            num_scalar_prefetch=1,
            grid=(turns,),
            in_specs=[
                whole(modality.shape),
                pl.BlockSpec((rows, tile), lambda i, r: (0, r[0] * turns + i)),
                pl.BlockSpec((2, tile, width), lambda i, r: (0, r[0] * turns + i, 0)),
                whole(back.shape),
            ],
            out_specs=pl.BlockSpec((rows, tile), lambda i, r: (0, i)),
        ),
        out_shape=jax.ShapeDtypeStruct((rows, depth // 2), f32),
        compiler_params=params(20),
        cost_estimate=cost(2),
        name="kept_stage",
    )(rank, modality, part, weights, back)


def finish(total_width, count, modality, gain, factor, inputs, backs, inners):
    rows, width = inputs.shape

    def kernel(modality_ref, gain_ref, factor_ref, inputs_ref, *refs):
        back_refs = refs[:count]
        inner_refs, out_ref = refs[count:-1], refs[-1]
        image = column(modality_ref[...]) > 0.0
        scaling = jnp.where(image, gain_ref[1:2, :], gain_ref[0:1, :])
        factor_column = column(factor_ref[...])
        back = back_refs[0][...].astype(f32)
        for ref in back_refs[1:]:
            back += ref[...].astype(f32)
        inner = inner_refs[0][...]
        for ref in inner_refs[1:]:
            inner += ref[...]
        unit_rows = inputs_ref[...].astype(f32) * factor_column
        inner_mean = column(inner) * (1.0 / total_width)
        out_ref[...] = (factor_column * (scaling * back - unit_rows * inner_mean)).astype(bf16)

    arrays = [modality, gain, factor, inputs, *backs, *inners]
    return pl.pallas_call(
        kernel,
        out_shape=jax.ShapeDtypeStruct((rows, width), bf16),
        in_specs=[whole(a.shape) for a in arrays],
        out_specs=whole((rows, width)),
        grid=(1,),
        compiler_params=params(20),
        cost_estimate=cost(1),
        name="finish",
    )(*arrays)


def local(
    inputs,
    cotangent,
    norm_gain,
    head_gain,
    query_weight,
    key_weight,
    output_weight,
    modality,
    segments,
    block_order,
):
    tensor_rank = lax.axis_index("tensor")
    block_rank = lax.axis_index("seq")
    tensor_count = lax.axis_size("tensor")
    block_count = lax.axis_size("seq")
    local_rows, local_width = inputs.shape
    full_width = local_width * tensor_count
    split = tensor_count == 2
    swap = [(0, 1), (1, 0)]
    rank = tensor_rank.astype(jnp.int32).reshape(1)
    modality = modality.reshape(1, local_rows)
    segments = segments.reshape(block_count, local_rows)

    def spread(part):
        if split:
            return [part, lax.ppermute(part, "tensor", swap)]
        return [lax.all_gather(part, "tensor", axis=1, tiled=True)]

    def scatter_columns(part):
        return lax.psum_scatter(part, "tensor", scatter_dimension=1, tiled=True)

    memory, key_raw, normed, row_factor = key_stage(
        rank, modality, norm_gain, head_gain, key_weight, spread(inputs)
    )
    shared = tensor_count > KV_HEADS
    is_even = tensor_rank % 2 == 0
    pair_swap = [(i, i ^ 1) for i in range(tensor_count)]
    if shared:
        partner = lax.ppermute(memory, "tensor", pair_swap)
        memory = jnp.where(
            is_even,
            jnp.concatenate([memory, partner], 1),
            jnp.concatenate([partner, memory], 1),
        )
    memories, order = [memory], [block_rank]
    for step in range(1, block_count):
        memories.append(lax.ppermute(memory, "seq", seq_pairs(step, block_count)))
        order.append(seq_source(block_rank, step, block_count))
    sources = block_order[jnp.stack(order)]

    query, query_raw = query_stage(modality, head_gain, query_weight, normed)
    back_attended = cotangent_stage(rank, modality, output_weight, spread(cotangent))
    attended, query_back, inner, own_grad, *grads = attention_stage(
        sources, segments, modality, head_gain, query, query_raw, back_attended, memories
    )
    incoming = [
        lax.ppermute(grad, "seq", inverted(seq_pairs(step, block_count)))
        for step, grad in enumerate(grads, 1)
    ]

    projected = output_stage(rank, modality, output_weight, attended, split)
    if split:
        sent, kept = projected
        attention_out = (kept + lax.ppermute(sent, "tensor", swap).astype(f32)).astype(bf16)
    else:
        attention_out = scatter_columns(projected[0])

    gradient_part = query_back_stage(modality, query_weight, query_back)

    if shared:
        total = own_grad + sum(grad.astype(f32) for grad in incoming)
        low, high = total[:, :HEAD_DIM], total[:, HEAD_DIM:]
        outgoing = jnp.where(is_even, high, low).astype(bf16)
        sums = [jnp.where(is_even, low, high), lax.ppermute(outgoing, "tensor", pair_swap)]
    else:
        sums = [own_grad, *incoming]
    sent, slice_back, inner = key_back_stage(
        rank, modality, head_gain, key_raw, inner, gradient_part, key_weight, sums, split
    )
    if split:
        inners = [inner, lax.ppermute(inner, "tensor", swap)]
        other = lax.ppermute(sent, "tensor", swap)
        kept = kept_stage(rank, modality, gradient_part, key_weight, slice_back)
        backs = [kept, other]
    else:
        inners = [lax.psum(inner, "tensor")]
        backs = [scatter_columns(sent)]
    gain = lax.dynamic_slice_in_dim(norm_gain, tensor_rank * local_width, local_width, 1)
    grad_input = finish(
        full_width, len(backs), modality, gain, row_factor, inputs, backs, inners
    )
    return (attention_out, grad_input)


def solution(mesh):
    return jax.shard_map(
        local,
        mesh=mesh,
        in_specs=(
            P(("dp", "seq"), "tensor"),
            P(("dp", "seq"), "tensor"),
            P(),
            P(),
            P(None, None, "tensor"),
            P(None, None, "tensor"),
            P(None, "tensor", None),
            P(("dp", "seq")),
            P("dp"),
            P("dp"),
        ),
        out_specs=(P(("dp", "seq"), "tensor"), P(("dp", "seq"), "tensor")),
        check_vma=False,
    )
```

```python
import functools
import math

import jax
import jax.numpy as jnp
from jax import lax
from jax.experimental import pallas as pl
from jax.experimental.pallas import tpu as pltpu
from jax.sharding import PartitionSpec as P

KV_HEADS = 4
HEAD_DIM = 128
MIB = 1024 * 1024

epsilon = 1e-06
bf16 = jnp.bfloat16
f32 = jnp.float32
SMEM = pl.BlockSpec(memory_space=pltpu.SMEM)


def seq_pairs(step, count):
    if count & (count - 1) == 0:
        return [(i, i ^ step) for i in range(count)]
    return [(i, (i + step) % count) for i in range(count)]


def seq_source(rank, step, count):
    if count & (count - 1) == 0:
        return rank ^ step
    return (rank - step) % count


def inverted(pairs):
    return [(b, a) for a, b in pairs]


def tile_of(extent, most):
    best = HEAD_DIM
    for size in range(HEAD_DIM, min(extent, most) + 1, HEAD_DIM):
        if extent % size == 0:
            best = size
    return best


def dot_nt(a, b):
    return lax.dot_general(a, b, (((1,), (1,)), ((), ())), preferred_element_type=f32)


def dot_tn(a, b):
    return lax.dot_general(a, b, (((0,), (0,)), ((), ())), preferred_element_type=f32)


def column(row):
    count = row.shape[1]
    return jnp.broadcast_to(row.astype(f32), (count, count)).T[:, :1]


def row_of(col):
    count = col.shape[0]
    return jnp.broadcast_to(col, (count, count)).T[:1, :]


def inverse_norm(values):
    return lax.rsqrt(jnp.mean(values * values, axis=-1, keepdims=True) + epsilon)


def norm_back(values, factor, scaling, upstream):
    unit_rows = values * factor
    inner_mean = jnp.mean(scaling * upstream * unit_rows, axis=-1, keepdims=True)
    return factor * (scaling * upstream - unit_rows * inner_mean)


def streamed(weights):
    return pltpu.with_memory_space_constraint(weights, pltpu.HBM)


def whole(shape):
    return pl.BlockSpec(shape, lambda *_: (0,) * len(shape))


def params(mib):
    return pltpu.CompilerParams(vmem_limit_bytes=mib * MIB)


def cost(micros):
    return pl.CostEstimate(
        flops=int(micros * 1e9), bytes_accessed=int(micros * 2e6), transcendentals=0
    )


def in_order(rank, part_refs):
    if len(part_refs) == 1:
        return part_refs[0][...]
    own, other = part_refs[0][...], part_refs[1][...]
    first = rank == 0
    return jnp.concatenate([jnp.where(first, own, other), jnp.where(first, other, own)], axis=1)


def both_experts(image, rows, weights):
    zero = jnp.zeros_like(rows)
    masked = jnp.concatenate([jnp.where(image, zero, rows), jnp.where(image, rows, zero)], axis=1)
    flat = weights.reshape(2 * weights.shape[1], weights.shape[2])
    return jnp.dot(masked, flat, preferred_element_type=f32)


def both_back(image, rows, weights):
    return jnp.where(image, dot_nt(rows, weights[1]), dot_nt(rows, weights[0]))


def key_kernel(count, chunk, *refs):
    rank_ref, modality_ref, gain_ref, head_ref, weight_ref = refs[:5]
    part_refs = refs[5 : 5 + count]
    memory_ref, raw_ref, normed_ref, factor_ref, total = refs[5 + count :]
    step = pl.program_id(0)
    image = column(modality_ref[...]) > 0.0

    @pl.when(step == 0)
    def _():
        rows = in_order(rank_ref[0], part_refs).astype(f32)
        factor = inverse_norm(rows)
        scaling = jnp.where(image, gain_ref[1:2, :], gain_ref[0:1, :])
        normed_ref[...] = (rows * factor * scaling).astype(bf16)
        factor_ref[...] = row_of(factor)
        total[...] = jnp.zeros_like(total)

    columns = pl.ds(pl.multiple_of(step * chunk, HEAD_DIM), chunk)
    total[...] += both_experts(image, normed_ref[:, columns], weight_ref[...])

    @pl.when(step == pl.num_programs(0) - 1)
    def _():
        blocks = total.shape[1] // HEAD_DIM
        scaling = jnp.where(image, head_ref[1, 1:2, :], head_ref[0, 1:2, :])
        raw_ref[...] = total[...]
        for b in range(blocks):
            part = slice(b * HEAD_DIM, (b + 1) * HEAD_DIM)
            raw = total[:, part]
            normed = raw * inverse_norm(raw) * scaling
            is_key = (rank_ref[0] * blocks + b) % 2 == 0
            memory_ref[:, part] = jnp.where(is_key, normed, raw).astype(bf16)


def key_stage(rank, modality, norm_gain, head_gain, weights, parts):
    _, depth, width = weights.shape
    rows = parts[0].shape[0]
    chunk = tile_of(depth, 896)
    return pl.pallas_call(
        functools.partial(key_kernel, len(parts), chunk),
        grid=(depth // chunk,),
        out_shape=[
            jax.ShapeDtypeStruct((rows, width), bf16),
            jax.ShapeDtypeStruct((rows, width), f32),
            jax.ShapeDtypeStruct((rows, depth), bf16),
            jax.ShapeDtypeStruct((1, rows), f32),
        ],
        in_specs=[
            SMEM,
            whole(modality.shape),
            whole(norm_gain.shape),
            whole(head_gain.shape),
            pl.BlockSpec((2, chunk, width), lambda i: (0, i, 0)),
        ]
        + [whole(p.shape) for p in parts],
        out_specs=[
            whole((rows, width)),
            whole((rows, width)),
            whole((rows, depth)),
            whole((1, rows)),
        ],
        scratch_shapes=[pltpu.VMEM((rows, width), f32)],
        compiler_params=params(20),
        cost_estimate=cost(3),
        name="key_stage",
    )(rank, modality, norm_gain, head_gain, weights, *parts)


def query_kernel(chunk, modality_ref, head_ref, weight_ref, normed_ref, query_ref, raw_ref):
    step = pl.program_id(0)
    image = column(modality_ref[...]) > 0.0
    columns = pl.ds(pl.multiple_of(step * chunk, HEAD_DIM), chunk)
    product = both_experts(image, normed_ref[:, columns], weight_ref[...])

    @pl.when(step == 0)
    def _():
        raw_ref[...] = product

    @pl.when(step > 0)
    def _():
        raw_ref[...] += product

    @pl.when(step == pl.num_programs(0) - 1)
    def _():
        scaling = jnp.where(image, head_ref[1, 0:1, :], head_ref[0, 0:1, :])
        for h in range(raw_ref.shape[1] // HEAD_DIM):
            part = slice(h * HEAD_DIM, (h + 1) * HEAD_DIM)
            raw = raw_ref[:, part]
            query_ref[:, part] = (raw * inverse_norm(raw) * scaling).astype(bf16)


def query_stage(modality, head_gain, weights, normed):
    _, depth, width = weights.shape
    rows = normed.shape[0]
    chunk = tile_of(depth, 512)
    return pl.pallas_call(
        functools.partial(query_kernel, chunk),
        grid=(depth // chunk,),
        out_shape=[
            jax.ShapeDtypeStruct((rows, width), bf16),
            jax.ShapeDtypeStruct((rows, width), f32),
        ],
        in_specs=[
            whole(modality.shape),
            whole(head_gain.shape),
            pl.BlockSpec((2, chunk, width), lambda i: (0, i, 0)),
            whole(normed.shape),
        ],
        out_specs=[whole((rows, width)), whole((rows, width))],
        compiler_params=params(20),
        cost_estimate=cost(5),
        name="query_stage",
    )(modality, head_gain, weights, normed)


def cotangent_kernel(count, *refs):
    rank_ref, modality_ref, weight_ref = refs[:3]
    part_refs = refs[3 : 3 + count]
    back_ref, held = refs[3 + count :]
    image = column(modality_ref[...]) > 0.0

    @pl.when(pl.program_id(0) == 0)
    def _():
        held[...] = in_order(rank_ref[0], part_refs)

    back_ref[...] = both_back(image, held[...], weight_ref[...]).astype(bf16)


def cotangent_stage(rank, modality, weights, parts):
    _, width, depth = weights.shape
    rows = parts[0].shape[0]
    tile = tile_of(width, 128)
    return pl.pallas_call(
        functools.partial(cotangent_kernel, len(parts)),
        grid=(width // tile,),
        out_shape=jax.ShapeDtypeStruct((rows, width), bf16),
        in_specs=[
            SMEM,
            whole(modality.shape),
            pl.BlockSpec((2, tile, depth), lambda i: (0, i, 0)),
        ]
        + [whole(p.shape) for p in parts],
        out_specs=pl.BlockSpec((rows, tile), lambda i: (0, i)),
        scratch_shapes=[pltpu.VMEM((rows, depth), bf16)],
        compiler_params=params(20),
        cost_estimate=cost(7),
        name="cotangent_stage",
    )(rank, modality, weights, *parts)


def attention_kernel(blocks, per_group, *refs):
    source_ref, segments_ref, modality_ref, head_ref, query_ref, raw_ref, back_ref = refs[:7]
    memory_refs = refs[7 : 7 + blocks]
    attended_ref, query_back_ref, inner_ref = refs[7 + blocks : 10 + blocks]
    grad_refs = refs[10 + blocks :]
    rows = query_ref.shape[0]
    scale = 1.0 / math.sqrt(HEAD_DIM)

    def heads(ref):
        return jnp.concatenate(
            [ref[:, h * HEAD_DIM : (h + 1) * HEAD_DIM] for h in range(per_group)], axis=0
        )

    query, back = heads(query_ref), heads(back_ref)
    key = jnp.concatenate([m[:, :HEAD_DIM] for m in memory_refs], axis=0)
    value = jnp.concatenate([m[:, HEAD_DIM:] for m in memory_refs], axis=0)
    key_segments = jnp.concatenate(
        [segments_ref[pl.ds(source_ref[b], 1), :] for b in range(blocks)], axis=1
    )
    query_segments = column(segments_ref[pl.ds(source_ref[0], 1), :])
    visible = jnp.where(key_segments.astype(f32) <= query_segments, 1.0, 0.0)
    visible = jnp.concatenate([visible] * per_group, axis=0)
    scores = dot_nt(query, key) * scale
    weights = jnp.where(visible > 0.0, jnp.exp(scores), 0.0).astype(bf16)
    weights32 = weights.astype(f32)
    denominator = jnp.sum(weights32, axis=1, keepdims=True)
    numerator = jnp.dot(weights, value, preferred_element_type=f32)
    attended = (numerator / denominator).astype(bf16)
    offset = jnp.sum(back.astype(f32) * attended.astype(f32), axis=1, keepdims=True)
    probability = (weights32 / denominator).astype(bf16)
    back_prob = dot_nt(back, value)
    back_score = (probability.astype(f32) * (back_prob - offset)).astype(bf16)
    back_query = jnp.dot(back_score, key, preferred_element_type=f32) * scale
    back_key = dot_tn(back_score, query) * scale
    back_value = dot_tn(probability, back)
    for b in range(blocks):
        part = slice(b * rows, (b + 1) * rows)
        grad_refs[b][:, :HEAD_DIM] = back_key[part].astype(grad_refs[b].dtype)
        grad_refs[b][:, HEAD_DIM:] = back_value[part].astype(grad_refs[b].dtype)
    image = column(modality_ref[...]) > 0.0
    scaling = jnp.where(image, head_ref[1, 0:1, :], head_ref[0, 0:1, :])
    inner = jnp.zeros((rows, 1), f32)
    for h in range(per_group):
        part = slice(h * rows, (h + 1) * rows)
        columns = slice(h * HEAD_DIM, (h + 1) * HEAD_DIM)
        attended_ref[:, columns] = attended[part]
        raw = raw_ref[:, columns]
        query_back = norm_back(raw, inverse_norm(raw), scaling, back_query[part]).astype(bf16)
        query_back_ref[:, columns] = query_back
        inner += jnp.sum(query_back.astype(f32) * raw, axis=1, keepdims=True)
    inner = row_of(inner)

    @pl.when(pl.program_id(0) == 0)
    def _():
        inner_ref[...] = inner

    @pl.when(pl.program_id(0) > 0)
    def _():
        inner_ref[...] += inner


def attention_stage(sources, segments, modality, head_gain, query, raw, back, memories):
    rows, width = query.shape
    blocks = len(memories)
    pairs = memories[0].shape[1] // (2 * HEAD_DIM)
    per_group = width // HEAD_DIM // pairs
    wide = pl.BlockSpec((rows, per_group * HEAD_DIM), lambda g: (0, g))
    narrow = pl.BlockSpec((rows, 2 * HEAD_DIM), lambda g: (0, g))
    outs = [
        jax.ShapeDtypeStruct((rows, width), bf16),
        jax.ShapeDtypeStruct((rows, width), bf16),
        jax.ShapeDtypeStruct((1, rows), f32),
    ] + [
        jax.ShapeDtypeStruct((rows, pairs * 2 * HEAD_DIM), f32 if b == 0 else bf16)
        for b in range(blocks)
    ]
    return pl.pallas_call(
        functools.partial(attention_kernel, blocks, per_group),
        grid=(pairs,),
        out_shape=outs,
        in_specs=[
            SMEM,
            whole(segments.shape),
            whole(modality.shape),
            whole(head_gain.shape),
            wide,
            wide,
            wide,
        ]
        + [narrow] * blocks,
        out_specs=[wide, wide, whole((1, rows))] + [narrow] * blocks,
        compiler_params=params(32),
        cost_estimate=cost(3.5),
        name="attention_stage",
    )(sources, segments, modality, head_gain, query, raw, back, *memories)


def output_kernel(turns, rank_ref, modality_ref, weight_ref, attended_ref, *out_refs):
    image = column(modality_ref[...]) > 0.0
    product = both_experts(image, attended_ref[...], weight_ref[...])
    if len(out_refs) == 1:
        out_refs[0][...] = product.astype(bf16)
        return
    sent_ref, kept_ref = out_refs

    @pl.when(pl.program_id(0) < turns)
    def _():
        sent_ref[...] = product.astype(bf16)

    @pl.when(pl.program_id(0) >= turns)
    def _():
        kept_ref[...] = product


def output_stage(rank, modality, weights, attended, split):
    _, depth, width = weights.shape
    rows = attended.shape[0]
    tile = tile_of(width // 2, 896)
    turns = width // 2 // tile
    if split:
        def place(i, rank_ref):
            half = jnp.where(i < turns, 1 - rank_ref[0], rank_ref[0])
            return half * turns + lax.rem(i, turns)

        outs = [
            jax.ShapeDtypeStruct((rows, width // 2), bf16),
            jax.ShapeDtypeStruct((rows, width // 2), f32),
        ]
        out_specs = [
            pl.BlockSpec((rows, tile), lambda i, r: (0, jnp.minimum(i, turns - 1))),
            pl.BlockSpec((rows, tile), lambda i, r: (0, jnp.maximum(i - turns, 0))),
        ]
    else:
        def place(i, rank_ref):
            return i

        outs = [jax.ShapeDtypeStruct((rows, width), bf16)]
        out_specs = [pl.BlockSpec((rows, tile), lambda i, r: (0, i))]
    return pl.pallas_call(
        functools.partial(output_kernel, turns),
        grid_spec=pltpu.PrefetchScalarGridSpec(
            num_scalar_prefetch=1,
            grid=(2 * turns,),
            in_specs=[
                whole(modality.shape),
                pl.BlockSpec((2, depth, tile), lambda i, r: (0, 0, place(i, r))),
                whole(attended.shape),
            ],
            out_specs=out_specs,
        ),
        out_shape=outs,
        compiler_params=params(20),
        cost_estimate=cost(5),
        name="output_stage",
    )(rank, modality, weights, attended)


def query_back_kernel(modality_ref, weight_ref, back_ref, out_ref):
    image = column(modality_ref[...]) > 0.0
    out_ref[...] = both_back(image, back_ref[...], weight_ref[...])


def query_back_stage(modality, weights, back):
    _, depth, width = weights.shape
    rows = back.shape[0]
    tile = tile_of(depth, 512)
    return pl.pallas_call(
        query_back_kernel,
        grid=(depth // tile,),
        out_shape=jax.ShapeDtypeStruct((rows, depth), f32),
        in_specs=[
            whole(modality.shape),
            pl.BlockSpec((2, tile, width), lambda i: (0, i, 0)),
            whole(back.shape),
        ],
        out_specs=pl.BlockSpec((rows, tile), lambda i: (0, i)),
        compiler_params=params(20),
        cost_estimate=cost(7),
        name="query_back_stage",
    )(modality, weights, back)


def key_back_kernel(
    count, rank_ref, modality_ref, head_ref, raw_ref, inner_in_ref, part_ref, weight_ref, *refs
):
    grad_refs = refs[:count]
    out_ref, back_ref, inner_ref = refs[count:]
    image = column(modality_ref[...]) > 0.0
    blocks = raw_ref.shape[1] // HEAD_DIM

    @pl.when(pl.program_id(0) == 0)
    def _():
        scaling = jnp.where(image, head_ref[1, 1:2, :], head_ref[0, 1:2, :])
        inner = jnp.zeros((raw_ref.shape[0], 1), f32)
        for b in range(blocks):
            part = slice(b * HEAD_DIM, (b + 1) * HEAD_DIM)
            raw = raw_ref[:, part]
            upstream = grad_refs[0][:, part].astype(f32)
            for grad_ref in grad_refs[1:]:
                upstream += grad_ref[:, part].astype(f32)
            is_key = (rank_ref[0] * blocks + b) % 2 == 0
            normed_back = norm_back(raw, inverse_norm(raw), scaling, upstream)
            back = jnp.where(is_key, normed_back, upstream).astype(bf16)
            back_ref[:, part] = back
            inner += jnp.sum(back.astype(f32) * raw, axis=1, keepdims=True)
        inner_ref[...] = inner_in_ref[...] + row_of(inner)

    product = both_back(image, back_ref[...], weight_ref[...])
    out_ref[...] = (product + part_ref[...]).astype(bf16)


def key_back_stage(rank, modality, head_gain, raw, inner, part, weights, grads, split):
    _, depth, width = weights.shape
    rows = raw.shape[0]
    tile = tile_of(depth // 2, 896)
    turns = depth // 2 // tile
    steps = turns if split else 2 * turns

    def place(i, rank_ref):
        return (1 - rank_ref[0]) * turns + i if split else i

    return pl.pallas_call(
        functools.partial(key_back_kernel, len(grads)),
        grid_spec=pltpu.PrefetchScalarGridSpec(
            num_scalar_prefetch=1,
            grid=(steps,),
            in_specs=[
                whole(modality.shape),
                whole(head_gain.shape),
                whole(raw.shape),
                whole(inner.shape),
                pl.BlockSpec((rows, tile), lambda i, r: (0, place(i, r))),
                pl.BlockSpec((2, tile, width), lambda i, r: (0, place(i, r), 0)),
            ]
            + [whole(g.shape) for g in grads],
            out_specs=[
                pl.BlockSpec((rows, tile), lambda i, r: (0, i)),
                whole((rows, width)),
                whole((1, rows)),
            ],
        ),
        out_shape=[
            jax.ShapeDtypeStruct((rows, steps * tile), bf16),
            jax.ShapeDtypeStruct((rows, width), bf16),
            jax.ShapeDtypeStruct((1, rows), f32),
        ],
        compiler_params=params(20),
        cost_estimate=cost(2),
        name="key_back_stage",
    )(rank, modality, head_gain, raw, inner, part, weights, *grads)


def kept_kernel(rank_ref, modality_ref, part_ref, weight_ref, back_ref, out_ref):
    image = column(modality_ref[...]) > 0.0
    out_ref[...] = both_back(image, back_ref[...], weight_ref[...]) + part_ref[...]


def kept_stage(rank, modality, part, weights, back):
    _, depth, width = weights.shape
    rows = back.shape[0]
    tile = tile_of(depth // 2, 896)
    turns = depth // 2 // tile
    return pl.pallas_call(
        kept_kernel,
        grid_spec=pltpu.PrefetchScalarGridSpec(
            num_scalar_prefetch=1,
            grid=(turns,),
            in_specs=[
                whole(modality.shape),
                pl.BlockSpec((rows, tile), lambda i, r: (0, r[0] * turns + i)),
                pl.BlockSpec((2, tile, width), lambda i, r: (0, r[0] * turns + i, 0)),
                whole(back.shape),
            ],
            out_specs=pl.BlockSpec((rows, tile), lambda i, r: (0, i)),
        ),
        out_shape=jax.ShapeDtypeStruct((rows, depth // 2), f32),
        compiler_params=params(20),
        cost_estimate=cost(2),
        name="kept_stage",
    )(rank, modality, part, weights, back)


def finish(total_width, count, modality, gain, factor, inputs, backs, inners):
    rows, width = inputs.shape

    def kernel(modality_ref, gain_ref, factor_ref, inputs_ref, *refs):
        back_refs = refs[:count]
        inner_refs, out_ref = refs[count:-1], refs[-1]
        image = column(modality_ref[...]) > 0.0
        scaling = jnp.where(image, gain_ref[1:2, :], gain_ref[0:1, :])
        factor_column = column(factor_ref[...])
        back = back_refs[0][...].astype(f32)
        for ref in back_refs[1:]:
            back += ref[...].astype(f32)
        inner = inner_refs[0][...]
        for ref in inner_refs[1:]:
            inner += ref[...]
        unit_rows = inputs_ref[...].astype(f32) * factor_column
        inner_mean = column(inner) * (1.0 / total_width)
        out_ref[...] = (factor_column * (scaling * back - unit_rows * inner_mean)).astype(bf16)

    arrays = [modality, gain, factor, inputs, *backs, *inners]
    return pl.pallas_call(
        kernel,
        out_shape=jax.ShapeDtypeStruct((rows, width), bf16),
        in_specs=[whole(a.shape) for a in arrays],
        out_specs=whole((rows, width)),
        grid=(1,),
        compiler_params=params(20),
        cost_estimate=cost(1),
        name="finish",
    )(*arrays)


def local(
    inputs,
    cotangent,
    norm_gain,
    head_gain,
    query_weight,
    key_weight,
    output_weight,
    modality,
    segments,
    block_order,
):
    tensor_rank = lax.axis_index("tensor")
    block_rank = lax.axis_index("seq")
    tensor_count = lax.axis_size("tensor")
    block_count = lax.axis_size("seq")
    local_rows, local_width = inputs.shape
    full_width = local_width * tensor_count
    split = tensor_count == 2
    swap = [(0, 1), (1, 0)]
    rank = tensor_rank.astype(jnp.int32).reshape(1)
    modality = streamed(modality.reshape(1, local_rows))
    segments = streamed(segments.reshape(block_count, local_rows))
    head_gain = streamed(head_gain)

    def spread(part):
        if split:
            return [streamed(part), lax.ppermute(part, "tensor", swap)]
        return [lax.all_gather(part, "tensor", axis=1, tiled=True)]

    def scatter_columns(part):
        return lax.psum_scatter(part, "tensor", scatter_dimension=1, tiled=True)

    memory, key_raw, normed, row_factor = key_stage(
        rank, modality, streamed(norm_gain), head_gain, streamed(key_weight), spread(inputs)
    )
    shared = tensor_count > KV_HEADS
    is_even = tensor_rank % 2 == 0
    pair_swap = [(i, i ^ 1) for i in range(tensor_count)]
    if shared:
        partner = lax.ppermute(memory, "tensor", pair_swap)
        memory = jnp.where(
            is_even,
            jnp.concatenate([memory, partner], 1),
            jnp.concatenate([partner, memory], 1),
        )
    memories, order = [memory], [block_rank]
    for step in range(1, block_count):
        memories.append(lax.ppermute(memory, "seq", seq_pairs(step, block_count)))
        order.append(seq_source(block_rank, step, block_count))
    sources = block_order[jnp.stack(order)]

    query, query_raw = query_stage(modality, head_gain, streamed(query_weight), normed)
    back_attended = cotangent_stage(
        rank, modality, streamed(output_weight), spread(cotangent)
    )
    attended, query_back, inner, own_grad, *grads = attention_stage(
        sources, segments, modality, head_gain, query, query_raw, back_attended, memories
    )
    incoming = [
        lax.ppermute(grad, "seq", inverted(seq_pairs(step, block_count)))
        for step, grad in enumerate(grads, 1)
    ]

    projected = output_stage(rank, modality, output_weight, attended, split)
    if split:
        sent, kept = projected
        attention_out = (kept + lax.ppermute(sent, "tensor", swap).astype(f32)).astype(bf16)
    else:
        attention_out = scatter_columns(projected[0])

    gradient_part = query_back_stage(modality, streamed(query_weight), query_back)

    if shared:
        total = own_grad + sum(grad.astype(f32) for grad in incoming)
        low, high = total[:, :HEAD_DIM], total[:, HEAD_DIM:]
        outgoing = jnp.where(is_even, high, low).astype(bf16)
        sums = [jnp.where(is_even, low, high), lax.ppermute(outgoing, "tensor", pair_swap)]
    else:
        sums = [own_grad, *incoming]
    sent, slice_back, inner = key_back_stage(
        rank, modality, head_gain, key_raw, inner, gradient_part, key_weight, sums, split
    )
    if split:
        inners = [inner, lax.ppermute(inner, "tensor", swap)]
        other = lax.ppermute(sent, "tensor", swap)
        kept = kept_stage(rank, modality, gradient_part, key_weight, slice_back)
        backs = [kept, other]
    else:
        inners = [lax.psum(inner, "tensor")]
        backs = [scatter_columns(sent)]
    gain = lax.dynamic_slice_in_dim(norm_gain, tensor_rank * local_width, local_width, 1)
    grad_input = finish(
        full_width, len(backs), modality, gain, row_factor, streamed(inputs), backs, inners
    )
    return (attention_out, grad_input)


def solution(mesh):
    return jax.shard_map(
        local,
        mesh=mesh,
        in_specs=(
            P(("dp", "seq"), "tensor"),
            P(("dp", "seq"), "tensor"),
            P(),
            P(),
            P(None, None, "tensor"),
            P(None, None, "tensor"),
            P(None, "tensor", None),
            P(("dp", "seq")),
            P("dp"),
            P("dp"),
        ),
        out_specs=(P(("dp", "seq"), "tensor"), P(("dp", "seq"), "tensor")),
        check_vma=False,
    )
```

```python
import functools
import math

import jax
import jax.numpy as jnp
from jax import lax
from jax.experimental import pallas as pl
from jax.experimental.pallas import tpu as pltpu
from jax.sharding import PartitionSpec as P

KV_HEADS = 4
HEAD_DIM = 128
MIB = 1024 * 1024

epsilon = 1e-06
bf16 = jnp.bfloat16
f32 = jnp.float32
SMEM = pl.BlockSpec(memory_space=pltpu.SMEM)
VMEM = pl.BlockSpec(memory_space=pltpu.VMEM)
ANY = pl.BlockSpec(memory_space=pl.ANY)


def seq_pairs(step, count):
    if count & (count - 1) == 0:
        return [(i, i ^ step) for i in range(count)]
    return [(i, (i + step) % count) for i in range(count)]


def seq_source(rank, step, count):
    if count & (count - 1) == 0:
        return rank ^ step
    return (rank - step) % count


def inverted(pairs):
    return [(b, a) for a, b in pairs]


def tile_of(extent, most):
    best = HEAD_DIM
    for size in range(HEAD_DIM, min(extent, most) + 1, HEAD_DIM):
        if extent % size == 0:
            best = size
    return best


def dot_nt(a, b):
    return lax.dot_general(a, b, (((1,), (1,)), ((), ())), preferred_element_type=f32)


def dot_tn(a, b):
    return lax.dot_general(a, b, (((0,), (0,)), ((), ())), preferred_element_type=f32)


def column(row):
    count = row.shape[1]
    return jnp.broadcast_to(row.astype(f32), (count, count)).T[:, :1]


def row_of(col):
    count = col.shape[0]
    return jnp.broadcast_to(col, (count, count)).T[:1, :]


def inverse_norm(values):
    return lax.rsqrt(jnp.mean(values * values, axis=-1, keepdims=True) + epsilon)


def norm_back(values, factor, scaling, upstream):
    unit_rows = values * factor
    inner_mean = jnp.mean(scaling * upstream * unit_rows, axis=-1, keepdims=True)
    return factor * (scaling * upstream - unit_rows * inner_mean)


def streamed(weights):
    return pltpu.with_memory_space_constraint(weights, pltpu.HBM)


def params(mib):
    return pltpu.CompilerParams(vmem_limit_bytes=mib * MIB)


def cost(micros):
    return pl.CostEstimate(
        flops=int(micros * 1e9), bytes_accessed=int(micros * 2e6), transcendentals=0
    )


def in_order(rank, part_refs):
    if len(part_refs) == 1:
        return part_refs[0][...]
    own, other = part_refs[0][...], part_refs[1][...]
    first = rank == 0
    return jnp.concatenate([jnp.where(first, own, other), jnp.where(first, other, own)], axis=1)


def both_experts(image, rows, weights):
    zero = jnp.zeros_like(rows)
    masked = jnp.concatenate([jnp.where(image, zero, rows), jnp.where(image, rows, zero)], axis=1)
    flat = weights.reshape(2 * weights.shape[1], weights.shape[2])
    return jnp.dot(masked, flat, preferred_element_type=f32)


def both_back(image, rows, weights):
    return jnp.where(image, dot_nt(rows, weights[1]), dot_nt(rows, weights[0]))


def chunks_of(extent, most):
    size = tile_of(extent, most)
    return [(start, size) for start in range(0, extent, size)]


AHEAD = 4


def copies_of(source_ref, target_ref, sem_ref, pieces, base=0, slots=0):
    copies = []
    for index, (start, size) in enumerate(pieces):
        pair = []
        for e in range(2):
            if slots:
                target = target_ref.at[index % slots, e]
            else:
                target = target_ref.at[e, pl.ds(start, size), :]
            source = source_ref.at[e, pl.ds(base + start, size), :]
            pair.append(pltpu.make_async_copy(source, target, sem_ref.at[index, e]))
        copies.append(pair)
    return copies


def begin(copies, index):
    if index < len(copies):
        for copy in copies[index]:
            copy.start()


def begin_first(copies):
    for index in range(AHEAD):
        begin(copies, index)


def arrive(copies, index):
    for copy in copies[index]:
        copy.wait()


def ring(weights, pieces):
    return pltpu.VMEM((AHEAD, 2, pieces[0][1], weights.shape[2]), weights.dtype)


def resident(weights):
    return pltpu.VMEM(weights.shape, weights.dtype)


def fetch_kernel(pieces, weight_ref, held_ref, sem_ref):
    copies = copies_of(weight_ref, held_ref, sem_ref, pieces)
    for pair in copies:
        for copy in pair:
            copy.start()
    for pair in copies:
        for copy in pair:
            copy.wait()


def fetch(weights):
    pieces = chunks_of(weights.shape[1], 896)
    return pl.pallas_call(
        functools.partial(fetch_kernel, pieces),
        out_shape=resident(weights),
        in_specs=[ANY],
        out_specs=VMEM,
        scratch_shapes=[pltpu.SemaphoreType.DMA((len(pieces), 2))],
        compiler_params=params(4),
        cost_estimate=cost(0.2),
        name="fetch",
    )(streamed(weights))


def key_kernel(count, *refs):
    rank_ref, modality_ref, gain_ref, head_ref, weight_ref = refs[:5]
    part_refs = refs[5 : 5 + count]
    memory_ref, raw_ref, normed_ref, factor_ref = refs[5 + count :]
    image = column(modality_ref[...]) > 0.0
    rows = in_order(rank_ref[0], part_refs).astype(f32)
    factor = inverse_norm(rows)
    scaling = jnp.where(image, gain_ref[1:2, :], gain_ref[0:1, :])
    normed_ref[...] = (rows * factor * scaling).astype(bf16)
    factor_ref[...] = row_of(factor)
    for index, (start, size) in enumerate(chunks_of(normed_ref.shape[1], 1792)):
        part = slice(start, start + size)
        product = both_experts(image, normed_ref[:, part], weight_ref[:, part, :])
        if index == 0:
            raw_ref[...] = product
        else:
            raw_ref[...] += product
    blocks = raw_ref.shape[1] // HEAD_DIM
    scaling = jnp.where(image, head_ref[1, 1:2, :], head_ref[0, 1:2, :])
    for b in range(blocks):
        part = slice(b * HEAD_DIM, (b + 1) * HEAD_DIM)
        raw = raw_ref[:, part]
        normed = raw * inverse_norm(raw) * scaling
        is_key = (rank_ref[0] * blocks + b) % 2 == 0
        memory_ref[:, part] = jnp.where(is_key, normed, raw).astype(bf16)


def key_stage(rank, modality, norm_gain, head_gain, weights, parts):
    _, depth, width = weights.shape
    rows = parts[0].shape[0]
    return pl.pallas_call(
        functools.partial(key_kernel, len(parts)),
        out_shape=[
            jax.ShapeDtypeStruct((rows, width), bf16),
            jax.ShapeDtypeStruct((rows, width), f32),
            jax.ShapeDtypeStruct((rows, depth), bf16),
            jax.ShapeDtypeStruct((1, rows), f32),
        ],
        in_specs=[SMEM] + [VMEM] * (4 + len(parts)),
        out_specs=[VMEM] * 4,
        compiler_params=params(12),
        cost_estimate=cost(0.2),
        name="key_stage",
    )(rank, modality, norm_gain, head_gain, weights, *parts)


def middle_kernel(count, output_pieces, query_pieces, *refs):
    rank_ref, modality_ref, head_ref, normed_ref, output_ref, query_weight_ref = refs[:6]
    part_refs = refs[6 : 6 + count]
    query_ref, raw_ref, back_ref, output_held = refs[6 + count : 10 + count]
    query_slots, output_sems, query_sems = refs[10 + count :]
    copies = copies_of(output_ref, output_held, output_sems, output_pieces)
    copies += copies_of(query_weight_ref, query_slots, query_sems, query_pieces, slots=AHEAD)
    begin_first(copies)
    image = column(modality_ref[...]) > 0.0
    cotangent = in_order(rank_ref[0], part_refs)
    for index, (start, size) in enumerate(output_pieces):
        arrive(copies, index)
        part = slice(start, start + size)
        back_ref[:, part] = both_back(image, cotangent, output_held[:, part, :]).astype(bf16)
        begin(copies, index + AHEAD)
    for index, (start, size) in enumerate(query_pieces):
        place = len(output_pieces) + index
        arrive(copies, place)
        part = slice(start, start + size)
        product = both_experts(image, normed_ref[:, part], query_slots[index % AHEAD])
        if index == 0:
            raw_ref[...] = product
        else:
            raw_ref[...] += product
        begin(copies, place + AHEAD)
    scaling = jnp.where(image, head_ref[1, 0:1, :], head_ref[0, 0:1, :])
    for h in range(raw_ref.shape[1] // HEAD_DIM):
        part = slice(h * HEAD_DIM, (h + 1) * HEAD_DIM)
        raw = raw_ref[:, part]
        query_ref[:, part] = (raw * inverse_norm(raw) * scaling).astype(bf16)


def middle_stage(rank, modality, head_gain, normed, output_weight, query_weight, parts):
    rows = normed.shape[0]
    width = query_weight.shape[2]
    output_pieces = chunks_of(output_weight.shape[1], 128)
    query_pieces = chunks_of(query_weight.shape[1], 512)
    return pl.pallas_call(
        functools.partial(middle_kernel, len(parts), output_pieces, query_pieces),
        out_shape=[
            jax.ShapeDtypeStruct((rows, width), bf16),
            jax.ShapeDtypeStruct((rows, width), f32),
            jax.ShapeDtypeStruct((rows, width), bf16),
            resident(output_weight),
        ],
        in_specs=[SMEM, VMEM, VMEM, VMEM, ANY, ANY] + [VMEM] * len(parts),
        out_specs=[VMEM] * 4,
        scratch_shapes=[
            ring(query_weight, query_pieces),
            pltpu.SemaphoreType.DMA((len(output_pieces), 2)),
            pltpu.SemaphoreType.DMA((len(query_pieces), 2)),
        ],
        compiler_params=params(16),
        cost_estimate=cost(0.2),
        name="middle_stage",
    )(rank, modality, head_gain, normed, streamed(output_weight), streamed(query_weight), *parts)


def attention_kernel(blocks, pairs, per_group, *refs):
    for pair in range(pairs):
        wide = pl.ds(pair * per_group * HEAD_DIM, per_group * HEAD_DIM)
        narrow = pl.ds(pair * 2 * HEAD_DIM, 2 * HEAD_DIM)
        views = list(refs[:4]) + [ref.at[:, wide] for ref in refs[4:7]]
        views += [ref.at[:, narrow] for ref in refs[7 : 7 + blocks]]
        views += [ref.at[:, wide] for ref in refs[7 + blocks : 9 + blocks]]
        views += [refs[9 + blocks]]
        views += [ref.at[:, narrow] for ref in refs[10 + blocks :]]
        attention_pair(blocks, per_group, pair == 0, *views)


def attention_pair(blocks, per_group, fresh, *refs):
    source_ref, segments_ref, modality_ref, head_ref, query_ref, raw_ref, back_ref = refs[:7]
    memory_refs = refs[7 : 7 + blocks]
    attended_ref, query_back_ref, inner_ref = refs[7 + blocks : 10 + blocks]
    grad_refs = refs[10 + blocks :]
    rows = query_ref.shape[0]
    scale = 1.0 / math.sqrt(HEAD_DIM)

    def heads(ref):
        return jnp.concatenate(
            [ref[:, h * HEAD_DIM : (h + 1) * HEAD_DIM] for h in range(per_group)], axis=0
        )

    query, back = heads(query_ref), heads(back_ref)
    key = jnp.concatenate([m[:, :HEAD_DIM] for m in memory_refs], axis=0)
    value = jnp.concatenate([m[:, HEAD_DIM:] for m in memory_refs], axis=0)
    key_segments = jnp.concatenate(
        [segments_ref[pl.ds(source_ref[b], 1), :] for b in range(blocks)], axis=1
    )
    query_segments = column(segments_ref[pl.ds(source_ref[0], 1), :])
    visible = jnp.where(key_segments.astype(f32) <= query_segments, 1.0, 0.0)
    visible = jnp.concatenate([visible] * per_group, axis=0)
    scores = dot_nt(query, key) * scale
    weights = jnp.where(visible > 0.0, jnp.exp(scores), 0.0).astype(bf16)
    weights32 = weights.astype(f32)
    denominator = jnp.sum(weights32, axis=1, keepdims=True)
    numerator = jnp.dot(weights, value, preferred_element_type=f32)
    attended = (numerator / denominator).astype(bf16)
    offset = jnp.sum(back.astype(f32) * attended.astype(f32), axis=1, keepdims=True)
    probability = (weights32 / denominator).astype(bf16)
    back_prob = dot_nt(back, value)
    back_score = (probability.astype(f32) * (back_prob - offset)).astype(bf16)
    back_query = jnp.dot(back_score, key, preferred_element_type=f32) * scale
    back_key = dot_tn(back_score, query) * scale
    back_value = dot_tn(probability, back)
    for b in range(blocks):
        part = slice(b * rows, (b + 1) * rows)
        grad_refs[b][:, :HEAD_DIM] = back_key[part].astype(grad_refs[b].dtype)
        grad_refs[b][:, HEAD_DIM:] = back_value[part].astype(grad_refs[b].dtype)
    image = column(modality_ref[...]) > 0.0
    scaling = jnp.where(image, head_ref[1, 0:1, :], head_ref[0, 0:1, :])
    inner = jnp.zeros((rows, 1), f32)
    for h in range(per_group):
        part = slice(h * rows, (h + 1) * rows)
        columns = slice(h * HEAD_DIM, (h + 1) * HEAD_DIM)
        attended_ref[:, columns] = attended[part]
        raw = raw_ref[:, columns]
        query_back = norm_back(raw, inverse_norm(raw), scaling, back_query[part]).astype(bf16)
        query_back_ref[:, columns] = query_back
        inner += jnp.sum(query_back.astype(f32) * raw, axis=1, keepdims=True)
    inner = row_of(inner)

    if fresh:
        inner_ref[...] = inner
    else:
        inner_ref[...] += inner


def attention_stage(sources, segments, modality, head_gain, query, raw, back, memories):
    rows, width = query.shape
    blocks = len(memories)
    pairs = memories[0].shape[1] // (2 * HEAD_DIM)
    per_group = width // HEAD_DIM // pairs
    outs = [
        jax.ShapeDtypeStruct((rows, width), bf16),
        jax.ShapeDtypeStruct((rows, width), bf16),
        jax.ShapeDtypeStruct((1, rows), f32),
    ] + [
        jax.ShapeDtypeStruct((rows, pairs * 2 * HEAD_DIM), f32 if b == 0 else bf16)
        for b in range(blocks)
    ]
    return pl.pallas_call(
        functools.partial(attention_kernel, blocks, pairs, per_group),
        out_shape=outs,
        in_specs=[SMEM] + [VMEM] * (6 + blocks),
        out_specs=[VMEM] * (3 + blocks),
        compiler_params=params(16),
        cost_estimate=cost(0.2),
        name="attention_stage",
    )(sources, segments, modality, head_gain, query, raw, back, *memories)


def half(rank, extent, other):
    size = extent // 2
    place = 1 - rank if other else rank
    return pl.ds(pl.multiple_of(place * size, HEAD_DIM), size)


def turn_kernel(pieces, outputs, *refs):
    rank_ref, modality_ref, output_ref, attended_ref, back_ref, query_ref = refs[:6]
    out_refs = refs[6 : 6 + outputs]
    part_ref, slots, sems = refs[6 + outputs :]
    copies = copies_of(query_ref, slots, sems, pieces, slots=AHEAD)
    begin_first(copies)
    image = column(modality_ref[...]) > 0.0
    attended = attended_ref[...]
    width = output_ref.shape[2]
    if outputs == 1:
        out_refs[0][...] = both_experts(image, attended, output_ref[...]).astype(bf16)
    else:
        sent_ref, kept_ref = out_refs
        weights = output_ref[:, :, half(rank_ref[0], width, True)]
        sent_ref[...] = both_experts(image, attended, weights).astype(bf16)
        weights = output_ref[:, :, half(rank_ref[0], width, False)]
        kept_ref[...] = both_experts(image, attended, weights)
    for index, (start, size) in enumerate(pieces):
        arrive(copies, index)
        part = slice(start, start + size)
        part_ref[:, part] = both_back(image, back_ref[...], slots[index % AHEAD])
        begin(copies, index + AHEAD)


def turn_stage(rank, modality, output_held, attended, query_back, query_weight, split):
    depth = query_weight.shape[1]
    width = output_held.shape[2]
    rows = attended.shape[0]
    pieces = chunks_of(depth, 512)
    if split:
        outs = [
            jax.ShapeDtypeStruct((rows, width // 2), bf16),
            jax.ShapeDtypeStruct((rows, width // 2), f32),
        ]
    else:
        outs = [jax.ShapeDtypeStruct((rows, width), bf16)]
    *projected, part = pl.pallas_call(
        functools.partial(turn_kernel, pieces, len(outs)),
        out_shape=outs + [jax.ShapeDtypeStruct((rows, depth), f32)],
        in_specs=[SMEM, VMEM, VMEM, VMEM, VMEM, ANY],
        out_specs=[VMEM] * (len(outs) + 1),
        scratch_shapes=[
            ring(query_weight, pieces),
            pltpu.SemaphoreType.DMA((len(pieces), 2)),
        ],
        compiler_params=params(16),
        cost_estimate=cost(0.2),
        name="turn_stage",
    )(rank, modality, output_held, attended, query_back, streamed(query_weight))
    return projected, part


def back_pieces(depth, split):
    return chunks_of(depth // 2 if split else depth, 896)


def key_back_kernel(split, *refs):
    rank_ref, modality_ref, head_ref, raw_ref, inner_in_ref, part_ref, weight_ref = refs[:7]
    grad_refs = refs[8:-6]
    out_ref, back_ref, inner_ref = refs[-6:-3]
    held, sems = refs[-2:]
    depth = part_ref.shape[1]
    base = pl.multiple_of((1 - rank_ref[0]) * (depth // 2), HEAD_DIM) if split else 0
    pieces = back_pieces(depth, split)
    copies = copies_of(weight_ref, held, sems, pieces, base)
    for index in range(len(copies)):
        begin(copies, index)
    image = column(modality_ref[...]) > 0.0
    blocks = raw_ref.shape[1] // HEAD_DIM
    scaling = jnp.where(image, head_ref[1, 1:2, :], head_ref[0, 1:2, :])
    inner = jnp.zeros((raw_ref.shape[0], 1), f32)
    for b in range(blocks):
        part = slice(b * HEAD_DIM, (b + 1) * HEAD_DIM)
        raw = raw_ref[:, part]
        upstream = grad_refs[0][:, part].astype(f32)
        for grad_ref in grad_refs[1:]:
            upstream += grad_ref[:, part].astype(f32)
        is_key = (rank_ref[0] * blocks + b) % 2 == 0
        normed_back = norm_back(raw, inverse_norm(raw), scaling, upstream)
        back = jnp.where(is_key, normed_back, upstream).astype(bf16)
        back_ref[:, part] = back
        inner += jnp.sum(back.astype(f32) * raw, axis=1, keepdims=True)
    inner_ref[...] = inner_in_ref[...] + row_of(inner)
    for index, (start, size) in enumerate(pieces):
        arrive(copies, index)
        part = slice(start, start + size)
        product = both_back(image, back_ref[...], held[:, part, :])
        given = part_ref[:, pl.ds(base + start, size)]
        out_ref[:, part] = (product + given).astype(bf16)


def key_back_stage(rank, modality, head_gain, raw, inner, part, weights, passed, grads, split):
    _, depth, width = weights.shape
    rows = raw.shape[0]
    pieces = back_pieces(depth, split)
    extent = depth // 2 if split else depth
    return pl.pallas_call(
        functools.partial(key_back_kernel, split),
        out_shape=[
            jax.ShapeDtypeStruct((rows, extent), bf16),
            jax.ShapeDtypeStruct((rows, width), bf16),
            jax.ShapeDtypeStruct((1, rows), f32),
            jax.ShapeDtypeStruct(passed.shape, passed.dtype),
        ],
        in_specs=[SMEM] + [VMEM] * 5 + [ANY, ANY] + [VMEM] * len(grads),
        out_specs=[VMEM] * 3 + [ANY],
        scratch_shapes=[
            pltpu.VMEM((2, extent, width), bf16),
            pltpu.SemaphoreType.DMA((len(pieces), 2)),
        ],
        input_output_aliases={7: 3},
        compiler_params=params(12),
        cost_estimate=cost(0.2),
        name="key_back_stage",
    )(rank, modality, head_gain, raw, inner, part, streamed(weights), passed, *grads)


def kept_kernel(rank_ref, modality_ref, part_ref, weight_ref, back_ref, out_ref, held, sems):
    depth = part_ref.shape[1]
    base = pl.multiple_of(rank_ref[0] * (depth // 2), HEAD_DIM)
    pieces = back_pieces(depth, True)
    copies = copies_of(weight_ref, held, sems, pieces, base)
    for index in range(len(copies)):
        begin(copies, index)
    image = column(modality_ref[...]) > 0.0
    for index, (start, size) in enumerate(pieces):
        arrive(copies, index)
        part = slice(start, start + size)
        product = both_back(image, back_ref[...], held[:, part, :])
        out_ref[:, part] = product + part_ref[:, pl.ds(base + start, size)]


def kept_stage(rank, modality, part, weights, back):
    _, depth, width = weights.shape
    pieces = back_pieces(depth, True)
    return pl.pallas_call(
        kept_kernel,
        out_shape=jax.ShapeDtypeStruct((back.shape[0], depth // 2), f32),
        in_specs=[SMEM, VMEM, VMEM, ANY, VMEM],
        out_specs=VMEM,
        scratch_shapes=[
            pltpu.VMEM((2, depth // 2, width), bf16),
            pltpu.SemaphoreType.DMA((len(pieces), 2)),
        ],
        compiler_params=params(12),
        cost_estimate=cost(0.2),
        name="kept_stage",
    )(rank, modality, part, streamed(weights), back)


def finish(total_width, count, modality, gain, factor, inputs, backs, inners):
    rows, width = inputs.shape

    def kernel(modality_ref, gain_ref, factor_ref, inputs_ref, *refs):
        back_refs = refs[:count]
        inner_refs, out_ref = refs[count:-1], refs[-1]
        image = column(modality_ref[...]) > 0.0
        scaling = jnp.where(image, gain_ref[1:2, :], gain_ref[0:1, :])
        factor_column = column(factor_ref[...])
        back = back_refs[0][...].astype(f32)
        for ref in back_refs[1:]:
            back += ref[...].astype(f32)
        inner = inner_refs[0][...]
        for ref in inner_refs[1:]:
            inner += ref[...]
        unit_rows = inputs_ref[...].astype(f32) * factor_column
        inner_mean = column(inner) * (1.0 / total_width)
        out_ref[...] = (factor_column * (scaling * back - unit_rows * inner_mean)).astype(bf16)

    arrays = [modality, gain, factor, inputs, *backs, *inners]
    return pl.pallas_call(
        kernel,
        out_shape=jax.ShapeDtypeStruct((rows, width), bf16),
        in_specs=[VMEM] * len(arrays),
        out_specs=VMEM,
        compiler_params=params(12),
        cost_estimate=cost(0.2),
        name="finish",
    )(*arrays)


def local(
    inputs,
    cotangent,
    norm_gain,
    head_gain,
    query_weight,
    key_weight,
    output_weight,
    modality,
    segments,
    block_order,
):
    tensor_rank = lax.axis_index("tensor")
    block_rank = lax.axis_index("seq")
    tensor_count = lax.axis_size("tensor")
    block_count = lax.axis_size("seq")
    local_rows, local_width = inputs.shape
    full_width = local_width * tensor_count
    split = tensor_count == 2
    swap = [(0, 1), (1, 0)]
    rank = tensor_rank.astype(jnp.int32).reshape(1)
    modality = modality.reshape(1, local_rows)
    segments = segments.reshape(block_count, local_rows)

    def spread(part):
        if split:
            return [part, lax.ppermute(part, "tensor", swap)]
        return [lax.all_gather(part, "tensor", axis=1, tiled=True)]

    def scatter_columns(part):
        return lax.psum_scatter(part, "tensor", scatter_dimension=1, tiled=True)

    memory, key_raw, normed, row_factor = key_stage(
        rank, modality, norm_gain, head_gain, fetch(key_weight), spread(inputs)
    )
    shared = tensor_count > KV_HEADS
    is_even = tensor_rank % 2 == 0
    pair_swap = [(i, i ^ 1) for i in range(tensor_count)]
    if shared:
        partner = lax.ppermute(memory, "tensor", pair_swap)
        memory = jnp.where(
            is_even,
            jnp.concatenate([memory, partner], 1),
            jnp.concatenate([partner, memory], 1),
        )
    memories, order = [memory], [block_rank]
    for step in range(1, block_count):
        memories.append(lax.ppermute(memory, "seq", seq_pairs(step, block_count)))
        order.append(seq_source(block_rank, step, block_count))
    sources = block_order[jnp.stack(order)]

    query, query_raw, back_attended, output_held = middle_stage(
        rank, modality, head_gain, normed, output_weight, query_weight, spread(cotangent)
    )
    attended, query_back, inner, own_grad, *grads = attention_stage(
        sources, segments, modality, head_gain, query, query_raw, back_attended, memories
    )
    incoming = [
        lax.ppermute(grad, "seq", inverted(seq_pairs(step, block_count)))
        for step, grad in enumerate(grads, 1)
    ]

    projected, gradient_part = turn_stage(
        rank, modality, output_held, attended, query_back, query_weight, split
    )
    if shared:
        total = own_grad + sum(grad.astype(f32) for grad in incoming)
        low, high = total[:, :HEAD_DIM], total[:, HEAD_DIM:]
        outgoing = jnp.where(is_even, high, low).astype(bf16)
        sums = [jnp.where(is_even, low, high), lax.ppermute(outgoing, "tensor", pair_swap)]
    else:
        sums = [own_grad, *incoming]
    sent, slice_back, inner, passed = key_back_stage(
        rank,
        modality,
        head_gain,
        key_raw,
        inner,
        gradient_part,
        key_weight,
        projected[0],
        sums,
        split,
    )
    if split:
        inners = [inner, lax.ppermute(inner, "tensor", swap)]
        other = lax.ppermute(sent, "tensor", swap)
        kept = kept_stage(rank, modality, gradient_part, key_weight, slice_back)
        backs = [kept, other]
        attention_out = projected[1] + lax.ppermute(passed, "tensor", swap).astype(f32)
        attention_out = attention_out.astype(bf16)
    else:
        inners = [lax.psum(inner, "tensor")]
        backs = [scatter_columns(sent)]
        attention_out = scatter_columns(passed)
    gain = lax.dynamic_slice_in_dim(norm_gain, tensor_rank * local_width, local_width, 1)
    grad_input = finish(
        full_width, len(backs), modality, gain, row_factor, inputs, backs, inners
    )
    return (attention_out, grad_input)


def solution(mesh):
    return jax.shard_map(
        local,
        mesh=mesh,
        in_specs=(
            P(("dp", "seq"), "tensor"),
            P(("dp", "seq"), "tensor"),
            P(),
            P(),
            P(None, None, "tensor"),
            P(None, None, "tensor"),
            P(None, "tensor", None),
            P(("dp", "seq")),
            P("dp"),
            P("dp"),
        ),
        out_specs=(P(("dp", "seq"), "tensor"), P(("dp", "seq"), "tensor")),
        check_vma=False,
    )
```

```python
import functools
import math

import jax
import jax.numpy as jnp
from jax import lax
from jax.experimental import pallas as pl
from jax.experimental.pallas import tpu as pltpu
from jax.sharding import PartitionSpec as P

KV_HEADS = 4
HEAD_DIM = 128
MIB = 1024 * 1024

epsilon = 1e-06
bf16 = jnp.bfloat16
f32 = jnp.float32
SMEM = pl.BlockSpec(memory_space=pltpu.SMEM)
VMEM = pl.BlockSpec(memory_space=pltpu.VMEM)
ANY = pl.BlockSpec(memory_space=pl.ANY)


def seq_pairs(step, count):
    if count & (count - 1) == 0:
        return [(i, i ^ step) for i in range(count)]
    return [(i, (i + step) % count) for i in range(count)]


def seq_source(rank, step, count):
    if count & (count - 1) == 0:
        return rank ^ step
    return (rank - step) % count


def inverted(pairs):
    return [(b, a) for a, b in pairs]


def tile_of(extent, most):
    best = HEAD_DIM
    for size in range(HEAD_DIM, min(extent, most) + 1, HEAD_DIM):
        if extent % size == 0:
            best = size
    return best


def dot_nt(a, b):
    return lax.dot_general(a, b, (((1,), (1,)), ((), ())), preferred_element_type=f32)


def dot_tn(a, b):
    return lax.dot_general(a, b, (((0,), (0,)), ((), ())), preferred_element_type=f32)


def column(row):
    count = row.shape[1]
    return jnp.broadcast_to(row.astype(f32), (count, count)).T[:, :1]


def row_of(col):
    count = col.shape[0]
    return jnp.broadcast_to(col, (count, count)).T[:1, :]


def inverse_norm(values):
    return lax.rsqrt(jnp.mean(values * values, axis=-1, keepdims=True) + epsilon)


def norm_back(values, factor, scaling, upstream):
    unit_rows = values * factor
    inner_mean = jnp.mean(scaling * upstream * unit_rows, axis=-1, keepdims=True)
    return factor * (scaling * upstream - unit_rows * inner_mean)


def streamed(weights):
    return pltpu.with_memory_space_constraint(weights, pltpu.HBM)


def params(mib):
    return pltpu.CompilerParams(vmem_limit_bytes=mib * MIB)


def cost(micros):
    return pl.CostEstimate(
        flops=int(micros * 1e9), bytes_accessed=int(micros * 2e6), transcendentals=0
    )


def in_order(rank, part_refs):
    if len(part_refs) == 1:
        return part_refs[0][...]
    own, other = part_refs[0][...], part_refs[1][...]
    first = rank == 0
    return jnp.concatenate([jnp.where(first, own, other), jnp.where(first, other, own)], axis=1)


def both_experts(image, rows, weights):
    zero = jnp.zeros_like(rows)
    masked = jnp.concatenate([jnp.where(image, zero, rows), jnp.where(image, rows, zero)], axis=1)
    flat = weights.reshape(2 * weights.shape[1], weights.shape[2])
    return jnp.dot(masked, flat, preferred_element_type=f32)


def both_back(image, rows, weights):
    return jnp.where(image, dot_nt(rows, weights[1]), dot_nt(rows, weights[0]))


def chunks_of(extent, most):
    size = tile_of(extent, most)
    return [(start, size) for start in range(0, extent, size)]


AHEAD = 4


def copies_of(source_ref, target_ref, sem_ref, pieces, base=0, slots=0):
    copies = []
    for index, (start, size) in enumerate(pieces):
        pair = []
        for e in range(2):
            if slots:
                target = target_ref.at[index % slots, e]
            else:
                target = target_ref.at[e, pl.ds(start, size), :]
            source = source_ref.at[e, pl.ds(base + start, size), :]
            pair.append(pltpu.make_async_copy(source, target, sem_ref.at[index, e]))
        copies.append(pair)
    return copies


def begin(copies, index):
    if index < len(copies):
        for copy in copies[index]:
            copy.start()


def begin_first(copies):
    for index in range(AHEAD):
        begin(copies, index)


def arrive(copies, index):
    for copy in copies[index]:
        copy.wait()


def ring(weights, pieces):
    return pltpu.VMEM((AHEAD, 2, pieces[0][1], weights.shape[2]), weights.dtype)


def resident(weights):
    return pltpu.VMEM(weights.shape, weights.dtype)


def fetch_kernel(pieces, weight_ref, held_ref, sem_ref):
    copies = copies_of(weight_ref, held_ref, sem_ref, pieces)
    for pair in copies:
        for copy in pair:
            copy.start()
    for pair in copies:
        for copy in pair:
            copy.wait()


def fetch(weights):
    pieces = chunks_of(weights.shape[1], 896)
    return pl.pallas_call(
        functools.partial(fetch_kernel, pieces),
        out_shape=resident(weights),
        in_specs=[ANY],
        out_specs=VMEM,
        scratch_shapes=[pltpu.SemaphoreType.DMA((len(pieces), 2))],
        compiler_params=params(1),
        cost_estimate=cost(0.2),
        name="fetch",
    )(streamed(weights))


def key_kernel(count, *refs):
    rank_ref, modality_ref, gain_ref, head_ref, weight_ref = refs[:5]
    part_refs = refs[5 : 5 + count]
    memory_ref, raw_ref, normed_ref, factor_ref = refs[5 + count :]
    image = column(modality_ref[...]) > 0.0
    rows = in_order(rank_ref[0], part_refs).astype(f32)
    factor = inverse_norm(rows)
    scaling = jnp.where(image, gain_ref[1:2, :], gain_ref[0:1, :])
    normed_ref[...] = (rows * factor * scaling).astype(bf16)
    factor_ref[...] = row_of(factor)
    for index, (start, size) in enumerate(chunks_of(normed_ref.shape[1], 1792)):
        part = slice(start, start + size)
        product = both_experts(image, normed_ref[:, part], weight_ref[:, part, :])
        if index == 0:
            raw_ref[...] = product
        else:
            raw_ref[...] += product
    blocks = raw_ref.shape[1] // HEAD_DIM
    scaling = jnp.where(image, head_ref[1, 1:2, :], head_ref[0, 1:2, :])
    for b in range(blocks):
        part = slice(b * HEAD_DIM, (b + 1) * HEAD_DIM)
        raw = raw_ref[:, part]
        normed = raw * inverse_norm(raw) * scaling
        is_key = (rank_ref[0] * blocks + b) % 2 == 0
        memory_ref[:, part] = jnp.where(is_key, normed, raw).astype(bf16)


def key_stage(rank, modality, norm_gain, head_gain, weights, parts):
    _, depth, width = weights.shape
    rows = parts[0].shape[0]
    return pl.pallas_call(
        functools.partial(key_kernel, len(parts)),
        out_shape=[
            jax.ShapeDtypeStruct((rows, width), bf16),
            jax.ShapeDtypeStruct((rows, width), f32),
            jax.ShapeDtypeStruct((rows, depth), bf16),
            jax.ShapeDtypeStruct((1, rows), f32),
        ],
        in_specs=[SMEM] + [VMEM] * (4 + len(parts)),
        out_specs=[VMEM] * 4,
        compiler_params=params(8),
        cost_estimate=cost(10),
        name="key_stage",
    )(rank, modality, norm_gain, head_gain, weights, *parts)


def middle_kernel(count, pieces, *refs):
    rank_ref, modality_ref, head_ref, normed_ref, output_ref, query_weight_ref = refs[:6]
    part_refs = refs[6 : 6 + count]
    query_ref, raw_ref, back_ref, slots, sems = refs[6 + count :]
    copies = copies_of(query_weight_ref, slots, sems, pieces, slots=AHEAD)
    begin_first(copies)
    image = column(modality_ref[...]) > 0.0
    cotangent = in_order(rank_ref[0], part_refs)
    for start, size in chunks_of(output_ref.shape[1], 256):
        part = slice(start, start + size)
        back_ref[:, part] = both_back(image, cotangent, output_ref[:, part, :]).astype(bf16)
    for index, (start, size) in enumerate(pieces):
        arrive(copies, index)
        part = slice(start, start + size)
        product = both_experts(image, normed_ref[:, part], slots[index % AHEAD])
        if index == 0:
            raw_ref[...] = product
        else:
            raw_ref[...] += product
        begin(copies, index + AHEAD)
    scaling = jnp.where(image, head_ref[1, 0:1, :], head_ref[0, 0:1, :])
    for h in range(raw_ref.shape[1] // HEAD_DIM):
        part = slice(h * HEAD_DIM, (h + 1) * HEAD_DIM)
        raw = raw_ref[:, part]
        query_ref[:, part] = (raw * inverse_norm(raw) * scaling).astype(bf16)


def middle_stage(rank, modality, head_gain, normed, output_weight, query_weight, parts):
    rows = normed.shape[0]
    width = query_weight.shape[2]
    pieces = chunks_of(query_weight.shape[1], 512)
    return pl.pallas_call(
        functools.partial(middle_kernel, len(parts), pieces),
        out_shape=[
            jax.ShapeDtypeStruct((rows, width), bf16),
            jax.ShapeDtypeStruct((rows, width), f32),
            jax.ShapeDtypeStruct((rows, width), bf16),
        ],
        in_specs=[SMEM, VMEM, VMEM, VMEM, VMEM, ANY] + [VMEM] * len(parts),
        out_specs=[VMEM] * 3,
        scratch_shapes=[
            ring(query_weight, pieces),
            pltpu.SemaphoreType.DMA((len(pieces), 2)),
        ],
        compiler_params=params(14),
        cost_estimate=cost(8),
        name="middle_stage",
    )(rank, modality, head_gain, normed, output_weight, streamed(query_weight), *parts)


def attention_kernel(blocks, pairs, per_group, *refs):
    for pair in range(pairs):
        wide = pl.ds(pair * per_group * HEAD_DIM, per_group * HEAD_DIM)
        narrow = pl.ds(pair * 2 * HEAD_DIM, 2 * HEAD_DIM)
        views = list(refs[:5]) + [ref.at[:, wide] for ref in refs[5:8]]
        views += [ref.at[:, narrow] for ref in refs[8 : 8 + blocks]]
        views += [ref.at[:, wide] for ref in refs[8 + blocks : 10 + blocks]]
        views += [refs[10 + blocks]]
        views += [ref.at[:, narrow] for ref in refs[11 + blocks :]]
        attention_pair(blocks, per_group, pair == 0, *views)


def attention_pair(blocks, per_group, fresh, *refs):
    place_ref, order_ref, segments_ref, modality_ref, head_ref = refs[:5]
    query_ref, raw_ref, back_ref = refs[5:8]
    memory_refs = refs[8 : 8 + blocks]
    attended_ref, query_back_ref, inner_ref = refs[8 + blocks : 11 + blocks]
    grad_refs = refs[11 + blocks :]
    rows = query_ref.shape[0]
    scale = 1.0 / math.sqrt(HEAD_DIM)

    def heads(ref):
        return jnp.concatenate(
            [ref[:, h * HEAD_DIM : (h + 1) * HEAD_DIM] for h in range(per_group)], axis=0
        )

    query, back = heads(query_ref), heads(back_ref)
    key = jnp.concatenate([m[:, :HEAD_DIM] for m in memory_refs], axis=0)
    value = jnp.concatenate([m[:, HEAD_DIM:] for m in memory_refs], axis=0)
    lines = [
        segments_ref[pl.ds(order_ref[seq_source(place_ref[0], b, blocks)], 1), :]
        for b in range(blocks)
    ]
    key_segments = jnp.concatenate(lines, axis=1)
    query_segments = column(lines[0])
    visible = jnp.where(key_segments.astype(f32) <= query_segments, 1.0, 0.0)
    visible = jnp.concatenate([visible] * per_group, axis=0)
    scores = dot_nt(query, key) * scale
    weights = jnp.where(visible > 0.0, jnp.exp(scores), 0.0).astype(bf16)
    weights32 = weights.astype(f32)
    denominator = jnp.sum(weights32, axis=1, keepdims=True)
    numerator = jnp.dot(weights, value, preferred_element_type=f32)
    attended = (numerator / denominator).astype(bf16)
    offset = jnp.sum(back.astype(f32) * attended.astype(f32), axis=1, keepdims=True)
    probability = (weights32 / denominator).astype(bf16)
    back_prob = dot_nt(back, value)
    back_score = (probability.astype(f32) * (back_prob - offset)).astype(bf16)
    back_query = jnp.dot(back_score, key, preferred_element_type=f32) * scale
    back_key = dot_tn(back_score, query) * scale
    back_value = dot_tn(probability, back)
    for b in range(blocks):
        part = slice(b * rows, (b + 1) * rows)
        grad_refs[b][:, :HEAD_DIM] = back_key[part].astype(grad_refs[b].dtype)
        grad_refs[b][:, HEAD_DIM:] = back_value[part].astype(grad_refs[b].dtype)
    image = column(modality_ref[...]) > 0.0
    scaling = jnp.where(image, head_ref[1, 0:1, :], head_ref[0, 0:1, :])
    inner = jnp.zeros((rows, 1), f32)
    for h in range(per_group):
        part = slice(h * rows, (h + 1) * rows)
        columns = slice(h * HEAD_DIM, (h + 1) * HEAD_DIM)
        attended_ref[:, columns] = attended[part]
        raw = raw_ref[:, columns]
        query_back = norm_back(raw, inverse_norm(raw), scaling, back_query[part]).astype(bf16)
        query_back_ref[:, columns] = query_back
        inner += jnp.sum(query_back.astype(f32) * raw, axis=1, keepdims=True)
    inner = row_of(inner)

    if fresh:
        inner_ref[...] = inner
    else:
        inner_ref[...] += inner


def attention_stage(place, order, segments, modality, head_gain, query, raw, back, memories):
    rows, width = query.shape
    blocks = len(memories)
    pairs = memories[0].shape[1] // (2 * HEAD_DIM)
    per_group = width // HEAD_DIM // pairs
    outs = [
        jax.ShapeDtypeStruct((rows, width), bf16),
        jax.ShapeDtypeStruct((rows, width), bf16),
        jax.ShapeDtypeStruct((1, rows), f32),
    ] + [
        jax.ShapeDtypeStruct((rows, pairs * 2 * HEAD_DIM), f32 if b == 0 else bf16)
        for b in range(blocks)
    ]
    return pl.pallas_call(
        functools.partial(attention_kernel, blocks, pairs, per_group),
        out_shape=outs,
        in_specs=[SMEM, SMEM] + [VMEM] * (6 + blocks),
        out_specs=[VMEM] * (3 + blocks),
        compiler_params=params(12),
        cost_estimate=cost(4),
        name="attention_stage",
    )(place, order, segments, modality, head_gain, query, raw, back, *memories)


def turn_kernel(pieces, outputs, *refs):
    rank_ref, modality_ref, output_ref, attended_ref, back_ref, query_ref = refs[:6]
    out_refs = refs[6 : 6 + outputs]
    part_ref, slots, sems = refs[6 + outputs :]
    copies = copies_of(query_ref, slots, sems, pieces, slots=AHEAD)
    begin_first(copies)
    image = column(modality_ref[...]) > 0.0
    attended = attended_ref[...]
    extent = output_ref.shape[2] // 2

    def project(rank):
        sent_ref, kept_ref = out_refs
        for start, size in chunks_of(extent, 896):
            part = slice(start, start + size)
            first = (1 - rank) * extent + start
            product = both_experts(image, attended, output_ref[:, :, first : first + size])
            sent_ref[:, part] = product.astype(bf16)
            first = rank * extent + start
            product = both_experts(image, attended, output_ref[:, :, first : first + size])
            kept_ref[:, part] = product

    if outputs == 1:
        out_refs[0][...] = both_experts(image, attended, output_ref[...]).astype(bf16)
    else:
        for rank in range(2):
            pl.when(rank_ref[0] == rank)(functools.partial(project, rank))
    for index, (start, size) in enumerate(pieces):
        arrive(copies, index)
        part = slice(start, start + size)
        part_ref[:, part] = both_back(image, back_ref[...], slots[index % AHEAD])
        begin(copies, index + AHEAD)


def turn_stage(rank, modality, output_weight, attended, query_back, query_weight, split):
    depth = query_weight.shape[1]
    width = output_weight.shape[2]
    rows = attended.shape[0]
    pieces = chunks_of(depth, 512)
    if split:
        outs = [
            jax.ShapeDtypeStruct((rows, width // 2), bf16),
            jax.ShapeDtypeStruct((rows, width // 2), f32),
        ]
    else:
        outs = [jax.ShapeDtypeStruct((rows, width), bf16)]
    *projected, part = pl.pallas_call(
        functools.partial(turn_kernel, pieces, len(outs)),
        out_shape=outs + [jax.ShapeDtypeStruct((rows, depth), f32)],
        in_specs=[SMEM, VMEM, VMEM, VMEM, VMEM, ANY],
        out_specs=[VMEM] * (len(outs) + 1),
        scratch_shapes=[
            ring(query_weight, pieces),
            pltpu.SemaphoreType.DMA((len(pieces), 2)),
        ],
        compiler_params=params(16),
        cost_estimate=cost(10),
        name="turn_stage",
    )(rank, modality, output_weight, attended, query_back, streamed(query_weight))
    return projected, part


def key_back_kernel(split, *refs):
    rank_ref, modality_ref, head_ref, raw_ref, inner_in_ref, part_ref, weight_ref = refs[:7]
    grad_refs = refs[8:-4]
    out_ref, back_ref, inner_ref = refs[-4:-1]
    base = pl.multiple_of((1 - rank_ref[0]) * out_ref.shape[1], HEAD_DIM) if split else 0
    image = column(modality_ref[...]) > 0.0
    blocks = raw_ref.shape[1] // HEAD_DIM
    scaling = jnp.where(image, head_ref[1, 1:2, :], head_ref[0, 1:2, :])
    inner = jnp.zeros((raw_ref.shape[0], 1), f32)
    for b in range(blocks):
        part = slice(b * HEAD_DIM, (b + 1) * HEAD_DIM)
        raw = raw_ref[:, part]
        upstream = grad_refs[0][:, part].astype(f32)
        for grad_ref in grad_refs[1:]:
            upstream += grad_ref[:, part].astype(f32)
        is_key = (rank_ref[0] * blocks + b) % 2 == 0
        normed_back = norm_back(raw, inverse_norm(raw), scaling, upstream)
        back = jnp.where(is_key, normed_back, upstream).astype(bf16)
        back_ref[:, part] = back
        inner += jnp.sum(back.astype(f32) * raw, axis=1, keepdims=True)
    inner_ref[...] = inner_in_ref[...] + row_of(inner)
    for start, size in chunks_of(out_ref.shape[1], 896):
        place = pl.ds(base + start, size)
        product = both_back(image, back_ref[...], weight_ref[:, place, :])
        out_ref[:, start : start + size] = (product + part_ref[:, place]).astype(bf16)


def key_back_stage(rank, modality, head_gain, raw, inner, part, weights, passed, grads, split):
    _, depth, width = weights.shape
    rows = raw.shape[0]
    return pl.pallas_call(
        functools.partial(key_back_kernel, split),
        out_shape=[
            jax.ShapeDtypeStruct((rows, depth // 2 if split else depth), bf16),
            jax.ShapeDtypeStruct((rows, width), bf16),
            jax.ShapeDtypeStruct((1, rows), f32),
            jax.ShapeDtypeStruct(passed.shape, passed.dtype),
        ],
        in_specs=[SMEM] + [VMEM] * 6 + [ANY] + [VMEM] * len(grads),
        out_specs=[VMEM] * 3 + [ANY],
        input_output_aliases={7: 3},
        compiler_params=params(6),
        cost_estimate=cost(2),
        name="key_back_stage",
    )(rank, modality, head_gain, raw, inner, part, weights, passed, *grads)


def kept_kernel(rank_ref, modality_ref, part_ref, weight_ref, back_ref, out_ref):
    base = pl.multiple_of(rank_ref[0] * out_ref.shape[1], HEAD_DIM)
    image = column(modality_ref[...]) > 0.0
    for start, size in chunks_of(out_ref.shape[1], 896):
        place = pl.ds(base + start, size)
        product = both_back(image, back_ref[...], weight_ref[:, place, :])
        out_ref[:, start : start + size] = product + part_ref[:, place]


def kept_stage(rank, modality, part, weights, back):
    return pl.pallas_call(
        kept_kernel,
        out_shape=jax.ShapeDtypeStruct((back.shape[0], weights.shape[1] // 2), f32),
        in_specs=[SMEM] + [VMEM] * 4,
        out_specs=VMEM,
        compiler_params=params(6),
        cost_estimate=cost(2),
        name="kept_stage",
    )(rank, modality, part, weights, back)


def finish_kernel(backs, inners, total_width, *refs):
    rank_ref, modality_ref, gain_ref, factor_ref, inputs_ref = refs[:5]
    back_refs = refs[5 : 5 + backs]
    inner_refs = refs[5 + backs : 5 + backs + inners]
    rest = refs[5 + backs + inners :]
    out_ref = rest[-1]
    width = inputs_ref.shape[1]
    image = column(modality_ref[...]) > 0.0
    gain = gain_ref[...]
    if gain.shape[1] != width:
        gain = gain_ref[:, pl.ds(pl.multiple_of(rank_ref[0] * width, HEAD_DIM), width)]
    scaling = jnp.where(image, gain[1:2, :], gain[0:1, :])
    factor = column(factor_ref[...])
    back = back_refs[0][...].astype(f32)
    for ref in back_refs[1:]:
        back += ref[...].astype(f32)
    inner = inner_refs[0][...]
    for ref in inner_refs[1:]:
        inner += ref[...]
    unit_rows = inputs_ref[...].astype(f32) * factor
    inner_mean = column(inner) * (1.0 / total_width)
    out_ref[...] = (factor * (scaling * back - unit_rows * inner_mean)).astype(bf16)
    if len(rest) == 4:
        kept_ref, other_ref, attention_ref, _ = rest
        attention_ref[...] = (kept_ref[...] + other_ref[...].astype(f32)).astype(bf16)


def finish(rank, total_width, modality, gain, factor, inputs, backs, inners, projected):
    shape = jax.ShapeDtypeStruct(inputs.shape, bf16)
    arrays = [modality, gain, factor, inputs, *backs, *inners, *projected]
    outs = [shape] * (2 if projected else 1)
    return pl.pallas_call(
        functools.partial(finish_kernel, len(backs), len(inners), total_width),
        out_shape=outs,
        in_specs=[SMEM] + [VMEM] * len(arrays),
        out_specs=[VMEM] * len(outs),
        compiler_params=params(6),
        cost_estimate=cost(1),
        name="finish",
    )(rank, *arrays)


def local(
    inputs,
    cotangent,
    norm_gain,
    head_gain,
    query_weight,
    key_weight,
    output_weight,
    modality,
    segments,
    block_order,
):
    tensor_rank = lax.axis_index("tensor")
    block_rank = lax.axis_index("seq")
    tensor_count = lax.axis_size("tensor")
    block_count = lax.axis_size("seq")
    local_rows, local_width = inputs.shape
    full_width = local_width * tensor_count
    split = tensor_count == 2
    swap = [(0, 1), (1, 0)]
    rank = tensor_rank.astype(jnp.int32).reshape(1)
    modality = modality.reshape(1, local_rows)
    segments = segments.reshape(block_count, local_rows)

    def spread(part):
        if split:
            return [part, lax.ppermute(part, "tensor", swap)]
        return [lax.all_gather(part, "tensor", axis=1, tiled=True)]

    def scatter_columns(part):
        return lax.psum_scatter(part, "tensor", scatter_dimension=1, tiled=True)

    memory, key_raw, normed, row_factor = key_stage(
        rank, modality, norm_gain, head_gain, fetch(key_weight), spread(inputs)
    )
    shared = tensor_count > KV_HEADS
    is_even = tensor_rank % 2 == 0
    pair_swap = [(i, i ^ 1) for i in range(tensor_count)]
    if shared:
        partner = lax.ppermute(memory, "tensor", pair_swap)
        memory = jnp.where(
            is_even,
            jnp.concatenate([memory, partner], 1),
            jnp.concatenate([partner, memory], 1),
        )
    memories = [memory]
    for step in range(1, block_count):
        memories.append(lax.ppermute(memory, "seq", seq_pairs(step, block_count)))

    query, query_raw, back_attended = middle_stage(
        rank, modality, head_gain, normed, output_weight, query_weight, spread(cotangent)
    )
    attended, query_back, inner, own_grad, *grads = attention_stage(
        block_rank.astype(jnp.int32).reshape(1),
        block_order,
        segments,
        modality,
        head_gain,
        query,
        query_raw,
        back_attended,
        memories,
    )
    incoming = [
        lax.ppermute(grad, "seq", inverted(seq_pairs(step, block_count)))
        for step, grad in enumerate(grads, 1)
    ]

    projected, gradient_part = turn_stage(
        rank, modality, output_weight, attended, query_back, query_weight, split
    )
    if shared:
        total = own_grad + sum(grad.astype(f32) for grad in incoming)
        low, high = total[:, :HEAD_DIM], total[:, HEAD_DIM:]
        outgoing = jnp.where(is_even, high, low).astype(bf16)
        sums = [jnp.where(is_even, low, high), lax.ppermute(outgoing, "tensor", pair_swap)]
    else:
        sums = [own_grad, *incoming]
    sent, slice_back, inner, passed = key_back_stage(
        rank,
        modality,
        head_gain,
        key_raw,
        inner,
        gradient_part,
        key_weight,
        projected[0],
        sums,
        split,
    )
    if split:
        inners = [inner, lax.ppermute(inner, "tensor", swap)]
        other = lax.ppermute(sent, "tensor", swap)
        kept = kept_stage(rank, modality, gradient_part, key_weight, slice_back)
        backs = [kept, other]
        projected = [projected[1], lax.ppermute(passed, "tensor", swap)]
        gain = norm_gain
    else:
        inners = [lax.psum(inner, "tensor")]
        backs = [scatter_columns(sent)]
        attention_out = scatter_columns(passed)
        projected = []
        gain = lax.dynamic_slice_in_dim(norm_gain, tensor_rank * local_width, local_width, 1)
    results = finish(
        rank, full_width, modality, gain, row_factor, inputs, backs, inners, projected
    )
    if split:
        attention_out = results[0]
    return (attention_out, results[-1])


def solution(mesh):
    return jax.shard_map(
        local,
        mesh=mesh,
        in_specs=(
            P(("dp", "seq"), "tensor"),
            P(("dp", "seq"), "tensor"),
            P(),
            P(),
            P(None, None, "tensor"),
            P(None, None, "tensor"),
            P(None, "tensor", None),
            P(("dp", "seq")),
            P("dp"),
            P("dp"),
        ),
        out_specs=(P(("dp", "seq"), "tensor"), P(("dp", "seq"), "tensor")),
        check_vma=False,
    )
```

```python
import functools
import math

import jax
import jax.numpy as jnp
from jax import lax
from jax.experimental import pallas as pl
from jax.experimental.pallas import tpu as pltpu
from jax.sharding import PartitionSpec as P

KV_HEADS = 4
HEAD_DIM = 128
MIB = 1024 * 1024

epsilon = 1e-06
bf16 = jnp.bfloat16
f32 = jnp.float32
SMEM = pl.BlockSpec(memory_space=pltpu.SMEM)
VMEM = pl.BlockSpec(memory_space=pltpu.VMEM)
ANY = pl.BlockSpec(memory_space=pl.ANY)


def seq_pairs(step, count):
    if count & (count - 1) == 0:
        return [(i, i ^ step) for i in range(count)]
    return [(i, (i + step) % count) for i in range(count)]


def seq_steps(count):
    return sorted(range(1, count), key=lambda step: (step != count // 2, step))


def seq_source(rank, step, count):
    if count & (count - 1) == 0:
        return rank ^ step
    return (rank - step) % count


def inverted(pairs):
    return [(b, a) for a, b in pairs]


def tile_of(extent, most):
    best = HEAD_DIM
    for size in range(HEAD_DIM, min(extent, most) + 1, HEAD_DIM):
        if extent % size == 0:
            best = size
    return best


def dot_nt(a, b):
    return lax.dot_general(a, b, (((1,), (1,)), ((), ())), preferred_element_type=f32)


def dot_tn(a, b):
    return lax.dot_general(a, b, (((0,), (0,)), ((), ())), preferred_element_type=f32)


def column(row):
    count = row.shape[1]
    return jnp.broadcast_to(row.astype(f32), (count, count)).T[:, :1]


def row_of(col):
    count = col.shape[0]
    return jnp.broadcast_to(col, (count, count)).T[:1, :]


def inverse_norm(values):
    return lax.rsqrt(jnp.mean(values * values, axis=-1, keepdims=True) + epsilon)


def norm_back(values, factor, scaling, upstream):
    unit_rows = values * factor
    inner_mean = jnp.mean(scaling * upstream * unit_rows, axis=-1, keepdims=True)
    return factor * (scaling * upstream - unit_rows * inner_mean)


def streamed(weights):
    return pltpu.with_memory_space_constraint(weights, pltpu.HBM)


def params(mib):
    return pltpu.CompilerParams(vmem_limit_bytes=mib * MIB)


def cost(micros):
    return pl.CostEstimate(
        flops=int(micros * 1e9), bytes_accessed=int(micros * 2e6), transcendentals=0
    )


def in_order(rank, part_refs):
    if len(part_refs) == 1:
        return part_refs[0][...]
    own, other = part_refs[0][...], part_refs[1][...]
    first = rank == 0
    return jnp.concatenate([jnp.where(first, own, other), jnp.where(first, other, own)], axis=1)


def both_experts(image, rows, weights):
    zero = jnp.zeros_like(rows)
    masked = jnp.concatenate([jnp.where(image, zero, rows), jnp.where(image, rows, zero)], axis=1)
    flat = weights.reshape(2 * weights.shape[1], weights.shape[2])
    return jnp.dot(masked, flat, preferred_element_type=f32)


def both_back(image, rows, weights):
    return jnp.where(image, dot_nt(rows, weights[1]), dot_nt(rows, weights[0]))


def chunks_of(extent, most):
    size = tile_of(extent, most)
    return [(start, size) for start in range(0, extent, size)]


AHEAD = 4


def copies_of(source_ref, target_ref, sem_ref, pieces, base=0, slots=0):
    copies = []
    for index, (start, size) in enumerate(pieces):
        pair = []
        for e in range(2):
            if slots:
                target = target_ref.at[index % slots, e]
            else:
                target = target_ref.at[e, pl.ds(start, size), :]
            source = source_ref.at[e, pl.ds(base + start, size), :]
            pair.append(pltpu.make_async_copy(source, target, sem_ref.at[index, e]))
        copies.append(pair)
    return copies


def begin(copies, index):
    if index < len(copies):
        for copy in copies[index]:
            copy.start()


def begin_first(copies):
    for index in range(AHEAD):
        begin(copies, index)


def arrive(copies, index):
    for copy in copies[index]:
        copy.wait()


def ring(weights, pieces):
    return pltpu.VMEM((AHEAD, 2, pieces[0][1], weights.shape[2]), weights.dtype)


def resident(weights):
    return pltpu.VMEM(weights.shape, weights.dtype)


def fetch_kernel(pieces, weight_ref, held_ref, sem_ref):
    copies = copies_of(weight_ref, held_ref, sem_ref, pieces)
    for pair in copies:
        for copy in pair:
            copy.start()
    for pair in copies:
        for copy in pair:
            copy.wait()


def fetch(weights):
    pieces = chunks_of(weights.shape[1], 896)
    return pl.pallas_call(
        functools.partial(fetch_kernel, pieces),
        out_shape=resident(weights),
        in_specs=[ANY],
        out_specs=VMEM,
        scratch_shapes=[pltpu.SemaphoreType.DMA((len(pieces), 2))],
        compiler_params=params(1),
        cost_estimate=cost(0.2),
        name="fetch",
    )(streamed(weights))


def key_kernel(count, *refs):
    rank_ref, modality_ref, gain_ref, head_ref, weight_ref = refs[:5]
    part_refs = refs[5 : 5 + count]
    memory_ref, raw_ref, normed_ref, factor_ref = refs[5 + count :]
    image = column(modality_ref[...]) > 0.0
    rows = in_order(rank_ref[0], part_refs).astype(f32)
    factor = inverse_norm(rows)
    scaling = jnp.where(image, gain_ref[1:2, :], gain_ref[0:1, :])
    normed_ref[...] = (rows * factor * scaling).astype(bf16)
    factor_ref[...] = row_of(factor)
    for index, (start, size) in enumerate(chunks_of(normed_ref.shape[1], 1792)):
        part = slice(start, start + size)
        product = both_experts(image, normed_ref[:, part], weight_ref[:, part, :])
        if index == 0:
            raw_ref[...] = product
        else:
            raw_ref[...] += product
    blocks = raw_ref.shape[1] // HEAD_DIM
    scaling = jnp.where(image, head_ref[1, 1:2, :], head_ref[0, 1:2, :])
    for b in range(blocks):
        part = slice(b * HEAD_DIM, (b + 1) * HEAD_DIM)
        raw = raw_ref[:, part]
        normed = raw * inverse_norm(raw) * scaling
        is_key = (rank_ref[0] * blocks + b) % 2 == 0
        memory_ref[:, part] = jnp.where(is_key, normed, raw).astype(bf16)


def key_stage(rank, modality, norm_gain, head_gain, weights, parts):
    _, depth, width = weights.shape
    rows = parts[0].shape[0]
    return pl.pallas_call(
        functools.partial(key_kernel, len(parts)),
        out_shape=[
            jax.ShapeDtypeStruct((rows, width), bf16),
            jax.ShapeDtypeStruct((rows, width), f32),
            jax.ShapeDtypeStruct((rows, depth), bf16),
            jax.ShapeDtypeStruct((1, rows), f32),
        ],
        in_specs=[SMEM] + [VMEM] * (4 + len(parts)),
        out_specs=[VMEM] * 4,
        compiler_params=params(8),
        cost_estimate=cost(10),
        name="key_stage",
    )(rank, modality, norm_gain, head_gain, weights, *parts)


def middle_kernel(count, pieces, *refs):
    rank_ref, modality_ref, head_ref, normed_ref, output_ref, query_weight_ref = refs[:6]
    part_refs = refs[6 : 6 + count]
    query_ref, raw_ref, back_ref, slots, sems = refs[6 + count :]
    copies = copies_of(query_weight_ref, slots, sems, pieces, slots=AHEAD)
    begin_first(copies)
    image = column(modality_ref[...]) > 0.0
    cotangent = in_order(rank_ref[0], part_refs)
    tiles = chunks_of(output_ref.shape[1], 256)
    done = 0
    for turn, (start, size) in enumerate(tiles, 1):
        part = slice(start, start + size)
        back_ref[:, part] = both_back(image, cotangent, output_ref[:, part, :]).astype(bf16)
        until = len(pieces) * turn // len(tiles)
        for index in range(done, until):
            arrive(copies, index)
            start, size = pieces[index]
            part = slice(start, start + size)
            product = both_experts(image, normed_ref[:, part], slots[index % AHEAD])
            if index == 0:
                raw_ref[...] = product
            else:
                raw_ref[...] += product
            begin(copies, index + AHEAD)
        done = until
    scaling = jnp.where(image, head_ref[1, 0:1, :], head_ref[0, 0:1, :])
    for h in range(raw_ref.shape[1] // HEAD_DIM):
        part = slice(h * HEAD_DIM, (h + 1) * HEAD_DIM)
        raw = raw_ref[:, part]
        query_ref[:, part] = (raw * inverse_norm(raw) * scaling).astype(bf16)


def middle_stage(rank, modality, head_gain, normed, output_weight, query_weight, parts):
    rows = normed.shape[0]
    width = query_weight.shape[2]
    pieces = chunks_of(query_weight.shape[1], 512)
    return pl.pallas_call(
        functools.partial(middle_kernel, len(parts), pieces),
        out_shape=[
            jax.ShapeDtypeStruct((rows, width), bf16),
            jax.ShapeDtypeStruct((rows, width), f32),
            jax.ShapeDtypeStruct((rows, width), bf16),
        ],
        in_specs=[SMEM, VMEM, VMEM, VMEM, VMEM, ANY] + [VMEM] * len(parts),
        out_specs=[VMEM] * 3,
        scratch_shapes=[
            ring(query_weight, pieces),
            pltpu.SemaphoreType.DMA((len(pieces), 2)),
        ],
        compiler_params=params(14),
        cost_estimate=cost(8),
        name="middle_stage",
    )(rank, modality, head_gain, normed, output_weight, streamed(query_weight), *parts)


def attention_kernel(blocks, pairs, per_group, *refs):
    for pair in range(pairs):
        wide = pl.ds(pair * per_group * HEAD_DIM, per_group * HEAD_DIM)
        narrow = pl.ds(pair * 2 * HEAD_DIM, 2 * HEAD_DIM)
        views = list(refs[:5]) + [ref.at[:, wide] for ref in refs[5:8]]
        views += [ref.at[:, narrow] for ref in refs[8 : 8 + blocks]]
        views += [ref.at[:, wide] for ref in refs[8 + blocks : 10 + blocks]]
        views += [refs[10 + blocks]]
        views += [ref.at[:, narrow] for ref in refs[11 + blocks :]]
        attention_pair(blocks, per_group, pair == 0, *views)


def attention_pair(blocks, per_group, fresh, *refs):
    place_ref, order_ref, segments_ref, modality_ref, head_ref = refs[:5]
    query_ref, raw_ref, back_ref = refs[5:8]
    memory_refs = refs[8 : 8 + blocks]
    attended_ref, query_back_ref, inner_ref = refs[8 + blocks : 11 + blocks]
    grad_refs = refs[11 + blocks :]
    rows = query_ref.shape[0]
    scale = 1.0 / math.sqrt(HEAD_DIM)

    def heads(ref):
        return jnp.concatenate(
            [ref[:, h * HEAD_DIM : (h + 1) * HEAD_DIM] for h in range(per_group)], axis=0
        )

    query, back = heads(query_ref), heads(back_ref)
    key = jnp.concatenate([m[:, :HEAD_DIM] for m in memory_refs], axis=0)
    value = jnp.concatenate([m[:, HEAD_DIM:] for m in memory_refs], axis=0)
    lines = [
        segments_ref[pl.ds(order_ref[seq_source(place_ref[0], step, blocks)], 1), :]
        for step in [0, *seq_steps(blocks)]
    ]
    key_segments = jnp.concatenate(lines, axis=1)
    query_segments = column(lines[0])
    visible = jnp.where(key_segments.astype(f32) <= query_segments, 1.0, 0.0)
    visible = jnp.concatenate([visible] * per_group, axis=0)
    scores = dot_nt(query, key) * scale
    weights = jnp.where(visible > 0.0, jnp.exp(scores), 0.0).astype(bf16)
    weights32 = weights.astype(f32)
    denominator = jnp.sum(weights32, axis=1, keepdims=True)
    numerator = jnp.dot(weights, value, preferred_element_type=f32)
    attended = (numerator / denominator).astype(bf16)
    offset = jnp.sum(back.astype(f32) * attended.astype(f32), axis=1, keepdims=True)
    probability = (weights32 / denominator).astype(bf16)
    back_prob = dot_nt(back, value)
    back_score = (probability.astype(f32) * (back_prob - offset)).astype(bf16)
    back_query = jnp.dot(back_score, key, preferred_element_type=f32) * scale
    back_key = dot_tn(back_score, query) * scale
    back_value = dot_tn(probability, back)
    for b in range(blocks):
        part = slice(b * rows, (b + 1) * rows)
        grad_refs[b][:, :HEAD_DIM] = back_key[part].astype(grad_refs[b].dtype)
        grad_refs[b][:, HEAD_DIM:] = back_value[part].astype(grad_refs[b].dtype)
    image = column(modality_ref[...]) > 0.0
    scaling = jnp.where(image, head_ref[1, 0:1, :], head_ref[0, 0:1, :])
    inner = jnp.zeros((rows, 1), f32)
    for h in range(per_group):
        part = slice(h * rows, (h + 1) * rows)
        columns = slice(h * HEAD_DIM, (h + 1) * HEAD_DIM)
        attended_ref[:, columns] = attended[part]
        raw = raw_ref[:, columns]
        query_back = norm_back(raw, inverse_norm(raw), scaling, back_query[part]).astype(bf16)
        query_back_ref[:, columns] = query_back
        inner += jnp.sum(query_back.astype(f32) * raw, axis=1, keepdims=True)
    inner = row_of(inner)

    if fresh:
        inner_ref[...] = inner
    else:
        inner_ref[...] += inner


def attention_stage(place, order, segments, modality, head_gain, query, raw, back, memories):
    rows, width = query.shape
    blocks = len(memories)
    pairs = memories[0].shape[1] // (2 * HEAD_DIM)
    per_group = width // HEAD_DIM // pairs
    outs = [
        jax.ShapeDtypeStruct((rows, width), bf16),
        jax.ShapeDtypeStruct((rows, width), bf16),
        jax.ShapeDtypeStruct((1, rows), f32),
    ] + [
        jax.ShapeDtypeStruct((rows, pairs * 2 * HEAD_DIM), f32 if b == 0 else bf16)
        for b in range(blocks)
    ]
    return pl.pallas_call(
        functools.partial(attention_kernel, blocks, pairs, per_group),
        out_shape=outs,
        in_specs=[SMEM, SMEM] + [VMEM] * (6 + blocks),
        out_specs=[VMEM] * (3 + blocks),
        compiler_params=params(12),
        cost_estimate=cost(4),
        name="attention_stage",
    )(place, order, segments, modality, head_gain, query, raw, back, *memories)


def turn_kernel(pieces, outputs, *refs):
    rank_ref, modality_ref, output_ref, attended_ref, back_ref, query_ref = refs[:6]
    out_refs = refs[6 : 6 + outputs]
    part_ref, slots, sems = refs[6 + outputs :]
    copies = copies_of(query_ref, slots, sems, pieces, slots=AHEAD)
    begin_first(copies)
    image = column(modality_ref[...]) > 0.0
    attended = attended_ref[...]
    extent = output_ref.shape[2] // 2

    def project(rank):
        sent_ref, kept_ref = out_refs
        for start, size in chunks_of(extent, 896):
            part = slice(start, start + size)
            first = (1 - rank) * extent + start
            product = both_experts(image, attended, output_ref[:, :, first : first + size])
            sent_ref[:, part] = product.astype(bf16)
            first = rank * extent + start
            product = both_experts(image, attended, output_ref[:, :, first : first + size])
            kept_ref[:, part] = product

    if outputs == 1:
        out_refs[0][...] = both_experts(image, attended, output_ref[...]).astype(bf16)
    else:
        for rank in range(2):
            pl.when(rank_ref[0] == rank)(functools.partial(project, rank))
    for index, (start, size) in enumerate(pieces):
        arrive(copies, index)
        part = slice(start, start + size)
        part_ref[:, part] = both_back(image, back_ref[...], slots[index % AHEAD])
        begin(copies, index + AHEAD)


def turn_stage(rank, modality, output_weight, attended, query_back, query_weight, split):
    depth = query_weight.shape[1]
    width = output_weight.shape[2]
    rows = attended.shape[0]
    pieces = chunks_of(depth, 512)
    if split:
        outs = [
            jax.ShapeDtypeStruct((rows, width // 2), bf16),
            jax.ShapeDtypeStruct((rows, width // 2), f32),
        ]
    else:
        outs = [jax.ShapeDtypeStruct((rows, width), bf16)]
    *projected, part = pl.pallas_call(
        functools.partial(turn_kernel, pieces, len(outs)),
        out_shape=outs + [jax.ShapeDtypeStruct((rows, depth), f32)],
        in_specs=[SMEM, VMEM, VMEM, VMEM, VMEM, ANY],
        out_specs=[VMEM] * (len(outs) + 1),
        scratch_shapes=[
            ring(query_weight, pieces),
            pltpu.SemaphoreType.DMA((len(pieces), 2)),
        ],
        compiler_params=params(16),
        cost_estimate=cost(10),
        name="turn_stage",
    )(rank, modality, output_weight, attended, query_back, streamed(query_weight))
    return projected, part


def key_back_kernel(split, *refs):
    rank_ref, modality_ref, head_ref, raw_ref, inner_in_ref, part_ref, weight_ref = refs[:7]
    grad_refs = refs[8:-4]
    out_ref, back_ref, inner_ref = refs[-4:-1]
    base = pl.multiple_of((1 - rank_ref[0]) * out_ref.shape[1], HEAD_DIM) if split else 0
    image = column(modality_ref[...]) > 0.0
    blocks = raw_ref.shape[1] // HEAD_DIM
    scaling = jnp.where(image, head_ref[1, 1:2, :], head_ref[0, 1:2, :])
    inner = jnp.zeros((raw_ref.shape[0], 1), f32)
    for b in range(blocks):
        part = slice(b * HEAD_DIM, (b + 1) * HEAD_DIM)
        raw = raw_ref[:, part]
        upstream = grad_refs[0][:, part].astype(f32)
        for grad_ref in grad_refs[1:]:
            upstream += grad_ref[:, part].astype(f32)
        is_key = (rank_ref[0] * blocks + b) % 2 == 0
        normed_back = norm_back(raw, inverse_norm(raw), scaling, upstream)
        back = jnp.where(is_key, normed_back, upstream).astype(bf16)
        back_ref[:, part] = back
        inner += jnp.sum(back.astype(f32) * raw, axis=1, keepdims=True)
    inner_ref[...] = inner_in_ref[...] + row_of(inner)
    for start, size in chunks_of(out_ref.shape[1], 896):
        place = pl.ds(base + start, size)
        product = both_back(image, back_ref[...], weight_ref[:, place, :])
        out_ref[:, start : start + size] = (product + part_ref[:, place]).astype(bf16)


def key_back_stage(rank, modality, head_gain, raw, inner, part, weights, passed, grads, split):
    _, depth, width = weights.shape
    rows = raw.shape[0]
    return pl.pallas_call(
        functools.partial(key_back_kernel, split),
        out_shape=[
            jax.ShapeDtypeStruct((rows, depth // 2 if split else depth), bf16),
            jax.ShapeDtypeStruct((rows, width), bf16),
            jax.ShapeDtypeStruct((1, rows), f32),
            jax.ShapeDtypeStruct(passed.shape, passed.dtype),
        ],
        in_specs=[SMEM] + [VMEM] * 6 + [ANY] + [VMEM] * len(grads),
        out_specs=[VMEM] * 3 + [ANY],
        input_output_aliases={7: 3},
        compiler_params=params(6),
        cost_estimate=cost(2),
        name="key_back_stage",
    )(rank, modality, head_gain, raw, inner, part, weights, passed, *grads)


def kept_kernel(rank_ref, modality_ref, part_ref, weight_ref, back_ref, out_ref):
    base = pl.multiple_of(rank_ref[0] * out_ref.shape[1], HEAD_DIM)
    image = column(modality_ref[...]) > 0.0
    for start, size in chunks_of(out_ref.shape[1], 896):
        place = pl.ds(base + start, size)
        product = both_back(image, back_ref[...], weight_ref[:, place, :])
        out_ref[:, start : start + size] = product + part_ref[:, place]


def kept_stage(rank, modality, part, weights, back):
    return pl.pallas_call(
        kept_kernel,
        out_shape=jax.ShapeDtypeStruct((back.shape[0], weights.shape[1] // 2), f32),
        in_specs=[SMEM] + [VMEM] * 4,
        out_specs=VMEM,
        compiler_params=params(6),
        cost_estimate=cost(2),
        name="kept_stage",
    )(rank, modality, part, weights, back)


def finish_kernel(backs, inners, total_width, *refs):
    rank_ref, modality_ref, gain_ref, factor_ref, inputs_ref = refs[:5]
    back_refs = refs[5 : 5 + backs]
    inner_refs = refs[5 + backs : 5 + backs + inners]
    rest = refs[5 + backs + inners :]
    out_ref = rest[-1]
    width = inputs_ref.shape[1]
    image = column(modality_ref[...]) > 0.0
    gain = gain_ref[...]
    if gain.shape[1] != width:
        gain = gain_ref[:, pl.ds(pl.multiple_of(rank_ref[0] * width, HEAD_DIM), width)]
    scaling = jnp.where(image, gain[1:2, :], gain[0:1, :])
    factor = column(factor_ref[...])
    back = back_refs[0][...].astype(f32)
    for ref in back_refs[1:]:
        back += ref[...].astype(f32)
    inner = inner_refs[0][...]
    for ref in inner_refs[1:]:
        inner += ref[...]
    unit_rows = inputs_ref[...].astype(f32) * factor
    inner_mean = column(inner) * (1.0 / total_width)
    out_ref[...] = (factor * (scaling * back - unit_rows * inner_mean)).astype(bf16)
    if len(rest) == 4:
        kept_ref, other_ref, attention_ref, _ = rest
        attention_ref[...] = (kept_ref[...] + other_ref[...].astype(f32)).astype(bf16)


def finish(rank, total_width, modality, gain, factor, inputs, backs, inners, projected):
    shape = jax.ShapeDtypeStruct(inputs.shape, bf16)
    arrays = [modality, gain, factor, inputs, *backs, *inners, *projected]
    outs = [shape] * (2 if projected else 1)
    return pl.pallas_call(
        functools.partial(finish_kernel, len(backs), len(inners), total_width),
        out_shape=outs,
        in_specs=[SMEM] + [VMEM] * len(arrays),
        out_specs=[VMEM] * len(outs),
        compiler_params=params(6),
        cost_estimate=cost(1),
        name="finish",
    )(rank, *arrays)


def local(
    inputs,
    cotangent,
    norm_gain,
    head_gain,
    query_weight,
    key_weight,
    output_weight,
    modality,
    segments,
    block_order,
):
    tensor_rank = lax.axis_index("tensor")
    block_rank = lax.axis_index("seq")
    tensor_count = lax.axis_size("tensor")
    block_count = lax.axis_size("seq")
    local_rows, local_width = inputs.shape
    full_width = local_width * tensor_count
    split = tensor_count == 2
    swap = [(0, 1), (1, 0)]
    rank = tensor_rank.astype(jnp.int32).reshape(1)
    modality = modality.reshape(1, local_rows)
    segments = segments.reshape(block_count, local_rows)

    def spread(part):
        if split:
            return [part, lax.ppermute(part, "tensor", swap)]
        return [lax.all_gather(part, "tensor", axis=1, tiled=True)]

    def scatter_columns(part):
        return lax.psum_scatter(part, "tensor", scatter_dimension=1, tiled=True)

    memory, key_raw, normed, row_factor = key_stage(
        rank, modality, norm_gain, head_gain, fetch(key_weight), spread(inputs)
    )
    shared = tensor_count > KV_HEADS
    is_even = tensor_rank % 2 == 0
    pair_swap = [(i, i ^ 1) for i in range(tensor_count)]
    if shared:
        partner = lax.ppermute(memory, "tensor", pair_swap)
        memory = jnp.where(
            is_even,
            jnp.concatenate([memory, partner], 1),
            jnp.concatenate([partner, memory], 1),
        )
    memories = [memory]
    for step in seq_steps(block_count):
        memories.append(lax.ppermute(memory, "seq", seq_pairs(step, block_count)))

    query, query_raw, back_attended = middle_stage(
        rank, modality, head_gain, normed, output_weight, query_weight, spread(cotangent)
    )
    attended, query_back, inner, own_grad, *grads = attention_stage(
        block_rank.astype(jnp.int32).reshape(1),
        block_order,
        segments,
        modality,
        head_gain,
        query,
        query_raw,
        back_attended,
        memories,
    )
    incoming = [
        lax.ppermute(grad, "seq", inverted(seq_pairs(step, block_count)))
        for step, grad in zip(seq_steps(block_count), grads)
    ]

    projected, gradient_part = turn_stage(
        rank, modality, output_weight, attended, query_back, query_weight, split
    )
    if shared:
        total = own_grad + sum(grad.astype(f32) for grad in incoming)
        low, high = total[:, :HEAD_DIM], total[:, HEAD_DIM:]
        outgoing = jnp.where(is_even, high, low).astype(bf16)
        sums = [jnp.where(is_even, low, high), lax.ppermute(outgoing, "tensor", pair_swap)]
    else:
        sums = [own_grad, *incoming]
    sent, slice_back, inner, passed = key_back_stage(
        rank,
        modality,
        head_gain,
        key_raw,
        inner,
        gradient_part,
        key_weight,
        projected[0],
        sums,
        split,
    )
    if split:
        inners = [inner, lax.ppermute(inner, "tensor", swap)]
        other = lax.ppermute(sent, "tensor", swap)
        kept = kept_stage(rank, modality, gradient_part, key_weight, slice_back)
        backs = [kept, other]
        projected = [projected[1], lax.ppermute(passed, "tensor", swap)]
        gain = norm_gain
    else:
        inners = [lax.psum(inner, "tensor")]
        backs = [scatter_columns(sent)]
        attention_out = scatter_columns(passed)
        projected = []
        gain = lax.dynamic_slice_in_dim(norm_gain, tensor_rank * local_width, local_width, 1)
    results = finish(
        rank, full_width, modality, gain, row_factor, inputs, backs, inners, projected
    )
    if split:
        attention_out = results[0]
    return (attention_out, results[-1])


def solution(mesh):
    return jax.shard_map(
        local,
        mesh=mesh,
        in_specs=(
            P(("dp", "seq"), "tensor"),
            P(("dp", "seq"), "tensor"),
            P(),
            P(),
            P(None, None, "tensor"),
            P(None, None, "tensor"),
            P(None, "tensor", None),
            P(("dp", "seq")),
            P("dp"),
            P("dp"),
        ),
        out_specs=(P(("dp", "seq"), "tensor"), P(("dp", "seq"), "tensor")),
        check_vma=False,
    )
```

```python
import functools
import math

import jax
import jax.numpy as jnp
from jax import lax
from jax.experimental import pallas as pl
from jax.experimental.pallas import tpu as pltpu
from jax.sharding import PartitionSpec as P

KV_HEADS = 4
HEAD_DIM = 128
MIB = 1024 * 1024

epsilon = 1e-06
bf16 = jnp.bfloat16
f32 = jnp.float32
SMEM = pl.BlockSpec(memory_space=pltpu.SMEM)
VMEM = pl.BlockSpec(memory_space=pltpu.VMEM)
ANY = pl.BlockSpec(memory_space=pl.ANY)


def seq_pairs(step, count):
    if count & (count - 1) == 0:
        return [(i, i ^ step) for i in range(count)]
    return [(i, (i + step) % count) for i in range(count)]


def seq_steps(count):
    return sorted(range(1, count), key=lambda step: (step == count // 2, -step))


def seq_source(rank, step, count):
    if count & (count - 1) == 0:
        return rank ^ step
    return (rank - step) % count


def inverted(pairs):
    return [(b, a) for a, b in pairs]


def tile_of(extent, most):
    best = HEAD_DIM
    for size in range(HEAD_DIM, min(extent, most) + 1, HEAD_DIM):
        if extent % size == 0:
            best = size
    return best


def dot_nt(a, b):
    return lax.dot_general(a, b, (((1,), (1,)), ((), ())), preferred_element_type=f32)


def dot_tn(a, b):
    return lax.dot_general(a, b, (((0,), (0,)), ((), ())), preferred_element_type=f32)


def column(row):
    count = row.shape[1]
    return jnp.broadcast_to(row.astype(f32), (count, count)).T[:, :1]


def row_of(col):
    count = col.shape[0]
    return jnp.broadcast_to(col, (count, count)).T[:1, :]


def inverse_norm(values):
    return lax.rsqrt(jnp.mean(values * values, axis=-1, keepdims=True) + epsilon)


def norm_back(values, factor, scaling, upstream):
    unit_rows = values * factor
    inner_mean = jnp.mean(scaling * upstream * unit_rows, axis=-1, keepdims=True)
    return factor * (scaling * upstream - unit_rows * inner_mean)


def streamed(weights):
    return pltpu.with_memory_space_constraint(weights, pltpu.HBM)


def params(mib):
    return pltpu.CompilerParams(vmem_limit_bytes=mib * MIB)


def cost(micros):
    return pl.CostEstimate(
        flops=int(micros * 1e9), bytes_accessed=int(micros * 2e6), transcendentals=0
    )


def in_order(rank, part_refs):
    if len(part_refs) == 1:
        return part_refs[0][...]
    own, other = part_refs[0][...], part_refs[1][...]
    first = rank == 0
    return jnp.concatenate([jnp.where(first, own, other), jnp.where(first, other, own)], axis=1)


def both_experts(image, rows, weights):
    zero = jnp.zeros_like(rows)
    masked = jnp.concatenate([jnp.where(image, zero, rows), jnp.where(image, rows, zero)], axis=1)
    flat = weights.reshape(2 * weights.shape[1], weights.shape[2])
    return jnp.dot(masked, flat, preferred_element_type=f32)


def both_back(image, rows, weights):
    return jnp.where(image, dot_nt(rows, weights[1]), dot_nt(rows, weights[0]))


def chunks_of(extent, most):
    size = tile_of(extent, most)
    return [(start, size) for start in range(0, extent, size)]


AHEAD = 4


def copies_of(source_ref, target_ref, sem_ref, pieces, base=0, slots=0):
    copies = []
    for index, (start, size) in enumerate(pieces):
        pair = []
        for e in range(2):
            if slots:
                target = target_ref.at[index % slots, e]
            else:
                target = target_ref.at[e, pl.ds(start, size), :]
            source = source_ref.at[e, pl.ds(base + start, size), :]
            pair.append(pltpu.make_async_copy(source, target, sem_ref.at[index, e]))
        copies.append(pair)
    return copies


def begin(copies, index):
    if index < len(copies):
        for copy in copies[index]:
            copy.start()


def begin_first(copies):
    for index in range(AHEAD):
        begin(copies, index)


def arrive(copies, index):
    for copy in copies[index]:
        copy.wait()


def ring(weights, pieces):
    return pltpu.VMEM((AHEAD, 2, pieces[0][1], weights.shape[2]), weights.dtype)


def key_kernel(count, *refs):
    rank_ref, modality_ref, gain_ref, head_ref, weight_ref = refs[:5]
    part_refs = refs[5 : 5 + count]
    memory_ref, raw_ref, normed_ref, factor_ref = refs[5 + count :]
    image = column(modality_ref[...]) > 0.0
    rows = in_order(rank_ref[0], part_refs).astype(f32)
    factor = inverse_norm(rows)
    scaling = jnp.where(image, gain_ref[1:2, :], gain_ref[0:1, :])
    normed_ref[...] = (rows * factor * scaling).astype(bf16)
    factor_ref[...] = row_of(factor)
    for index, (start, size) in enumerate(chunks_of(normed_ref.shape[1], 1792)):
        part = slice(start, start + size)
        product = both_experts(image, normed_ref[:, part], weight_ref[:, part, :])
        if index == 0:
            raw_ref[...] = product
        else:
            raw_ref[...] += product
    blocks = raw_ref.shape[1] // HEAD_DIM
    scaling = jnp.where(image, head_ref[1, 1:2, :], head_ref[0, 1:2, :])
    for b in range(blocks):
        part = slice(b * HEAD_DIM, (b + 1) * HEAD_DIM)
        raw = raw_ref[:, part]
        normed = raw * inverse_norm(raw) * scaling
        is_key = (rank_ref[0] * blocks + b) % 2 == 0
        memory_ref[:, part] = jnp.where(is_key, normed, raw).astype(bf16)


def key_stage(rank, modality, norm_gain, head_gain, weights, parts):
    _, depth, width = weights.shape
    rows = parts[0].shape[0]
    return pl.pallas_call(
        functools.partial(key_kernel, len(parts)),
        out_shape=[
            jax.ShapeDtypeStruct((rows, width), bf16),
            jax.ShapeDtypeStruct((rows, width), f32),
            jax.ShapeDtypeStruct((rows, depth), bf16),
            jax.ShapeDtypeStruct((1, rows), f32),
        ],
        in_specs=[SMEM] + [VMEM] * (4 + len(parts)),
        out_specs=[VMEM] * 4,
        compiler_params=params(8),
        cost_estimate=cost(10),
        name="key_stage",
    )(rank, modality, norm_gain, head_gain, weights, *parts)


def middle_kernel(count, pieces, *refs):
    rank_ref, modality_ref, head_ref, normed_ref, output_ref, query_weight_ref = refs[:6]
    part_refs = refs[6 : 6 + count]
    query_ref, raw_ref, back_ref, slots, sems = refs[6 + count :]
    copies = copies_of(query_weight_ref, slots, sems, pieces, slots=AHEAD)
    begin_first(copies)
    image = column(modality_ref[...]) > 0.0
    cotangent = in_order(rank_ref[0], part_refs)
    tiles = chunks_of(output_ref.shape[1], HEAD_DIM)
    done = 0
    for turn, (start, size) in enumerate(tiles, 1):
        part = slice(start, start + size)
        back_ref[:, part] = both_back(image, cotangent, output_ref[:, part, :]).astype(bf16)
        until = len(pieces) * turn // len(tiles)
        for index in range(done, until):
            arrive(copies, index)
            start, size = pieces[index]
            part = slice(start, start + size)
            product = both_experts(image, normed_ref[:, part], slots[index % AHEAD])
            if index == 0:
                raw_ref[...] = product
            else:
                raw_ref[...] += product
            begin(copies, index + AHEAD)
        done = until
    scaling = jnp.where(image, head_ref[1, 0:1, :], head_ref[0, 0:1, :])
    for h in range(raw_ref.shape[1] // HEAD_DIM):
        part = slice(h * HEAD_DIM, (h + 1) * HEAD_DIM)
        raw = raw_ref[:, part]
        query_ref[:, part] = (raw * inverse_norm(raw) * scaling).astype(bf16)


def middle_stage(rank, modality, head_gain, normed, output_weight, query_weight, parts):
    rows = normed.shape[0]
    width = query_weight.shape[2]
    pieces = chunks_of(query_weight.shape[1], 512)
    return pl.pallas_call(
        functools.partial(middle_kernel, len(parts), pieces),
        out_shape=[
            jax.ShapeDtypeStruct((rows, width), bf16),
            jax.ShapeDtypeStruct((rows, width), f32),
            jax.ShapeDtypeStruct((rows, width), bf16),
        ],
        in_specs=[SMEM, VMEM, VMEM, VMEM, VMEM, ANY] + [VMEM] * len(parts),
        out_specs=[VMEM] * 3,
        scratch_shapes=[
            ring(query_weight, pieces),
            pltpu.SemaphoreType.DMA((len(pieces), 2)),
        ],
        compiler_params=params(14),
        cost_estimate=cost(8),
        name="middle_stage",
    )(rank, modality, head_gain, normed, output_weight, streamed(query_weight), *parts)


def attention_kernel(blocks, pairs, per_group, *refs):
    place_ref, order_ref, segments_ref, modality_ref, head_ref = refs[:5]
    query_ref, raw_ref, back_ref = refs[5:8]
    memory_refs = refs[8 : 8 + blocks]
    attended_ref, query_back_ref, inner_ref = refs[8 + blocks : 11 + blocks]
    grad_refs = refs[11 + blocks :]
    rows = query_ref.shape[0]
    scale = 1.0 / math.sqrt(HEAD_DIM)
    lines = [
        segments_ref[pl.ds(order_ref[seq_source(place_ref[0], step, blocks)], 1), :]
        for step in [0, *seq_steps(blocks)]
    ]
    key_segments = jnp.concatenate(lines, axis=1).astype(f32)
    visible = key_segments <= column(lines[0])
    image = column(modality_ref[...]) > 0.0
    scaling = jnp.where(image, head_ref[1, 0:1, :], head_ref[0, 0:1, :])
    inner = jnp.zeros((rows, 1), f32)
    for pair in range(pairs):
        columns = [
            slice(h * HEAD_DIM, (h + 1) * HEAD_DIM)
            for h in range(pair * per_group, (pair + 1) * per_group)
        ]
        parts = [slice(h * rows, (h + 1) * rows) for h in range(per_group)]
        keys = slice(2 * pair * HEAD_DIM, (2 * pair + 1) * HEAD_DIM)
        values = slice((2 * pair + 1) * HEAD_DIM, (2 * pair + 2) * HEAD_DIM)
        query = jnp.concatenate([query_ref[:, c] for c in columns], axis=0)
        back = jnp.concatenate([back_ref[:, c] for c in columns], axis=0)
        key = jnp.concatenate([m[:, keys] for m in memory_refs], axis=0)
        value = jnp.concatenate([m[:, values] for m in memory_refs], axis=0)
        scores = dot_nt(query, key) * (scale * math.log2(math.e))
        weights = jnp.concatenate(
            [jnp.where(visible, jnp.exp2(scores[p]), 0.0).astype(bf16) for p in parts], axis=0
        )
        weights32 = weights.astype(f32)
        inverse = 1.0 / jnp.sum(weights32, axis=1, keepdims=True)
        numerator = jnp.dot(weights, value, preferred_element_type=f32)
        attended = (numerator * inverse).astype(bf16)
        offset = jnp.sum(back.astype(f32) * attended.astype(f32), axis=1, keepdims=True)
        probability = (weights32 * inverse).astype(bf16)
        back_prob = dot_nt(back, value)
        back_score = (probability.astype(f32) * (back_prob - offset)).astype(bf16)
        back_query = jnp.dot(back_score, key, preferred_element_type=f32) * scale
        back_key = dot_tn(back_score, query) * scale
        back_value = dot_tn(probability, back)
        for b, grad_ref in enumerate(grad_refs):
            part = slice(b * rows, (b + 1) * rows)
            grad_ref[:, keys] = back_key[part].astype(grad_ref.dtype)
            grad_ref[:, values] = back_value[part].astype(grad_ref.dtype)
        for part, place in zip(parts, columns):
            attended_ref[:, place] = attended[part]
            raw = raw_ref[:, place]
            query_back = norm_back(raw, inverse_norm(raw), scaling, back_query[part]).astype(bf16)
            query_back_ref[:, place] = query_back
            inner += jnp.sum(query_back.astype(f32) * raw, axis=1, keepdims=True)
    inner_ref[...] = row_of(inner)


def attention_stage(place, order, segments, modality, head_gain, query, raw, back, memories):
    rows, width = query.shape
    blocks = len(memories)
    pairs = memories[0].shape[1] // (2 * HEAD_DIM)
    per_group = width // HEAD_DIM // pairs
    outs = [
        jax.ShapeDtypeStruct((rows, width), bf16),
        jax.ShapeDtypeStruct((rows, width), bf16),
        jax.ShapeDtypeStruct((1, rows), f32),
    ] + [
        jax.ShapeDtypeStruct((rows, pairs * 2 * HEAD_DIM), f32 if b == 0 else bf16)
        for b in range(blocks)
    ]
    return pl.pallas_call(
        functools.partial(attention_kernel, blocks, pairs, per_group),
        out_shape=outs,
        in_specs=[SMEM, SMEM] + [VMEM] * (6 + blocks),
        out_specs=[VMEM] * (3 + blocks),
        compiler_params=params(12),
        cost_estimate=cost(4),
        name="attention_stage",
    )(place, order, segments, modality, head_gain, query, raw, back, *memories)


def turn_kernel(pieces, outputs, *refs):
    rank_ref, modality_ref, output_ref, attended_ref, back_ref, query_ref = refs[:6]
    out_refs = refs[6 : 6 + outputs]
    part_ref, slots, sems = refs[6 + outputs :]
    copies = copies_of(query_ref, slots, sems, pieces, slots=AHEAD)
    begin_first(copies)
    image = column(modality_ref[...]) > 0.0
    attended = attended_ref[...]
    extent = output_ref.shape[2] // 2

    def project(rank):
        sent_ref, kept_ref = out_refs
        for start, size in chunks_of(extent, 896):
            part = slice(start, start + size)
            first = (1 - rank) * extent + start
            product = both_experts(image, attended, output_ref[:, :, first : first + size])
            sent_ref[:, part] = product.astype(bf16)
            first = rank * extent + start
            product = both_experts(image, attended, output_ref[:, :, first : first + size])
            kept_ref[:, part] = product

    if outputs == 1:
        out_refs[0][...] = both_experts(image, attended, output_ref[...]).astype(bf16)
    else:
        for rank in range(2):
            pl.when(rank_ref[0] == rank)(functools.partial(project, rank))
    for index, (start, size) in enumerate(pieces):
        arrive(copies, index)
        for inside, tile in chunks_of(size, HEAD_DIM):
            weights = slots[index % AHEAD, :, inside : inside + tile, :]
            part = slice(start + inside, start + inside + tile)
            part_ref[:, part] = both_back(image, back_ref[...], weights)
        begin(copies, index + AHEAD)


def turn_stage(rank, modality, output_weight, attended, query_back, query_weight, split):
    depth = query_weight.shape[1]
    width = output_weight.shape[2]
    rows = attended.shape[0]
    pieces = chunks_of(depth, 512)
    if split:
        outs = [
            jax.ShapeDtypeStruct((rows, width // 2), bf16),
            jax.ShapeDtypeStruct((rows, width // 2), f32),
        ]
    else:
        outs = [jax.ShapeDtypeStruct((rows, width), bf16)]
    *projected, part = pl.pallas_call(
        functools.partial(turn_kernel, pieces, len(outs)),
        out_shape=outs + [jax.ShapeDtypeStruct((rows, depth), f32)],
        in_specs=[SMEM, VMEM, VMEM, VMEM, VMEM, ANY],
        out_specs=[VMEM] * (len(outs) + 1),
        scratch_shapes=[
            ring(query_weight, pieces),
            pltpu.SemaphoreType.DMA((len(pieces), 2)),
        ],
        compiler_params=params(16),
        cost_estimate=cost(10),
        name="turn_stage",
    )(rank, modality, output_weight, attended, query_back, streamed(query_weight))
    return projected, part


def key_back_kernel(split, *refs):
    rank_ref, modality_ref, head_ref, raw_ref, inner_in_ref, part_ref, weight_ref = refs[:7]
    grad_refs = refs[8:-4]
    out_ref, back_ref, inner_ref = refs[-4:-1]
    base = pl.multiple_of((1 - rank_ref[0]) * out_ref.shape[1], HEAD_DIM) if split else 0
    image = column(modality_ref[...]) > 0.0
    blocks = raw_ref.shape[1] // HEAD_DIM
    scaling = jnp.where(image, head_ref[1, 1:2, :], head_ref[0, 1:2, :])
    inner = jnp.zeros((raw_ref.shape[0], 1), f32)
    for b in range(blocks):
        part = slice(b * HEAD_DIM, (b + 1) * HEAD_DIM)
        raw = raw_ref[:, part]
        upstream = grad_refs[0][:, part].astype(f32)
        for grad_ref in grad_refs[1:]:
            upstream += grad_ref[:, part].astype(f32)
        is_key = (rank_ref[0] * blocks + b) % 2 == 0
        normed_back = norm_back(raw, inverse_norm(raw), scaling, upstream)
        back = jnp.where(is_key, normed_back, upstream).astype(bf16)
        back_ref[:, part] = back
        inner += jnp.sum(back.astype(f32) * raw, axis=1, keepdims=True)
    inner_ref[...] = inner_in_ref[...] + row_of(inner)
    for start, size in chunks_of(out_ref.shape[1], HEAD_DIM):
        place = pl.ds(base + start, size)
        product = both_back(image, back_ref[...], weight_ref[:, place, :])
        out_ref[:, start : start + size] = (product + part_ref[:, place]).astype(bf16)


def key_back_stage(rank, modality, head_gain, raw, inner, part, weights, passed, grads, split):
    _, depth, width = weights.shape
    rows = raw.shape[0]
    return pl.pallas_call(
        functools.partial(key_back_kernel, split),
        out_shape=[
            jax.ShapeDtypeStruct((rows, depth // 2 if split else depth), bf16),
            jax.ShapeDtypeStruct((rows, width), bf16),
            jax.ShapeDtypeStruct((1, rows), f32),
            jax.ShapeDtypeStruct(passed.shape, passed.dtype),
        ],
        in_specs=[SMEM] + [VMEM] * 6 + [ANY] + [VMEM] * len(grads),
        out_specs=[VMEM] * 3 + [ANY],
        input_output_aliases={7: 3},
        compiler_params=params(6),
        cost_estimate=cost(2),
        name="key_back_stage",
    )(rank, modality, head_gain, raw, inner, part, weights, passed, *grads)


def kept_kernel(rank_ref, modality_ref, part_ref, weight_ref, back_ref, out_ref):
    base = pl.multiple_of(rank_ref[0] * out_ref.shape[1], HEAD_DIM)
    image = column(modality_ref[...]) > 0.0
    for start, size in chunks_of(out_ref.shape[1], HEAD_DIM):
        place = pl.ds(base + start, size)
        product = both_back(image, back_ref[...], weight_ref[:, place, :])
        out_ref[:, start : start + size] = product + part_ref[:, place]


def kept_stage(rank, modality, part, weights, back):
    return pl.pallas_call(
        kept_kernel,
        out_shape=jax.ShapeDtypeStruct((back.shape[0], weights.shape[1] // 2), f32),
        in_specs=[SMEM] + [VMEM] * 4,
        out_specs=VMEM,
        compiler_params=params(6),
        cost_estimate=cost(2),
        name="kept_stage",
    )(rank, modality, part, weights, back)


def finish_kernel(backs, inners, total_width, *refs):
    rank_ref, modality_ref, gain_ref, factor_ref, inputs_ref = refs[:5]
    back_refs = refs[5 : 5 + backs]
    inner_refs = refs[5 + backs : 5 + backs + inners]
    rest = refs[5 + backs + inners :]
    out_ref = rest[-1]
    width = inputs_ref.shape[1]
    image = column(modality_ref[...]) > 0.0
    gain = gain_ref[...]
    if gain.shape[1] != width:
        gain = gain_ref[:, pl.ds(pl.multiple_of(rank_ref[0] * width, HEAD_DIM), width)]
    scaling = jnp.where(image, gain[1:2, :], gain[0:1, :])
    factor = column(factor_ref[...])
    back = back_refs[0][...].astype(f32)
    for ref in back_refs[1:]:
        back += ref[...].astype(f32)
    inner = inner_refs[0][...]
    for ref in inner_refs[1:]:
        inner += ref[...]
    unit_rows = inputs_ref[...].astype(f32) * factor
    inner_mean = column(inner) * (1.0 / total_width)
    out_ref[...] = (factor * (scaling * back - unit_rows * inner_mean)).astype(bf16)
    if len(rest) == 4:
        kept_ref, other_ref, attention_ref, _ = rest
        attention_ref[...] = (kept_ref[...] + other_ref[...].astype(f32)).astype(bf16)


def finish(rank, total_width, modality, gain, factor, inputs, backs, inners, projected):
    shape = jax.ShapeDtypeStruct(inputs.shape, bf16)
    arrays = [modality, gain, factor, inputs, *backs, *inners, *projected]
    outs = [shape] * (2 if projected else 1)
    return pl.pallas_call(
        functools.partial(finish_kernel, len(backs), len(inners), total_width),
        out_shape=outs,
        in_specs=[SMEM] + [VMEM] * len(arrays),
        out_specs=[VMEM] * len(outs),
        compiler_params=params(6),
        cost_estimate=cost(1),
        name="finish",
    )(rank, *arrays)


def local(
    inputs,
    cotangent,
    norm_gain,
    head_gain,
    query_weight,
    key_weight,
    output_weight,
    modality,
    segments,
    block_order,
):
    tensor_rank = lax.axis_index("tensor")
    block_rank = lax.axis_index("seq")
    tensor_count = lax.axis_size("tensor")
    block_count = lax.axis_size("seq")
    local_rows, local_width = inputs.shape
    full_width = local_width * tensor_count
    split = tensor_count == 2
    swap = [(0, 1), (1, 0)]
    rank = tensor_rank.astype(jnp.int32).reshape(1)
    modality = modality.reshape(1, local_rows)
    segments = segments.reshape(block_count, local_rows)

    def spread(part):
        if split:
            return [part, lax.ppermute(part, "tensor", swap)]
        return [lax.all_gather(part, "tensor", axis=1, tiled=True)]

    def scatter_columns(part):
        return lax.psum_scatter(part, "tensor", scatter_dimension=1, tiled=True)

    memory, key_raw, normed, row_factor = key_stage(
        rank, modality, norm_gain, head_gain, key_weight, spread(inputs)
    )
    shared = tensor_count > KV_HEADS
    is_even = tensor_rank % 2 == 0
    pair_swap = [(i, i ^ 1) for i in range(tensor_count)]
    if shared:
        partner = lax.ppermute(memory, "tensor", pair_swap)
        memory = jnp.where(
            is_even,
            jnp.concatenate([memory, partner], 1),
            jnp.concatenate([partner, memory], 1),
        )
    memories = [memory]
    for step in seq_steps(block_count):
        memories.append(lax.ppermute(memory, "seq", seq_pairs(step, block_count)))

    query, query_raw, back_attended = middle_stage(
        rank, modality, head_gain, normed, output_weight, query_weight, spread(cotangent)
    )
    attended, query_back, inner, own_grad, *grads = attention_stage(
        block_rank.astype(jnp.int32).reshape(1),
        block_order,
        segments,
        modality,
        head_gain,
        query,
        query_raw,
        back_attended,
        memories,
    )
    incoming = [
        lax.ppermute(grad, "seq", inverted(seq_pairs(step, block_count)))
        for step, grad in reversed(list(zip(seq_steps(block_count), grads)))
    ]

    projected, gradient_part = turn_stage(
        rank, modality, output_weight, attended, query_back, query_weight, split
    )
    if shared:
        total = own_grad + sum(grad.astype(f32) for grad in incoming)
        low, high = total[:, :HEAD_DIM], total[:, HEAD_DIM:]
        outgoing = jnp.where(is_even, high, low).astype(bf16)
        sums = [jnp.where(is_even, low, high), lax.ppermute(outgoing, "tensor", pair_swap)]
    else:
        sums = [own_grad, *incoming]
    sent, slice_back, inner, passed = key_back_stage(
        rank,
        modality,
        head_gain,
        key_raw,
        inner,
        gradient_part,
        key_weight,
        projected[0],
        sums,
        split,
    )
    if split:
        inners = [inner, lax.ppermute(inner, "tensor", swap)]
        other = lax.ppermute(sent, "tensor", swap)
        kept = kept_stage(rank, modality, gradient_part, key_weight, slice_back)
        backs = [kept, other]
        projected = [projected[1], lax.ppermute(passed, "tensor", swap)]
        gain = norm_gain
    else:
        inners = [lax.psum(inner, "tensor")]
        backs = [scatter_columns(sent)]
        attention_out = scatter_columns(passed)
        projected = []
        gain = lax.dynamic_slice_in_dim(norm_gain, tensor_rank * local_width, local_width, 1)
    results = finish(
        rank, full_width, modality, gain, row_factor, inputs, backs, inners, projected
    )
    if split:
        attention_out = results[0]
    return (attention_out, results[-1])


def solution(mesh):
    return jax.shard_map(
        local,
        mesh=mesh,
        in_specs=(
            P(("dp", "seq"), "tensor"),
            P(("dp", "seq"), "tensor"),
            P(),
            P(),
            P(None, None, "tensor"),
            P(None, None, "tensor"),
            P(None, "tensor", None),
            P(("dp", "seq")),
            P("dp"),
            P("dp"),
        ),
        out_specs=(P(("dp", "seq"), "tensor"), P(("dp", "seq"), "tensor")),
        check_vma=False,
    )
```

```python
import functools
import math

import jax
import jax.numpy as jnp
from jax import lax
from jax.experimental import pallas as pl
from jax.experimental.pallas import tpu as pltpu
from jax.sharding import PartitionSpec as P

KV_HEADS = 4
HEAD_DIM = 128
MIB = 1024 * 1024

epsilon = 1e-06
bf16 = jnp.bfloat16
f32 = jnp.float32
SMEM = pl.BlockSpec(memory_space=pltpu.SMEM)
VMEM = pl.BlockSpec(memory_space=pltpu.VMEM)
ANY = pl.BlockSpec(memory_space=pl.ANY)


def seq_pairs(step, count):
    if count & (count - 1) == 0:
        return [(i, i ^ step) for i in range(count)]
    return [(i, (i + step) % count) for i in range(count)]


def seq_steps(count):
    return sorted(range(1, count), key=lambda step: (step != count // 2, step))


def seq_source(rank, step, count):
    if count & (count - 1) == 0:
        return rank ^ step
    return (rank - step) % count


def inverted(pairs):
    return [(b, a) for a, b in pairs]


def tile_of(extent, most):
    best = HEAD_DIM
    for size in range(HEAD_DIM, min(extent, most) + 1, HEAD_DIM):
        if extent % size == 0:
            best = size
    return best


def dot_nt(a, b):
    return lax.dot_general(a, b, (((1,), (1,)), ((), ())), preferred_element_type=f32)


def dot_tn(a, b):
    return lax.dot_general(a, b, (((0,), (0,)), ((), ())), preferred_element_type=f32)


def column(row):
    count = row.shape[1]
    return jnp.broadcast_to(row.astype(f32), (count, count)).T[:, :1]


def row_of(col):
    count = col.shape[0]
    return jnp.broadcast_to(col, (count, count)).T[:1, :]


def inverse_norm(values):
    return lax.rsqrt(jnp.mean(values * values, axis=-1, keepdims=True) + epsilon)


def norm_back(values, factor, scaling, upstream):
    unit_rows = values * factor
    inner_mean = jnp.mean(scaling * upstream * unit_rows, axis=-1, keepdims=True)
    return factor * (scaling * upstream - unit_rows * inner_mean)


def streamed(weights):
    return pltpu.with_memory_space_constraint(weights, pltpu.HBM)


def params(mib):
    return pltpu.CompilerParams(vmem_limit_bytes=mib * MIB)


def cost(micros):
    return pl.CostEstimate(
        flops=int(micros * 1e9), bytes_accessed=int(micros * 2e6), transcendentals=0
    )


def in_order(rank, part_refs):
    if len(part_refs) == 1:
        return part_refs[0][...]
    own, other = part_refs[0][...], part_refs[1][...]
    first = rank == 0
    return jnp.concatenate([jnp.where(first, own, other), jnp.where(first, other, own)], axis=1)


def both_experts(image, rows, weights):
    zero = jnp.zeros_like(rows)
    masked = jnp.concatenate([jnp.where(image, zero, rows), jnp.where(image, rows, zero)], axis=1)
    flat = weights.reshape(2 * weights.shape[1], weights.shape[2])
    return jnp.dot(masked, flat, preferred_element_type=f32)


def both_back(image, rows, weights):
    return jnp.where(image, dot_nt(rows, weights[1]), dot_nt(rows, weights[0]))


def chunks_of(extent, most):
    size = tile_of(extent, most)
    return [(start, size) for start in range(0, extent, size)]


AHEAD = 4


def copies_of(source_ref, target_ref, sem_ref, pieces, base=0, slots=0):
    copies = []
    for index, (start, size) in enumerate(pieces):
        pair = []
        for e in range(2):
            if slots:
                target = target_ref.at[index % slots, e]
            else:
                target = target_ref.at[e, pl.ds(start, size), :]
            source = source_ref.at[e, pl.ds(base + start, size), :]
            pair.append(pltpu.make_async_copy(source, target, sem_ref.at[index, e]))
        copies.append(pair)
    return copies


def begin(copies, index):
    if index < len(copies):
        for copy in copies[index]:
            copy.start()


def begin_first(copies):
    for index in range(AHEAD):
        begin(copies, index)


def arrive(copies, index):
    for copy in copies[index]:
        copy.wait()


def ring(weights, pieces):
    return pltpu.VMEM((AHEAD, 2, pieces[0][1], weights.shape[2]), weights.dtype)


def resident(weights):
    return pltpu.VMEM(weights.shape, weights.dtype)


def fetch_kernel(pieces, weight_ref, held_ref, sem_ref):
    copies = copies_of(weight_ref, held_ref, sem_ref, pieces)
    for pair in copies:
        for copy in pair:
            copy.start()
    for pair in copies:
        for copy in pair:
            copy.wait()


def fetch(weights):
    pieces = chunks_of(weights.shape[1], 896)
    return pl.pallas_call(
        functools.partial(fetch_kernel, pieces),
        out_shape=resident(weights),
        in_specs=[ANY],
        out_specs=VMEM,
        scratch_shapes=[pltpu.SemaphoreType.DMA((len(pieces), 2))],
        compiler_params=params(1),
        cost_estimate=cost(0.2),
        name="fetch",
    )(streamed(weights))


def key_kernel(count, *refs):
    rank_ref, modality_ref, gain_ref, head_ref, weight_ref = refs[:5]
    part_refs = refs[5 : 5 + count]
    memory_ref, raw_ref, normed_ref, factor_ref = refs[5 + count :]
    image = column(modality_ref[...]) > 0.0
    rows = in_order(rank_ref[0], part_refs).astype(f32)
    factor = inverse_norm(rows)
    scaling = jnp.where(image, gain_ref[1:2, :], gain_ref[0:1, :])
    normed_ref[...] = (rows * factor * scaling).astype(bf16)
    factor_ref[...] = row_of(factor)
    for index, (start, size) in enumerate(chunks_of(normed_ref.shape[1], 1792)):
        part = slice(start, start + size)
        product = both_experts(image, normed_ref[:, part], weight_ref[:, part, :])
        if index == 0:
            raw_ref[...] = product
        else:
            raw_ref[...] += product
    blocks = raw_ref.shape[1] // HEAD_DIM
    scaling = jnp.where(image, head_ref[1, 1:2, :], head_ref[0, 1:2, :])
    for b in range(blocks):
        part = slice(b * HEAD_DIM, (b + 1) * HEAD_DIM)
        raw = raw_ref[:, part]
        normed = raw * inverse_norm(raw) * scaling
        is_key = (rank_ref[0] * blocks + b) % 2 == 0
        memory_ref[:, part] = jnp.where(is_key, normed, raw).astype(bf16)


def key_stage(rank, modality, norm_gain, head_gain, weights, parts):
    _, depth, width = weights.shape
    rows = parts[0].shape[0]
    return pl.pallas_call(
        functools.partial(key_kernel, len(parts)),
        out_shape=[
            jax.ShapeDtypeStruct((rows, width), bf16),
            jax.ShapeDtypeStruct((rows, width), f32),
            jax.ShapeDtypeStruct((rows, depth), bf16),
            jax.ShapeDtypeStruct((1, rows), f32),
        ],
        in_specs=[SMEM] + [VMEM] * (4 + len(parts)),
        out_specs=[VMEM] * 4,
        compiler_params=params(8),
        cost_estimate=cost(10),
        name="key_stage",
    )(rank, modality, norm_gain, head_gain, weights, *parts)


def middle_kernel(count, pieces, *refs):
    rank_ref, modality_ref, head_ref, normed_ref, output_ref, query_weight_ref = refs[:6]
    part_refs = refs[6 : 6 + count]
    query_ref, raw_ref, back_ref, slots, sems = refs[6 + count :]
    copies = copies_of(query_weight_ref, slots, sems, pieces, slots=AHEAD)
    begin_first(copies)
    image = column(modality_ref[...]) > 0.0
    cotangent = in_order(rank_ref[0], part_refs)
    tiles = chunks_of(output_ref.shape[1], HEAD_DIM)
    done = 0
    for turn, (start, size) in enumerate(tiles, 1):
        part = slice(start, start + size)
        back_ref[:, part] = both_back(image, cotangent, output_ref[:, part, :]).astype(bf16)
        until = len(pieces) * turn // len(tiles)
        for index in range(done, until):
            arrive(copies, index)
            start, size = pieces[index]
            part = slice(start, start + size)
            product = both_experts(image, normed_ref[:, part], slots[index % AHEAD])
            if index == 0:
                raw_ref[...] = product
            else:
                raw_ref[...] += product
            begin(copies, index + AHEAD)
        done = until
    scaling = jnp.where(image, head_ref[1, 0:1, :], head_ref[0, 0:1, :])
    for h in range(raw_ref.shape[1] // HEAD_DIM):
        part = slice(h * HEAD_DIM, (h + 1) * HEAD_DIM)
        raw = raw_ref[:, part]
        query_ref[:, part] = (raw * inverse_norm(raw) * scaling).astype(bf16)


def middle_stage(rank, modality, head_gain, normed, output_weight, query_weight, parts):
    rows = normed.shape[0]
    width = query_weight.shape[2]
    pieces = chunks_of(query_weight.shape[1], 512)
    return pl.pallas_call(
        functools.partial(middle_kernel, len(parts), pieces),
        out_shape=[
            jax.ShapeDtypeStruct((rows, width), bf16),
            jax.ShapeDtypeStruct((rows, width), f32),
            jax.ShapeDtypeStruct((rows, width), bf16),
        ],
        in_specs=[SMEM, VMEM, VMEM, VMEM, VMEM, ANY] + [VMEM] * len(parts),
        out_specs=[VMEM] * 3,
        scratch_shapes=[
            ring(query_weight, pieces),
            pltpu.SemaphoreType.DMA((len(pieces), 2)),
        ],
        compiler_params=params(14),
        cost_estimate=cost(8),
        name="middle_stage",
    )(rank, modality, head_gain, normed, output_weight, streamed(query_weight), *parts)


def attention_kernel(blocks, pairs, per_group, *refs):
    place_ref, order_ref, segments_ref, modality_ref, head_ref = refs[:5]
    query_ref, raw_ref, back_ref = refs[5:8]
    memory_refs = refs[8 : 8 + blocks]
    attended_ref, query_back_ref, inner_ref = refs[8 + blocks : 11 + blocks]
    grad_refs = refs[11 + blocks :]
    rows = query_ref.shape[0]
    scale = 1.0 / math.sqrt(HEAD_DIM)
    lines = [
        segments_ref[pl.ds(order_ref[seq_source(place_ref[0], step, blocks)], 1), :]
        for step in [0, *seq_steps(blocks)]
    ]
    key_segments = jnp.concatenate(lines, axis=1).astype(f32)
    visible = key_segments <= column(lines[0])
    image = column(modality_ref[...]) > 0.0
    scaling = jnp.where(image, head_ref[1, 0:1, :], head_ref[0, 0:1, :])
    inner = jnp.zeros((rows, 1), f32)
    for pair in range(pairs):
        columns = [
            slice(h * HEAD_DIM, (h + 1) * HEAD_DIM)
            for h in range(pair * per_group, (pair + 1) * per_group)
        ]
        parts = [slice(h * rows, (h + 1) * rows) for h in range(per_group)]
        keys = slice(2 * pair * HEAD_DIM, (2 * pair + 1) * HEAD_DIM)
        values = slice((2 * pair + 1) * HEAD_DIM, (2 * pair + 2) * HEAD_DIM)
        query = jnp.concatenate([query_ref[:, c] for c in columns], axis=0)
        back = jnp.concatenate([back_ref[:, c] for c in columns], axis=0)
        key = jnp.concatenate([m[:, keys] for m in memory_refs], axis=0)
        value = jnp.concatenate([m[:, values] for m in memory_refs], axis=0)
        scores = dot_nt(query, key) * (scale * math.log2(math.e))
        weights = jnp.concatenate(
            [jnp.where(visible, jnp.exp2(scores[p]), 0.0).astype(bf16) for p in parts], axis=0
        )
        weights32 = weights.astype(f32)
        inverse = 1.0 / jnp.sum(weights32, axis=1, keepdims=True)
        numerator = jnp.dot(weights, value, preferred_element_type=f32)
        attended = (numerator * inverse).astype(bf16)
        offset = jnp.sum(back.astype(f32) * attended.astype(f32), axis=1, keepdims=True)
        probability = (weights32 * inverse).astype(bf16)
        back_prob = dot_nt(back, value)
        back_score = (probability.astype(f32) * (back_prob - offset)).astype(bf16)
        back_query = jnp.dot(back_score, key, preferred_element_type=f32) * scale
        back_key = dot_tn(back_score, query) * scale
        back_value = dot_tn(probability, back)
        for b, grad_ref in enumerate(grad_refs):
            part = slice(b * rows, (b + 1) * rows)
            grad_ref[:, keys] = back_key[part].astype(grad_ref.dtype)
            grad_ref[:, values] = back_value[part].astype(grad_ref.dtype)
        for part, place in zip(parts, columns):
            attended_ref[:, place] = attended[part]
            raw = raw_ref[:, place]
            query_back = norm_back(raw, inverse_norm(raw), scaling, back_query[part]).astype(bf16)
            query_back_ref[:, place] = query_back
            inner += jnp.sum(query_back.astype(f32) * raw, axis=1, keepdims=True)
    inner_ref[...] = row_of(inner)


def attention_stage(place, order, segments, modality, head_gain, query, raw, back, memories):
    rows, width = query.shape
    blocks = len(memories)
    pairs = memories[0].shape[1] // (2 * HEAD_DIM)
    per_group = width // HEAD_DIM // pairs
    outs = [
        jax.ShapeDtypeStruct((rows, width), bf16),
        jax.ShapeDtypeStruct((rows, width), bf16),
        jax.ShapeDtypeStruct((1, rows), f32),
    ] + [
        jax.ShapeDtypeStruct((rows, pairs * 2 * HEAD_DIM), f32 if b == 0 else bf16)
        for b in range(blocks)
    ]
    return pl.pallas_call(
        functools.partial(attention_kernel, blocks, pairs, per_group),
        out_shape=outs,
        in_specs=[SMEM, SMEM] + [VMEM] * (6 + blocks),
        out_specs=[VMEM] * (3 + blocks),
        compiler_params=params(12),
        cost_estimate=cost(4),
        name="attention_stage",
    )(place, order, segments, modality, head_gain, query, raw, back, *memories)


def turn_kernel(pieces, outputs, *refs):
    rank_ref, modality_ref, output_ref, attended_ref, back_ref, query_ref = refs[:6]
    out_refs = refs[6 : 6 + outputs]
    part_ref, slots, sems = refs[6 + outputs :]
    copies = copies_of(query_ref, slots, sems, pieces, slots=AHEAD)
    begin_first(copies)
    image = column(modality_ref[...]) > 0.0
    attended = attended_ref[...]
    extent = output_ref.shape[2] // 2

    def project(rank):
        sent_ref, kept_ref = out_refs
        for start, size in chunks_of(extent, 896):
            part = slice(start, start + size)
            first = (1 - rank) * extent + start
            product = both_experts(image, attended, output_ref[:, :, first : first + size])
            sent_ref[:, part] = product.astype(bf16)
            first = rank * extent + start
            product = both_experts(image, attended, output_ref[:, :, first : first + size])
            kept_ref[:, part] = product

    if outputs == 1:
        out_refs[0][...] = both_experts(image, attended, output_ref[...]).astype(bf16)
    else:
        for rank in range(2):
            pl.when(rank_ref[0] == rank)(functools.partial(project, rank))
    for index, (start, size) in enumerate(pieces):
        arrive(copies, index)
        for inside, tile in chunks_of(size, HEAD_DIM):
            weights = slots[index % AHEAD, :, inside : inside + tile, :]
            part = slice(start + inside, start + inside + tile)
            part_ref[:, part] = both_back(image, back_ref[...], weights)
        begin(copies, index + AHEAD)


def turn_stage(rank, modality, output_weight, attended, query_back, query_weight, split):
    depth = query_weight.shape[1]
    width = output_weight.shape[2]
    rows = attended.shape[0]
    pieces = chunks_of(depth, 512)
    if split:
        outs = [
            jax.ShapeDtypeStruct((rows, width // 2), bf16),
            jax.ShapeDtypeStruct((rows, width // 2), f32),
        ]
    else:
        outs = [jax.ShapeDtypeStruct((rows, width), bf16)]
    *projected, part = pl.pallas_call(
        functools.partial(turn_kernel, pieces, len(outs)),
        out_shape=outs + [jax.ShapeDtypeStruct((rows, depth), f32)],
        in_specs=[SMEM, VMEM, VMEM, VMEM, VMEM, ANY],
        out_specs=[VMEM] * (len(outs) + 1),
        scratch_shapes=[
            ring(query_weight, pieces),
            pltpu.SemaphoreType.DMA((len(pieces), 2)),
        ],
        compiler_params=params(16),
        cost_estimate=cost(10),
        name="turn_stage",
    )(rank, modality, output_weight, attended, query_back, streamed(query_weight))
    return projected, part


def tie(passed, arrived):
    def kernel(passed_ref, arrived_ref, out_ref):
        del passed_ref, arrived_ref, out_ref

    return pl.pallas_call(
        kernel,
        out_shape=jax.ShapeDtypeStruct(passed.shape, passed.dtype),
        in_specs=[ANY, ANY],
        out_specs=ANY,
        input_output_aliases={0: 0},
        compiler_params=params(1),
        cost_estimate=cost(0.1),
        name="tie",
    )(passed, arrived)


def merge_kernel(kept_ref, other_ref, out_ref):
    out_ref[...] = (kept_ref[...] + other_ref[...].astype(f32)).astype(bf16)


def merge(kept, other):
    return pl.pallas_call(
        merge_kernel,
        out_shape=jax.ShapeDtypeStruct(other.shape, bf16),
        in_specs=[VMEM, VMEM],
        out_specs=VMEM,
        compiler_params=params(4),
        cost_estimate=cost(0.5),
        name="merge",
    )(kept, other)


def key_back_kernel(split, *refs):
    rank_ref, modality_ref, head_ref, raw_ref, inner_in_ref, part_ref, weight_ref = refs[:7]
    grad_refs = refs[7:-3]
    out_ref, back_ref, inner_ref = refs[-3:]
    base = pl.multiple_of((1 - rank_ref[0]) * out_ref.shape[1], HEAD_DIM) if split else 0
    image = column(modality_ref[...]) > 0.0
    blocks = raw_ref.shape[1] // HEAD_DIM
    scaling = jnp.where(image, head_ref[1, 1:2, :], head_ref[0, 1:2, :])
    inner = jnp.zeros((raw_ref.shape[0], 1), f32)
    for b in range(blocks):
        part = slice(b * HEAD_DIM, (b + 1) * HEAD_DIM)
        raw = raw_ref[:, part]
        upstream = grad_refs[0][:, part].astype(f32)
        for grad_ref in grad_refs[1:]:
            upstream += grad_ref[:, part].astype(f32)
        is_key = (rank_ref[0] * blocks + b) % 2 == 0
        normed_back = norm_back(raw, inverse_norm(raw), scaling, upstream)
        back = jnp.where(is_key, normed_back, upstream).astype(bf16)
        back_ref[:, part] = back
        inner += jnp.sum(back.astype(f32) * raw, axis=1, keepdims=True)
    inner_ref[...] = inner_in_ref[...] + row_of(inner)
    for start, size in chunks_of(out_ref.shape[1], HEAD_DIM):
        place = pl.ds(base + start, size)
        product = both_back(image, back_ref[...], weight_ref[:, place, :])
        out_ref[:, start : start + size] = (product + part_ref[:, place]).astype(bf16)


def key_back_stage(rank, modality, head_gain, raw, inner, part, weights, grads, split):
    _, depth, width = weights.shape
    rows = raw.shape[0]
    return pl.pallas_call(
        functools.partial(key_back_kernel, split),
        out_shape=[
            jax.ShapeDtypeStruct((rows, depth // 2 if split else depth), bf16),
            jax.ShapeDtypeStruct((rows, width), bf16),
            jax.ShapeDtypeStruct((1, rows), f32),
        ],
        in_specs=[SMEM] + [VMEM] * (6 + len(grads)),
        out_specs=[VMEM] * 3,
        compiler_params=params(6),
        cost_estimate=cost(2),
        name="key_back_stage",
    )(rank, modality, head_gain, raw, inner, part, weights, *grads)


def kept_kernel(rank_ref, modality_ref, part_ref, weight_ref, back_ref, out_ref):
    base = pl.multiple_of(rank_ref[0] * out_ref.shape[1], HEAD_DIM)
    image = column(modality_ref[...]) > 0.0
    for start, size in chunks_of(out_ref.shape[1], HEAD_DIM):
        place = pl.ds(base + start, size)
        product = both_back(image, back_ref[...], weight_ref[:, place, :])
        out_ref[:, start : start + size] = product + part_ref[:, place]


def kept_stage(rank, modality, part, weights, back):
    return pl.pallas_call(
        kept_kernel,
        out_shape=jax.ShapeDtypeStruct((back.shape[0], weights.shape[1] // 2), f32),
        in_specs=[SMEM] + [VMEM] * 4,
        out_specs=VMEM,
        compiler_params=params(6),
        cost_estimate=cost(2),
        name="kept_stage",
    )(rank, modality, part, weights, back)


def finish_kernel(backs, inners, total_width, *refs):
    rank_ref, modality_ref, gain_ref, factor_ref, inputs_ref = refs[:5]
    back_refs = refs[5 : 5 + backs]
    inner_refs = refs[5 + backs : 5 + backs + inners]
    out_ref = refs[-1]
    width = inputs_ref.shape[1]
    image = column(modality_ref[...]) > 0.0
    gain = gain_ref[...]
    if gain.shape[1] != width:
        gain = gain_ref[:, pl.ds(pl.multiple_of(rank_ref[0] * width, HEAD_DIM), width)]
    scaling = jnp.where(image, gain[1:2, :], gain[0:1, :])
    factor = column(factor_ref[...])
    back = back_refs[0][...].astype(f32)
    for ref in back_refs[1:]:
        back += ref[...].astype(f32)
    inner = inner_refs[0][...]
    for ref in inner_refs[1:]:
        inner += ref[...]
    unit_rows = inputs_ref[...].astype(f32) * factor
    inner_mean = column(inner) * (1.0 / total_width)
    out_ref[...] = (factor * (scaling * back - unit_rows * inner_mean)).astype(bf16)


def finish(rank, total_width, modality, gain, factor, inputs, backs, inners):
    arrays = [modality, gain, factor, inputs, *backs, *inners]
    return pl.pallas_call(
        functools.partial(finish_kernel, len(backs), len(inners), total_width),
        out_shape=jax.ShapeDtypeStruct(inputs.shape, bf16),
        in_specs=[SMEM] + [VMEM] * len(arrays),
        out_specs=VMEM,
        compiler_params=params(6),
        cost_estimate=cost(1),
        name="finish",
    )(rank, *arrays)


def local(
    inputs,
    cotangent,
    norm_gain,
    head_gain,
    query_weight,
    key_weight,
    output_weight,
    modality,
    segments,
    block_order,
):
    tensor_rank = lax.axis_index("tensor")
    block_rank = lax.axis_index("seq")
    tensor_count = lax.axis_size("tensor")
    block_count = lax.axis_size("seq")
    local_rows, local_width = inputs.shape
    full_width = local_width * tensor_count
    split = tensor_count == 2
    swap = [(0, 1), (1, 0)]
    rank = tensor_rank.astype(jnp.int32).reshape(1)
    modality = modality.reshape(1, local_rows)
    segments = segments.reshape(block_count, local_rows)

    def spread(part):
        if split:
            return [part, lax.ppermute(part, "tensor", swap)]
        return [lax.all_gather(part, "tensor", axis=1, tiled=True)]

    def scatter_columns(part):
        return lax.psum_scatter(part, "tensor", scatter_dimension=1, tiled=True)

    memory, key_raw, normed, row_factor = key_stage(
        rank, modality, norm_gain, head_gain, fetch(key_weight), spread(inputs)
    )
    shared = tensor_count > KV_HEADS
    is_even = tensor_rank % 2 == 0
    pair_swap = [(i, i ^ 1) for i in range(tensor_count)]
    if shared:
        partner = lax.ppermute(memory, "tensor", pair_swap)
        memory = jnp.where(
            is_even,
            jnp.concatenate([memory, partner], 1),
            jnp.concatenate([partner, memory], 1),
        )
    memories = [memory]
    for step in seq_steps(block_count):
        memories.append(lax.ppermute(memory, "seq", seq_pairs(step, block_count)))

    query, query_raw, back_attended = middle_stage(
        rank, modality, head_gain, normed, output_weight, query_weight, spread(cotangent)
    )
    attended, query_back, inner, own_grad, *grads = attention_stage(
        block_rank.astype(jnp.int32).reshape(1),
        block_order,
        segments,
        modality,
        head_gain,
        query,
        query_raw,
        back_attended,
        memories,
    )
    incoming = [
        lax.ppermute(grad, "seq", inverted(seq_pairs(step, block_count)))
        for step, grad in zip(seq_steps(block_count), grads)
    ]

    projected, gradient_part = turn_stage(
        rank, modality, output_weight, attended, query_back, query_weight, split
    )
    if split:
        passed = tie(projected[0], incoming[0])
        attention_out = merge(projected[1], lax.ppermute(passed, "tensor", swap))
    else:
        attention_out = scatter_columns(projected[0])

    if shared:
        total = own_grad + sum(grad.astype(f32) for grad in incoming)
        low, high = total[:, :HEAD_DIM], total[:, HEAD_DIM:]
        outgoing = jnp.where(is_even, high, low).astype(bf16)
        sums = [jnp.where(is_even, low, high), lax.ppermute(outgoing, "tensor", pair_swap)]
    else:
        sums = [own_grad, *incoming]
    sent, slice_back, inner = key_back_stage(
        rank,
        modality,
        head_gain,
        key_raw,
        inner,
        gradient_part,
        key_weight,
        sums,
        split,
    )
    if split:
        inners = [inner, lax.ppermute(inner, "tensor", swap)]
        other = lax.ppermute(sent, "tensor", swap)
        kept = kept_stage(rank, modality, gradient_part, key_weight, slice_back)
        backs = [kept, other]
        gain = norm_gain
    else:
        inners = [lax.psum(inner, "tensor")]
        backs = [scatter_columns(sent)]
        gain = lax.dynamic_slice_in_dim(norm_gain, tensor_rank * local_width, local_width, 1)
    grad_input = finish(rank, full_width, modality, gain, row_factor, inputs, backs, inners)
    return (attention_out, grad_input)


def solution(mesh):
    return jax.shard_map(
        local,
        mesh=mesh,
        in_specs=(
            P(("dp", "seq"), "tensor"),
            P(("dp", "seq"), "tensor"),
            P(),
            P(),
            P(None, None, "tensor"),
            P(None, None, "tensor"),
            P(None, "tensor", None),
            P(("dp", "seq")),
            P("dp"),
            P("dp"),
        ),
        out_specs=(P(("dp", "seq"), "tensor"), P(("dp", "seq"), "tensor")),
        check_vma=False,
    )
```

```python
import functools
import math

import jax
import jax.numpy as jnp
from jax import lax
from jax.experimental import pallas as pl
from jax.experimental.pallas import tpu as pltpu
from jax.sharding import PartitionSpec as P

KV_HEADS = 4
HEAD_DIM = 128
MIB = 1024 * 1024

epsilon = 1e-06
bf16 = jnp.bfloat16
f32 = jnp.float32
SMEM = pl.BlockSpec(memory_space=pltpu.SMEM)
VMEM = pl.BlockSpec(memory_space=pltpu.VMEM)
ANY = pl.BlockSpec(memory_space=pl.ANY)


def seq_pairs(step, count):
    if count & (count - 1) == 0:
        return [(i, i ^ step) for i in range(count)]
    return [(i, (i + step) % count) for i in range(count)]


def seq_steps(count):
    return sorted(range(1, count), key=lambda step: (step != count // 2, step))


def seq_source(rank, step, count):
    if count & (count - 1) == 0:
        return rank ^ step
    return (rank - step) % count


def inverted(pairs):
    return [(b, a) for a, b in pairs]


def tile_of(extent, most):
    best = HEAD_DIM
    for size in range(HEAD_DIM, min(extent, most) + 1, HEAD_DIM):
        if extent % size == 0:
            best = size
    return best


def dot_nt(a, b):
    return lax.dot_general(a, b, (((1,), (1,)), ((), ())), preferred_element_type=f32)


def dot_tn(a, b):
    return lax.dot_general(a, b, (((0,), (0,)), ((), ())), preferred_element_type=f32)


def column(row):
    count = row.shape[1]
    return jnp.broadcast_to(row.astype(f32), (count, count)).T[:, :1]


def row_of(col):
    count = col.shape[0]
    return jnp.broadcast_to(col, (count, count)).T[:1, :]


def inverse_norm(values):
    return lax.rsqrt(jnp.mean(values * values, axis=-1, keepdims=True) + epsilon)


def norm_back(values, factor, scaling, upstream):
    unit_rows = values * factor
    inner_mean = jnp.mean(scaling * upstream * unit_rows, axis=-1, keepdims=True)
    return factor * (scaling * upstream - unit_rows * inner_mean)


def streamed(weights):
    return pltpu.with_memory_space_constraint(weights, pltpu.HBM)


def params(mib):
    return pltpu.CompilerParams(vmem_limit_bytes=mib * MIB)


def cost(micros):
    return pl.CostEstimate(
        flops=int(micros * 1e9), bytes_accessed=int(micros * 2e6), transcendentals=0
    )


def in_order(rank, part_refs):
    if len(part_refs) == 1:
        return part_refs[0][...]
    own, other = part_refs[0][...], part_refs[1][...]
    first = rank == 0
    return jnp.concatenate([jnp.where(first, own, other), jnp.where(first, other, own)], axis=1)


def both_experts(image, rows, weights):
    zero = jnp.zeros_like(rows)
    masked = jnp.concatenate([jnp.where(image, zero, rows), jnp.where(image, rows, zero)], axis=1)
    flat = weights.reshape(2 * weights.shape[1], weights.shape[2])
    return jnp.dot(masked, flat, preferred_element_type=f32)


def both_back(image, rows, weights):
    return jnp.where(image, dot_nt(rows, weights[1]), dot_nt(rows, weights[0]))


def chunks_of(extent, most):
    size = tile_of(extent, most)
    return [(start, size) for start in range(0, extent, size)]


AHEAD = 4


def copies_of(source_ref, target_ref, sem_ref, pieces, base=0, slots=0):
    copies = []
    for index, (start, size) in enumerate(pieces):
        pair = []
        for e in range(2):
            if slots:
                target = target_ref.at[index % slots, e]
            else:
                target = target_ref.at[e, pl.ds(start, size), :]
            source = source_ref.at[e, pl.ds(base + start, size), :]
            pair.append(pltpu.make_async_copy(source, target, sem_ref.at[index, e]))
        copies.append(pair)
    return copies


def begin(copies, index):
    if index < len(copies):
        for copy in copies[index]:
            copy.start()


def begin_first(copies):
    for index in range(AHEAD):
        begin(copies, index)


def arrive(copies, index):
    for copy in copies[index]:
        copy.wait()


def ring(weights, pieces):
    return pltpu.VMEM((AHEAD, 2, pieces[0][1], weights.shape[2]), weights.dtype)


def gain_of(image, gain_ref, columns):
    return jnp.where(image, gain_ref[1:2, columns], gain_ref[0:1, columns])


def early_kernel(pieces, *refs):
    rank_ref, weight_ref = refs[:2]
    given_refs, (scaled_ref, squares_ref, total_ref, held_ref) = refs[2:5], refs[5:9]
    own_held, sems, held_sems, given_sems = refs[9:13]
    modality_ref, gain_ref, own_ref = refs[13:]
    given = [
        pltpu.make_async_copy(source, target, given_sems.at[index])
        for index, (source, target) in enumerate(zip(given_refs, refs[13:]))
    ]
    for copy in given:
        copy.start()
    extent = own_ref.shape[1]
    base = pl.multiple_of(rank_ref[0] * extent, HEAD_DIM)
    away = pl.multiple_of((1 - rank_ref[0]) * extent, HEAD_DIM)
    copies = copies_of(weight_ref, own_held, sems, pieces, base)
    copies += copies_of(weight_ref, held_ref, held_sems, pieces, away)
    for index in range(len(copies)):
        begin(copies, index)
    for copy in given:
        copy.wait()
    image = column(modality_ref[...]) > 0.0
    rows = own_ref[...].astype(f32)
    squares_ref[...] = row_of(jnp.sum(rows * rows, axis=1, keepdims=True))
    scaled_ref[...] = (rows * gain_of(image, gain_ref, pl.ds(base, extent))).astype(bf16)
    for index, (start, size) in enumerate(pieces):
        arrive(copies, index)
        part = slice(start, start + size)
        product = both_experts(image, scaled_ref[:, part], own_held[:, part, :])
        if index == 0:
            total_ref[...] = product
        else:
            total_ref[...] += product
    for index in range(len(pieces), len(copies)):
        arrive(copies, index)


def early_stage(rank, modality, norm_gain, own, weights):
    _, depth, width = weights.shape
    rows, extent = own.shape
    pieces = chunks_of(extent, 896)
    half_weights = (2, extent, width)
    given = [modality, norm_gain, own]
    return pl.pallas_call(
        functools.partial(early_kernel, pieces),
        out_shape=[
            jax.ShapeDtypeStruct((rows, extent), bf16),
            jax.ShapeDtypeStruct((1, rows), f32),
            jax.ShapeDtypeStruct((rows, width), f32),
            pltpu.VMEM(half_weights, bf16),
        ],
        in_specs=[SMEM] + [ANY] * 4,
        out_specs=[VMEM] * 4,
        scratch_shapes=[
            pltpu.VMEM(half_weights, bf16),
            pltpu.SemaphoreType.DMA((len(pieces), 2)),
            pltpu.SemaphoreType.DMA((len(pieces), 2)),
            pltpu.SemaphoreType.DMA((len(given),)),
        ]
        + [pltpu.VMEM(g.shape, g.dtype) for g in given],
        compiler_params=params(8),
        cost_estimate=cost(0.2),
        name="early_stage",
    )(rank, streamed(weights), *(streamed(g) for g in given))


def key_kernel(split, *refs):
    rank_ref, modality_ref, gain_ref, head_ref, weight_ref, rows_ref = refs[:6]
    memory_ref, raw_ref, scaled_ref, factor_ref = refs[-4:]
    image = column(modality_ref[...]) > 0.0
    rows = rows_ref[...].astype(f32)
    extent = rows.shape[1]
    squares = jnp.sum(rows * rows, axis=1, keepdims=True)
    if split:
        own_ref, own_squares_ref, own_total_ref = refs[6:9]
        squares += column(own_squares_ref[...])
        columns = pl.ds(pl.multiple_of((1 - rank_ref[0]) * extent, HEAD_DIM), extent)
    else:
        columns = slice(0, extent)
    scaled = (rows * gain_of(image, gain_ref, columns)).astype(bf16)
    total = both_experts(image, scaled, weight_ref[...])
    factor = lax.rsqrt(squares * (1.0 / scaled_ref.shape[1]) + epsilon)
    factor_ref[...] = row_of(factor)
    if split:
        total += own_total_ref[...]
        first = rank_ref[0] == 0
        own = own_ref[...]
        scaled_ref[:, :extent] = jnp.where(first, own, scaled)
        scaled_ref[:, extent:] = jnp.where(first, scaled, own)
    else:
        scaled_ref[...] = scaled
    raw_ref[...] = total * factor
    blocks = raw_ref.shape[1] // HEAD_DIM
    scaling = jnp.where(image, head_ref[1, 1:2, :], head_ref[0, 1:2, :])
    for b in range(blocks):
        part = slice(b * HEAD_DIM, (b + 1) * HEAD_DIM)
        raw = raw_ref[:, part]
        normed = raw * inverse_norm(raw) * scaling
        is_key = (rank_ref[0] * blocks + b) % 2 == 0
        memory_ref[:, part] = jnp.where(is_key, normed, raw).astype(bf16)


def key_stage(rank, modality, norm_gain, head_gain, weights, part, early):
    width = weights.shape[2]
    rows = part.shape[0]
    depth = norm_gain.shape[1]
    return pl.pallas_call(
        functools.partial(key_kernel, len(early) > 0),
        out_shape=[
            jax.ShapeDtypeStruct((rows, width), bf16),
            jax.ShapeDtypeStruct((rows, width), f32),
            jax.ShapeDtypeStruct((rows, depth), bf16),
            jax.ShapeDtypeStruct((1, rows), f32),
        ],
        in_specs=[SMEM] + [VMEM] * (5 + len(early)),
        out_specs=[VMEM] * 4,
        compiler_params=params(8),
        cost_estimate=cost(10),
        name="key_stage",
    )(rank, modality, norm_gain, head_gain, weights, part, *early)


def middle_kernel(count, pieces, *refs):
    rank_ref, modality_ref, head_ref, scaled_ref, factor_ref, output_ref = refs[:6]
    query_weight_ref = refs[6]
    part_refs = refs[7 : 7 + count]
    query_ref, raw_ref, back_ref, slots, sems = refs[7 + count :]
    copies = copies_of(query_weight_ref, slots, sems, pieces, slots=AHEAD)
    begin_first(copies)
    image = column(modality_ref[...]) > 0.0
    cotangent = in_order(rank_ref[0], part_refs)
    tiles = chunks_of(output_ref.shape[1], HEAD_DIM)
    done = 0
    for turn, (start, size) in enumerate(tiles, 1):
        part = slice(start, start + size)
        back_ref[:, part] = both_back(image, cotangent, output_ref[:, part, :]).astype(bf16)
        until = len(pieces) * turn // len(tiles)
        for index in range(done, until):
            arrive(copies, index)
            start, size = pieces[index]
            part = slice(start, start + size)
            product = both_experts(image, scaled_ref[:, part], slots[index % AHEAD])
            if index == 0:
                raw_ref[...] = product
            else:
                raw_ref[...] += product
            begin(copies, index + AHEAD)
        done = until
    factor = column(factor_ref[...])
    scaling = jnp.where(image, head_ref[1, 0:1, :], head_ref[0, 0:1, :])
    for h in range(raw_ref.shape[1] // HEAD_DIM):
        part = slice(h * HEAD_DIM, (h + 1) * HEAD_DIM)
        raw = raw_ref[:, part] * factor
        raw_ref[:, part] = raw
        query_ref[:, part] = (raw * inverse_norm(raw) * scaling).astype(bf16)


def middle_stage(rank, modality, head_gain, scaled, factor, output_weight, query_weight, parts):
    rows = scaled.shape[0]
    width = query_weight.shape[2]
    pieces = chunks_of(query_weight.shape[1], 512)
    return pl.pallas_call(
        functools.partial(middle_kernel, len(parts), pieces),
        out_shape=[
            jax.ShapeDtypeStruct((rows, width), bf16),
            jax.ShapeDtypeStruct((rows, width), f32),
            jax.ShapeDtypeStruct((rows, width), bf16),
        ],
        in_specs=[SMEM, VMEM, VMEM, VMEM, VMEM, VMEM, ANY] + [VMEM] * len(parts),
        out_specs=[VMEM] * 3,
        scratch_shapes=[
            ring(query_weight, pieces),
            pltpu.SemaphoreType.DMA((len(pieces), 2)),
        ],
        compiler_params=params(14),
        cost_estimate=cost(8),
        name="middle_stage",
    )(
        rank,
        modality,
        head_gain,
        scaled,
        factor,
        output_weight,
        streamed(query_weight),
        *parts,
    )


def attention_kernel(blocks, pairs, per_group, *refs):
    place_ref, order_ref, segments_ref, modality_ref, head_ref = refs[:5]
    query_ref, raw_ref, back_ref = refs[5:8]
    memory_refs = refs[8 : 8 + blocks]
    attended_ref, query_back_ref, inner_ref = refs[8 + blocks : 11 + blocks]
    grad_refs = refs[11 + blocks :]
    rows = query_ref.shape[0]
    scale = 1.0 / math.sqrt(HEAD_DIM)
    lines = [
        segments_ref[pl.ds(order_ref[seq_source(place_ref[0], step, blocks)], 1), :]
        for step in [0, *seq_steps(blocks)]
    ]
    key_segments = jnp.concatenate(lines, axis=1).astype(f32)
    visible = key_segments <= column(lines[0])
    image = column(modality_ref[...]) > 0.0
    scaling = jnp.where(image, head_ref[1, 0:1, :], head_ref[0, 0:1, :])
    inner = jnp.zeros((rows, 1), f32)
    for pair in range(pairs):
        columns = [
            slice(h * HEAD_DIM, (h + 1) * HEAD_DIM)
            for h in range(pair * per_group, (pair + 1) * per_group)
        ]
        parts = [slice(h * rows, (h + 1) * rows) for h in range(per_group)]
        keys = slice(2 * pair * HEAD_DIM, (2 * pair + 1) * HEAD_DIM)
        values = slice((2 * pair + 1) * HEAD_DIM, (2 * pair + 2) * HEAD_DIM)
        query = jnp.concatenate([query_ref[:, c] for c in columns], axis=0)
        back = jnp.concatenate([back_ref[:, c] for c in columns], axis=0)
        key = jnp.concatenate([m[:, keys] for m in memory_refs], axis=0)
        value = jnp.concatenate([m[:, values] for m in memory_refs], axis=0)
        scores = dot_nt(query, key) * (scale * math.log2(math.e))
        weights = jnp.concatenate(
            [jnp.where(visible, jnp.exp2(scores[p]), 0.0).astype(bf16) for p in parts], axis=0
        )
        weights32 = weights.astype(f32)
        inverse = 1.0 / jnp.sum(weights32, axis=1, keepdims=True)
        numerator = jnp.dot(weights, value, preferred_element_type=f32)
        attended = (numerator * inverse).astype(bf16)
        offset = jnp.sum(back.astype(f32) * attended.astype(f32), axis=1, keepdims=True)
        probability = (weights32 * inverse).astype(bf16)
        back_prob = dot_nt(back, value)
        back_score = (probability.astype(f32) * (back_prob - offset)).astype(bf16)
        back_query = jnp.dot(back_score, key, preferred_element_type=f32) * scale
        back_key = dot_tn(back_score, query) * scale
        back_value = dot_tn(probability, back)
        for b, grad_ref in enumerate(grad_refs):
            part = slice(b * rows, (b + 1) * rows)
            grad_ref[:, keys] = back_key[part].astype(grad_ref.dtype)
            grad_ref[:, values] = back_value[part].astype(grad_ref.dtype)
        for part, place in zip(parts, columns):
            attended_ref[:, place] = attended[part]
            raw = raw_ref[:, place]
            query_back = norm_back(raw, inverse_norm(raw), scaling, back_query[part]).astype(bf16)
            query_back_ref[:, place] = query_back
            inner += jnp.sum(query_back.astype(f32) * raw, axis=1, keepdims=True)
    inner_ref[...] = row_of(inner)


def attention_stage(place, order, segments, modality, head_gain, query, raw, back, memories):
    rows, width = query.shape
    blocks = len(memories)
    pairs = memories[0].shape[1] // (2 * HEAD_DIM)
    per_group = width // HEAD_DIM // pairs
    outs = [
        jax.ShapeDtypeStruct((rows, width), bf16),
        jax.ShapeDtypeStruct((rows, width), bf16),
        jax.ShapeDtypeStruct((1, rows), f32),
    ] + [
        jax.ShapeDtypeStruct((rows, pairs * 2 * HEAD_DIM), f32 if b == 0 else bf16)
        for b in range(blocks)
    ]
    return pl.pallas_call(
        functools.partial(attention_kernel, blocks, pairs, per_group),
        out_shape=outs,
        in_specs=[SMEM, SMEM] + [VMEM] * (6 + blocks),
        out_specs=[VMEM] * (3 + blocks),
        compiler_params=params(12),
        cost_estimate=cost(4),
        name="attention_stage",
    )(place, order, segments, modality, head_gain, query, raw, back, *memories)


def turn_kernel(pieces, outputs, *refs):
    rank_ref, modality_ref, output_ref, attended_ref, back_ref, query_ref = refs[:6]
    out_refs = refs[6 : 6 + outputs]
    part_ref, slots, sems = refs[6 + outputs :]
    copies = copies_of(query_ref, slots, sems, pieces, slots=AHEAD)
    begin_first(copies)
    image = column(modality_ref[...]) > 0.0
    attended = attended_ref[...]
    extent = output_ref.shape[2] // 2

    def project(rank):
        sent_ref, kept_ref = out_refs
        for start, size in chunks_of(extent, 896):
            part = slice(start, start + size)
            first = (1 - rank) * extent + start
            product = both_experts(image, attended, output_ref[:, :, first : first + size])
            sent_ref[:, part] = product.astype(bf16)
            first = rank * extent + start
            product = both_experts(image, attended, output_ref[:, :, first : first + size])
            kept_ref[:, part] = product

    if outputs == 1:
        out_refs[0][...] = both_experts(image, attended, output_ref[...]).astype(bf16)
    else:
        for rank in range(2):
            pl.when(rank_ref[0] == rank)(functools.partial(project, rank))
    for index, (start, size) in enumerate(pieces):
        arrive(copies, index)
        for inside, tile in chunks_of(size, HEAD_DIM):
            weights = slots[index % AHEAD, :, inside : inside + tile, :]
            part = slice(start + inside, start + inside + tile)
            part_ref[:, part] = both_back(image, back_ref[...], weights)
        begin(copies, index + AHEAD)


def turn_stage(rank, modality, output_weight, attended, query_back, query_weight, split):
    depth = query_weight.shape[1]
    width = output_weight.shape[2]
    rows = attended.shape[0]
    pieces = chunks_of(depth, 512)
    if split:
        outs = [
            jax.ShapeDtypeStruct((rows, width // 2), bf16),
            jax.ShapeDtypeStruct((rows, width // 2), f32),
        ]
    else:
        outs = [jax.ShapeDtypeStruct((rows, width), bf16)]
    *projected, part = pl.pallas_call(
        functools.partial(turn_kernel, pieces, len(outs)),
        out_shape=outs + [jax.ShapeDtypeStruct((rows, depth), f32)],
        in_specs=[SMEM, VMEM, VMEM, VMEM, VMEM, ANY],
        out_specs=[VMEM] * (len(outs) + 1),
        scratch_shapes=[
            ring(query_weight, pieces),
            pltpu.SemaphoreType.DMA((len(pieces), 2)),
        ],
        compiler_params=params(16),
        cost_estimate=cost(10),
        name="turn_stage",
    )(rank, modality, output_weight, attended, query_back, streamed(query_weight))
    return projected, part


def tie(passed, arrived):
    def kernel(passed_ref, arrived_ref, out_ref):
        del passed_ref, arrived_ref, out_ref

    return pl.pallas_call(
        kernel,
        out_shape=jax.ShapeDtypeStruct(passed.shape, passed.dtype),
        in_specs=[ANY, ANY],
        out_specs=ANY,
        input_output_aliases={0: 0},
        compiler_params=params(1),
        cost_estimate=cost(0.1),
        name="tie",
    )(passed, arrived)


def key_back_kernel(split, *refs):
    rank_ref, modality_ref, head_ref, raw_ref, inner_in_ref, part_ref, weight_ref = refs[:7]
    grad_refs = refs[7:-3]
    out_ref, back_ref, inner_ref = refs[-3:]
    base = pl.multiple_of((1 - rank_ref[0]) * out_ref.shape[1], HEAD_DIM) if split else 0
    image = column(modality_ref[...]) > 0.0
    blocks = raw_ref.shape[1] // HEAD_DIM
    scaling = jnp.where(image, head_ref[1, 1:2, :], head_ref[0, 1:2, :])
    inner = jnp.zeros((raw_ref.shape[0], 1), f32)
    for b in range(blocks):
        part = slice(b * HEAD_DIM, (b + 1) * HEAD_DIM)
        raw = raw_ref[:, part]
        upstream = grad_refs[0][:, part].astype(f32)
        for grad_ref in grad_refs[1:]:
            upstream += grad_ref[:, part].astype(f32)
        is_key = (rank_ref[0] * blocks + b) % 2 == 0
        normed_back = norm_back(raw, inverse_norm(raw), scaling, upstream)
        back = jnp.where(is_key, normed_back, upstream).astype(bf16)
        back_ref[:, part] = back
        inner += jnp.sum(back.astype(f32) * raw, axis=1, keepdims=True)
    inner_ref[...] = inner_in_ref[...] + row_of(inner)
    for start, size in chunks_of(out_ref.shape[1], HEAD_DIM):
        place = pl.ds(base + start, size)
        product = both_back(image, back_ref[...], weight_ref[:, place, :])
        out_ref[:, start : start + size] = (product + part_ref[:, place]).astype(bf16)


def key_back_stage(rank, modality, head_gain, raw, inner, part, weights, grads, split):
    _, depth, width = weights.shape
    rows = raw.shape[0]
    return pl.pallas_call(
        functools.partial(key_back_kernel, split),
        out_shape=[
            jax.ShapeDtypeStruct((rows, depth // 2 if split else depth), bf16),
            jax.ShapeDtypeStruct((rows, width), bf16),
            jax.ShapeDtypeStruct((1, rows), f32),
        ],
        in_specs=[SMEM] + [VMEM] * (6 + len(grads)),
        out_specs=[VMEM] * 3,
        compiler_params=params(6),
        cost_estimate=cost(2),
        name="key_back_stage",
    )(rank, modality, head_gain, raw, inner, part, weights, *grads)


def kept_kernel(rank_ref, modality_ref, part_ref, weight_ref, back_ref, out_ref):
    base = pl.multiple_of(rank_ref[0] * out_ref.shape[1], HEAD_DIM)
    image = column(modality_ref[...]) > 0.0
    for start, size in chunks_of(out_ref.shape[1], HEAD_DIM):
        place = pl.ds(base + start, size)
        product = both_back(image, back_ref[...], weight_ref[:, place, :])
        out_ref[:, start : start + size] = product + part_ref[:, place]


def kept_stage(rank, modality, part, weights, back):
    return pl.pallas_call(
        kept_kernel,
        out_shape=jax.ShapeDtypeStruct((back.shape[0], weights.shape[1] // 2), f32),
        in_specs=[SMEM] + [VMEM] * 4,
        out_specs=VMEM,
        compiler_params=params(6),
        cost_estimate=cost(2),
        name="kept_stage",
    )(rank, modality, part, weights, back)


def finish_kernel(backs, inners, total_width, *refs):
    rank_ref, modality_ref, gain_ref, factor_ref, inputs_ref = refs[:5]
    back_refs = refs[5 : 5 + backs]
    inner_refs = refs[5 + backs : 5 + backs + inners]
    rest = refs[5 + backs + inners :]
    width = inputs_ref.shape[1]
    copies = []

    def send(staged_ref, out_ref, sem, part):
        copy = pltpu.make_async_copy(staged_ref.at[:, part], out_ref.at[:, part], sem)
        copy.start()
        copies.append(copy)

    pieces = [slice(start, start + size) for start, size in chunks_of(width, 896)]
    if len(rest) == 7:
        kept_ref, other_ref, attention_ref, out_ref, staged, staged_attention, sems = rest
        for index, part in enumerate(pieces):
            whole = kept_ref[:, part] + other_ref[:, part].astype(f32)
            staged_attention[:, part] = whole.astype(bf16)
            send(staged_attention, attention_ref, sems.at[1, index], part)
    else:
        out_ref, staged, sems = rest
    image = column(modality_ref[...]) > 0.0
    factor = column(factor_ref[...])
    inner = inner_refs[0][...]
    for ref in inner_refs[1:]:
        inner += ref[...]
    inner_mean = factor * column(inner) * (1.0 / total_width)
    gathered = gain_ref.shape[1] != width
    for index, part in enumerate(pieces):
        columns = part
        if gathered:
            first = pl.multiple_of(rank_ref[0] * width, HEAD_DIM) + part.start
            columns = pl.ds(first, part.stop - part.start)
        back = back_refs[0][:, part].astype(f32)
        for ref in back_refs[1:]:
            back += ref[:, part].astype(f32)
        rows = inputs_ref[:, part].astype(f32)
        result = factor * (gain_of(image, gain_ref, columns) * back - rows * inner_mean)
        staged[:, part] = result.astype(bf16)
        send(staged, out_ref, sems.at[0, index], part)
    for copy in copies:
        copy.wait()


def finish(rank, total_width, modality, gain, factor, inputs, backs, inners, projected):
    shape = jax.ShapeDtypeStruct(inputs.shape, bf16)
    arrays = [modality, gain, factor, inputs, *backs, *inners, *projected]
    count = 2 if projected else 1
    pieces = len(chunks_of(inputs.shape[1], 896))
    return pl.pallas_call(
        functools.partial(finish_kernel, len(backs), len(inners), total_width),
        out_shape=[shape] * count,
        in_specs=[SMEM] + [VMEM] * len(arrays),
        out_specs=[ANY] * count,
        scratch_shapes=[pltpu.VMEM(inputs.shape, bf16)] * count
        + [pltpu.SemaphoreType.DMA((count, pieces))],
        compiler_params=params(6),
        cost_estimate=cost(1),
        name="finish",
    )(rank, *arrays)


def local(
    inputs,
    cotangent,
    norm_gain,
    head_gain,
    query_weight,
    key_weight,
    output_weight,
    modality,
    segments,
    block_order,
):
    tensor_rank = lax.axis_index("tensor")
    block_rank = lax.axis_index("seq")
    tensor_count = lax.axis_size("tensor")
    block_count = lax.axis_size("seq")
    local_rows, local_width = inputs.shape
    full_width = local_width * tensor_count
    split = tensor_count == 2
    swap = [(0, 1), (1, 0)]
    rank = tensor_rank.astype(jnp.int32).reshape(1)
    modality = modality.reshape(1, local_rows)
    segments = segments.reshape(block_count, local_rows)

    def spread(part):
        if split:
            return [part, lax.ppermute(part, "tensor", swap)]
        return [lax.all_gather(part, "tensor", axis=1, tiled=True)]

    def scatter_columns(part):
        return lax.psum_scatter(part, "tensor", scatter_dimension=1, tiled=True)

    if split:
        other = lax.ppermute(inputs, "tensor", swap)
        *early, key_held = early_stage(rank, modality, norm_gain, inputs, key_weight)
    else:
        other = lax.all_gather(inputs, "tensor", axis=1, tiled=True)
        early, key_held = [], key_weight
    memory, key_raw, scaled, row_factor = key_stage(
        rank, modality, norm_gain, head_gain, key_held, other, early
    )
    shared = tensor_count > KV_HEADS
    is_even = tensor_rank % 2 == 0
    pair_swap = [(i, i ^ 1) for i in range(tensor_count)]
    if shared:
        partner = lax.ppermute(memory, "tensor", pair_swap)
        memory = jnp.where(
            is_even,
            jnp.concatenate([memory, partner], 1),
            jnp.concatenate([partner, memory], 1),
        )
    memories = [memory]
    for step in seq_steps(block_count):
        memories.append(lax.ppermute(memory, "seq", seq_pairs(step, block_count)))

    query, query_raw, back_attended = middle_stage(
        rank,
        modality,
        head_gain,
        scaled,
        row_factor,
        output_weight,
        query_weight,
        spread(cotangent),
    )
    attended, query_back, inner, own_grad, *grads = attention_stage(
        block_rank.astype(jnp.int32).reshape(1),
        block_order,
        segments,
        modality,
        head_gain,
        query,
        query_raw,
        back_attended,
        memories,
    )
    incoming = [
        lax.ppermute(grad, "seq", inverted(seq_pairs(step, block_count)))
        for step, grad in zip(seq_steps(block_count), grads)
    ]

    projected, gradient_part = turn_stage(
        rank, modality, output_weight, attended, query_back, query_weight, split
    )
    if split:
        passed = tie(projected[0], incoming[0])
        projected = [projected[1], lax.ppermute(passed, "tensor", swap)]
    else:
        attention_out = scatter_columns(projected[0])
        projected = []

    if shared:
        total = own_grad + sum(grad.astype(f32) for grad in incoming)
        low, high = total[:, :HEAD_DIM], total[:, HEAD_DIM:]
        outgoing = jnp.where(is_even, high, low).astype(bf16)
        sums = [jnp.where(is_even, low, high), lax.ppermute(outgoing, "tensor", pair_swap)]
    else:
        sums = [own_grad, *incoming]
    sent, slice_back, inner = key_back_stage(
        rank,
        modality,
        head_gain,
        key_raw,
        inner,
        gradient_part,
        key_weight,
        sums,
        split,
    )
    if split:
        inners = [inner, lax.ppermute(inner, "tensor", swap)]
        other = lax.ppermute(sent, "tensor", swap)
        kept = kept_stage(rank, modality, gradient_part, key_weight, slice_back)
        backs = [kept, other]
        gain = norm_gain
    else:
        inners = [lax.psum(inner, "tensor")]
        backs = [scatter_columns(sent)]
        gain = lax.dynamic_slice_in_dim(norm_gain, tensor_rank * local_width, local_width, 1)
    results = finish(
        rank, full_width, modality, gain, row_factor, inputs, backs, inners, projected
    )
    if split:
        attention_out = results[0]
    return (attention_out, results[-1])


def solution(mesh):
    return jax.shard_map(
        local,
        mesh=mesh,
        in_specs=(
            P(("dp", "seq"), "tensor"),
            P(("dp", "seq"), "tensor"),
            P(),
            P(),
            P(None, None, "tensor"),
            P(None, None, "tensor"),
            P(None, "tensor", None),
            P(("dp", "seq")),
            P("dp"),
            P("dp"),
        ),
        out_specs=(P(("dp", "seq"), "tensor"), P(("dp", "seq"), "tensor")),
        check_vma=False,
    )
```

```python
import functools
import math

import jax
import jax.numpy as jnp
from jax import lax
from jax.experimental import pallas as pl
from jax.experimental.pallas import tpu as pltpu
from jax.sharding import PartitionSpec as P

KV_HEADS = 4
HEAD_DIM = 128
MIB = 1024 * 1024

epsilon = 1e-06
bf16 = jnp.bfloat16
f32 = jnp.float32
SMEM = pl.BlockSpec(memory_space=pltpu.SMEM)
VMEM = pl.BlockSpec(memory_space=pltpu.VMEM)
ANY = pl.BlockSpec(memory_space=pl.ANY)


def seq_pairs(step, count):
    if count & (count - 1) == 0:
        return [(i, i ^ step) for i in range(count)]
    return [(i, (i + step) % count) for i in range(count)]


def seq_steps(count):
    return sorted(range(1, count), key=lambda step: (step != count // 2, step))


def seq_source(rank, step, count):
    if count & (count - 1) == 0:
        return rank ^ step
    return (rank - step) % count


def inverted(pairs):
    return [(b, a) for a, b in pairs]


def tile_of(extent, most):
    best = HEAD_DIM
    for size in range(HEAD_DIM, min(extent, most) + 1, HEAD_DIM):
        if extent % size == 0:
            best = size
    return best


def dot_nt(a, b):
    return lax.dot_general(a, b, (((1,), (1,)), ((), ())), preferred_element_type=f32)


def dot_tn(a, b):
    return lax.dot_general(a, b, (((0,), (0,)), ((), ())), preferred_element_type=f32)


def column(row):
    count = row.shape[1]
    return jnp.broadcast_to(row.astype(f32), (count, count)).T[:, :1]


def row_of(col):
    count = col.shape[0]
    return jnp.broadcast_to(col, (count, count)).T[:1, :]


def inverse_norm(values):
    return lax.rsqrt(jnp.mean(values * values, axis=-1, keepdims=True) + epsilon)


def norm_back(values, factor, scaling, upstream):
    unit_rows = values * factor
    inner_mean = jnp.mean(scaling * upstream * unit_rows, axis=-1, keepdims=True)
    return factor * (scaling * upstream - unit_rows * inner_mean)


def streamed(weights):
    return pltpu.with_memory_space_constraint(weights, pltpu.HBM)


def params(mib):
    return pltpu.CompilerParams(vmem_limit_bytes=mib * MIB)


def cost(micros):
    return pl.CostEstimate(
        flops=int(micros * 1e9), bytes_accessed=int(micros * 2e6), transcendentals=0
    )


def in_order(rank, part_refs):
    if len(part_refs) == 1:
        return part_refs[0][...]
    own, other = part_refs[0][...], part_refs[1][...]
    first = rank == 0
    return jnp.concatenate([jnp.where(first, own, other), jnp.where(first, other, own)], axis=1)


def both_experts(image, rows, weights):
    zero = jnp.zeros_like(rows)
    masked = jnp.concatenate([jnp.where(image, zero, rows), jnp.where(image, rows, zero)], axis=1)
    flat = weights.reshape(2 * weights.shape[1], weights.shape[2])
    return jnp.dot(masked, flat, preferred_element_type=f32)


def both_back(image, rows, weights):
    return jnp.where(image, dot_nt(rows, weights[1]), dot_nt(rows, weights[0]))


def chunks_of(extent, most):
    size = tile_of(extent, most)
    return [(start, size) for start in range(0, extent, size)]


AHEAD = 4


def copies_of(source_ref, target_ref, sem_ref, pieces, base=0, slots=0):
    copies = []
    for index, (start, size) in enumerate(pieces):
        pair = []
        for e in range(2):
            if slots:
                target = target_ref.at[index % slots, e]
            else:
                target = target_ref.at[e, pl.ds(start, size), :]
            source = source_ref.at[e, pl.ds(base + start, size), :]
            pair.append(pltpu.make_async_copy(source, target, sem_ref.at[index, e]))
        copies.append(pair)
    return copies


def begin(copies, index):
    if index < len(copies):
        for copy in copies[index]:
            copy.start()


def begin_first(copies):
    for index in range(AHEAD):
        begin(copies, index)


def arrive(copies, index):
    for copy in copies[index]:
        copy.wait()


def ring(weights, pieces):
    return pltpu.VMEM((AHEAD, 2, pieces[0][1], weights.shape[2]), weights.dtype)


def gain_of(image, gain_ref, columns):
    return jnp.where(image, gain_ref[1:2, columns], gain_ref[0:1, columns])


def early_kernel(pieces, *refs):
    rank_ref, weight_ref = refs[:2]
    given_refs, (scaled_ref, squares_ref, total_ref, held_ref) = refs[2:5], refs[5:9]
    own_held, sems, held_sems, given_sems = refs[9:13]
    modality_ref, gain_ref, own_ref = refs[13:]
    given = [
        pltpu.make_async_copy(source, target, given_sems.at[index])
        for index, (source, target) in enumerate(zip(given_refs, refs[13:]))
    ]
    for copy in given:
        copy.start()
    extent = own_ref.shape[1]
    base = pl.multiple_of(rank_ref[0] * extent, HEAD_DIM)
    away = pl.multiple_of((1 - rank_ref[0]) * extent, HEAD_DIM)
    copies = copies_of(weight_ref, own_held, sems, pieces, base)
    copies += copies_of(weight_ref, held_ref, held_sems, pieces, away)
    for index in range(len(pieces)):
        begin(copies, index)
    for copy in given:
        copy.wait()
    image = column(modality_ref[...]) > 0.0
    rows = own_ref[...].astype(f32)
    squares_ref[...] = row_of(jnp.sum(rows * rows, axis=1, keepdims=True))
    scaled_ref[...] = (rows * gain_of(image, gain_ref, pl.ds(base, extent))).astype(bf16)
    for index in range(len(pieces), len(copies)):
        begin(copies, index)
    for index, (start, size) in enumerate(pieces):
        arrive(copies, index)
        part = slice(start, start + size)
        product = both_experts(image, scaled_ref[:, part], own_held[:, part, :])
        if index == 0:
            total_ref[...] = product
        else:
            total_ref[...] += product
    for index in range(len(pieces), len(copies)):
        arrive(copies, index)


def early_stage(rank, modality, norm_gain, own, weights):
    _, depth, width = weights.shape
    rows, extent = own.shape
    pieces = chunks_of(extent, 896)
    half_weights = (2, extent, width)
    given = [modality, norm_gain, own]
    return pl.pallas_call(
        functools.partial(early_kernel, pieces),
        out_shape=[
            jax.ShapeDtypeStruct((rows, extent), bf16),
            jax.ShapeDtypeStruct((1, rows), f32),
            jax.ShapeDtypeStruct((rows, width), f32),
            pltpu.VMEM(half_weights, bf16),
        ],
        in_specs=[SMEM] + [ANY] * 4,
        out_specs=[VMEM] * 4,
        scratch_shapes=[
            pltpu.VMEM(half_weights, bf16),
            pltpu.SemaphoreType.DMA((len(pieces), 2)),
            pltpu.SemaphoreType.DMA((len(pieces), 2)),
            pltpu.SemaphoreType.DMA((len(given),)),
        ]
        + [pltpu.VMEM(g.shape, g.dtype) for g in given],
        compiler_params=params(8),
        cost_estimate=cost(0.2),
        name="early_stage",
    )(rank, streamed(weights), *(streamed(g) for g in given))


def key_kernel(split, *refs):
    rank_ref, modality_ref, gain_ref, head_ref, weight_ref, rows_ref = refs[:6]
    memory_ref, raw_ref, scaled_ref, factor_ref = refs[-4:]
    image = column(modality_ref[...]) > 0.0
    rows = rows_ref[...].astype(f32)
    extent = rows.shape[1]
    squares = jnp.sum(rows * rows, axis=1, keepdims=True)
    if split:
        own_ref, own_squares_ref, own_total_ref = refs[6:9]
        squares += column(own_squares_ref[...])
        columns = pl.ds(pl.multiple_of((1 - rank_ref[0]) * extent, HEAD_DIM), extent)
    else:
        columns = slice(0, extent)
    scaled = (rows * gain_of(image, gain_ref, columns)).astype(bf16)
    total = both_experts(image, scaled, weight_ref[...])
    factor = lax.rsqrt(squares * (1.0 / scaled_ref.shape[1]) + epsilon)
    factor_ref[...] = row_of(factor)
    if split:
        total += own_total_ref[...]
        first = rank_ref[0] == 0
        own = own_ref[...]
        scaled_ref[:, :extent] = jnp.where(first, own, scaled)
        scaled_ref[:, extent:] = jnp.where(first, scaled, own)
    else:
        scaled_ref[...] = scaled
    raw_ref[...] = total * factor
    blocks = raw_ref.shape[1] // HEAD_DIM
    scaling = jnp.where(image, head_ref[1, 1:2, :], head_ref[0, 1:2, :])
    for b in range(blocks):
        part = slice(b * HEAD_DIM, (b + 1) * HEAD_DIM)
        raw = raw_ref[:, part]
        normed = raw * inverse_norm(raw) * scaling
        is_key = (rank_ref[0] * blocks + b) % 2 == 0
        memory_ref[:, part] = jnp.where(is_key, normed, raw).astype(bf16)


def key_stage(rank, modality, norm_gain, head_gain, weights, part, early):
    width = weights.shape[2]
    rows = part.shape[0]
    depth = norm_gain.shape[1]
    return pl.pallas_call(
        functools.partial(key_kernel, len(early) > 0),
        out_shape=[
            jax.ShapeDtypeStruct((rows, width), bf16),
            jax.ShapeDtypeStruct((rows, width), f32),
            jax.ShapeDtypeStruct((rows, depth), bf16),
            jax.ShapeDtypeStruct((1, rows), f32),
        ],
        in_specs=[SMEM] + [VMEM] * (5 + len(early)),
        out_specs=[VMEM] * 4,
        compiler_params=params(8),
        cost_estimate=cost(10),
        name="key_stage",
    )(rank, modality, norm_gain, head_gain, weights, part, *early)


def middle_kernel(count, pieces, *refs):
    rank_ref, modality_ref, head_ref, scaled_ref, factor_ref, output_ref = refs[:6]
    query_weight_ref = refs[6]
    part_refs = refs[7 : 7 + count]
    query_ref, raw_ref, back_ref, slots, sems = refs[7 + count :]
    copies = copies_of(query_weight_ref, slots, sems, pieces, slots=AHEAD)
    begin_first(copies)
    image = column(modality_ref[...]) > 0.0
    cotangent = in_order(rank_ref[0], part_refs)
    tiles = chunks_of(output_ref.shape[1], HEAD_DIM)
    done = 0
    for turn, (start, size) in enumerate(tiles, 1):
        part = slice(start, start + size)
        back_ref[:, part] = both_back(image, cotangent, output_ref[:, part, :]).astype(bf16)
        until = len(pieces) * turn // len(tiles)
        for index in range(done, until):
            arrive(copies, index)
            start, size = pieces[index]
            part = slice(start, start + size)
            product = both_experts(image, scaled_ref[:, part], slots[index % AHEAD])
            if index == 0:
                raw_ref[...] = product
            else:
                raw_ref[...] += product
            begin(copies, index + AHEAD)
        done = until
    factor = column(factor_ref[...])
    scaling = jnp.where(image, head_ref[1, 0:1, :], head_ref[0, 0:1, :])
    for h in range(raw_ref.shape[1] // HEAD_DIM):
        part = slice(h * HEAD_DIM, (h + 1) * HEAD_DIM)
        raw = raw_ref[:, part] * factor
        raw_ref[:, part] = raw
        query_ref[:, part] = (raw * inverse_norm(raw) * scaling).astype(bf16)


def middle_stage(rank, modality, head_gain, scaled, factor, output_weight, query_weight, parts):
    rows = scaled.shape[0]
    width = query_weight.shape[2]
    pieces = chunks_of(query_weight.shape[1], 512)
    return pl.pallas_call(
        functools.partial(middle_kernel, len(parts), pieces),
        out_shape=[
            jax.ShapeDtypeStruct((rows, width), bf16),
            jax.ShapeDtypeStruct((rows, width), f32),
            jax.ShapeDtypeStruct((rows, width), bf16),
        ],
        in_specs=[SMEM, VMEM, VMEM, VMEM, VMEM, VMEM, ANY] + [VMEM] * len(parts),
        out_specs=[VMEM] * 3,
        scratch_shapes=[
            ring(query_weight, pieces),
            pltpu.SemaphoreType.DMA((len(pieces), 2)),
        ],
        compiler_params=params(14),
        cost_estimate=cost(8),
        name="middle_stage",
    )(
        rank,
        modality,
        head_gain,
        scaled,
        factor,
        output_weight,
        streamed(query_weight),
        *parts,
    )


def attention_kernel(blocks, pairs, per_group, *refs):
    place_ref, order_ref, segments_ref, modality_ref, head_ref = refs[:5]
    query_ref, raw_ref, back_ref = refs[5:8]
    memory_refs = refs[8 : 8 + blocks]
    attended_ref, query_back_ref, inner_ref = refs[8 + blocks : 11 + blocks]
    grad_refs = refs[11 + blocks :]
    rows = query_ref.shape[0]
    scale = 1.0 / math.sqrt(HEAD_DIM)
    lines = [
        segments_ref[pl.ds(order_ref[seq_source(place_ref[0], step, blocks)], 1), :]
        for step in [0, *seq_steps(blocks)]
    ]
    key_segments = jnp.concatenate(lines, axis=1).astype(f32)
    visible = key_segments <= column(lines[0])
    image = column(modality_ref[...]) > 0.0
    scaling = jnp.where(image, head_ref[1, 0:1, :], head_ref[0, 0:1, :])
    inner = jnp.zeros((rows, 1), f32)
    for pair in range(pairs):
        columns = [
            slice(h * HEAD_DIM, (h + 1) * HEAD_DIM)
            for h in range(pair * per_group, (pair + 1) * per_group)
        ]
        parts = [slice(h * rows, (h + 1) * rows) for h in range(per_group)]
        keys = slice(2 * pair * HEAD_DIM, (2 * pair + 1) * HEAD_DIM)
        values = slice((2 * pair + 1) * HEAD_DIM, (2 * pair + 2) * HEAD_DIM)
        query = jnp.concatenate([query_ref[:, c] for c in columns], axis=0)
        back = jnp.concatenate([back_ref[:, c] for c in columns], axis=0)
        key = jnp.concatenate([m[:, keys] for m in memory_refs], axis=0)
        value = jnp.concatenate([m[:, values] for m in memory_refs], axis=0)
        scores = dot_nt(query, key) * (scale * math.log2(math.e))
        weights = jnp.concatenate(
            [jnp.where(visible, jnp.exp2(scores[p]), 0.0).astype(bf16) for p in parts], axis=0
        )
        weights32 = weights.astype(f32)
        inverse = 1.0 / jnp.sum(weights32, axis=1, keepdims=True)
        numerator = jnp.dot(weights, value, preferred_element_type=f32)
        attended = (numerator * inverse).astype(bf16)
        offset = jnp.sum(back.astype(f32) * attended.astype(f32), axis=1, keepdims=True)
        probability = (weights32 * inverse).astype(bf16)
        back_prob = dot_nt(back, value)
        back_score = (probability.astype(f32) * (back_prob - offset)).astype(bf16)
        back_query = jnp.dot(back_score, key, preferred_element_type=f32) * scale
        back_key = dot_tn(back_score, query) * scale
        back_value = dot_tn(probability, back)
        for b, grad_ref in enumerate(grad_refs):
            part = slice(b * rows, (b + 1) * rows)
            grad_ref[:, keys] = back_key[part].astype(grad_ref.dtype)
            grad_ref[:, values] = back_value[part].astype(grad_ref.dtype)
        for part, place in zip(parts, columns):
            attended_ref[:, place] = attended[part]
            raw = raw_ref[:, place]
            query_back = norm_back(raw, inverse_norm(raw), scaling, back_query[part]).astype(bf16)
            query_back_ref[:, place] = query_back
            inner += jnp.sum(query_back.astype(f32) * raw, axis=1, keepdims=True)
    inner_ref[...] = row_of(inner)


def attention_stage(place, order, segments, modality, head_gain, query, raw, back, memories):
    rows, width = query.shape
    blocks = len(memories)
    pairs = memories[0].shape[1] // (2 * HEAD_DIM)
    per_group = width // HEAD_DIM // pairs
    outs = [
        jax.ShapeDtypeStruct((rows, width), bf16),
        jax.ShapeDtypeStruct((rows, width), bf16),
        jax.ShapeDtypeStruct((1, rows), f32),
    ] + [
        jax.ShapeDtypeStruct((rows, pairs * 2 * HEAD_DIM), f32 if b == 0 else bf16)
        for b in range(blocks)
    ]
    return pl.pallas_call(
        functools.partial(attention_kernel, blocks, pairs, per_group),
        out_shape=outs,
        in_specs=[SMEM, SMEM] + [VMEM] * (6 + blocks),
        out_specs=[VMEM] * (3 + blocks),
        compiler_params=params(12),
        cost_estimate=cost(4),
        name="attention_stage",
    )(place, order, segments, modality, head_gain, query, raw, back, *memories)


def turn_kernel(pieces, outputs, *refs):
    rank_ref, modality_ref, output_ref, attended_ref, back_ref, query_ref = refs[:6]
    out_refs = refs[6 : 6 + outputs]
    part_ref, slots, sems = refs[6 + outputs :]
    copies = copies_of(query_ref, slots, sems, pieces, slots=AHEAD)
    begin_first(copies)
    image = column(modality_ref[...]) > 0.0
    attended = attended_ref[...]
    extent = output_ref.shape[2] // 2

    def project(rank):
        sent_ref, kept_ref = out_refs
        for start, size in chunks_of(extent, 896):
            part = slice(start, start + size)
            first = (1 - rank) * extent + start
            product = both_experts(image, attended, output_ref[:, :, first : first + size])
            sent_ref[:, part] = product.astype(bf16)
            first = rank * extent + start
            product = both_experts(image, attended, output_ref[:, :, first : first + size])
            kept_ref[:, part] = product

    if outputs == 1:
        out_refs[0][...] = both_experts(image, attended, output_ref[...]).astype(bf16)
    else:
        for rank in range(2):
            pl.when(rank_ref[0] == rank)(functools.partial(project, rank))
    for index, (start, size) in enumerate(pieces):
        arrive(copies, index)
        for inside, tile in chunks_of(size, HEAD_DIM):
            weights = slots[index % AHEAD, :, inside : inside + tile, :]
            part = slice(start + inside, start + inside + tile)
            part_ref[:, part] = both_back(image, back_ref[...], weights)
        begin(copies, index + AHEAD)


def turn_stage(rank, modality, output_weight, attended, query_back, query_weight, split):
    depth = query_weight.shape[1]
    width = output_weight.shape[2]
    rows = attended.shape[0]
    pieces = chunks_of(depth, 512)
    if split:
        outs = [
            jax.ShapeDtypeStruct((rows, width // 2), bf16),
            jax.ShapeDtypeStruct((rows, width // 2), f32),
        ]
    else:
        outs = [jax.ShapeDtypeStruct((rows, width), bf16)]
    *projected, part = pl.pallas_call(
        functools.partial(turn_kernel, pieces, len(outs)),
        out_shape=outs + [jax.ShapeDtypeStruct((rows, depth), f32)],
        in_specs=[SMEM, VMEM, VMEM, VMEM, VMEM, ANY],
        out_specs=[VMEM] * (len(outs) + 1),
        scratch_shapes=[
            ring(query_weight, pieces),
            pltpu.SemaphoreType.DMA((len(pieces), 2)),
        ],
        compiler_params=params(16),
        cost_estimate=cost(10),
        name="turn_stage",
    )(rank, modality, output_weight, attended, query_back, streamed(query_weight))
    return projected, part


def tie(passed, arrived):
    def kernel(passed_ref, arrived_ref, out_ref):
        del passed_ref, arrived_ref, out_ref

    return pl.pallas_call(
        kernel,
        out_shape=jax.ShapeDtypeStruct(passed.shape, passed.dtype),
        in_specs=[ANY, ANY],
        out_specs=ANY,
        input_output_aliases={0: 0},
        compiler_params=params(1),
        cost_estimate=cost(0.1),
        name="tie",
    )(passed, arrived)


def key_back_kernel(split, *refs):
    rank_ref, modality_ref, head_ref, raw_ref, inner_in_ref, part_ref, weight_ref = refs[:7]
    grad_refs = refs[7:-3]
    out_ref, back_ref, inner_ref = refs[-3:]
    base = pl.multiple_of((1 - rank_ref[0]) * out_ref.shape[1], HEAD_DIM) if split else 0
    image = column(modality_ref[...]) > 0.0
    blocks = raw_ref.shape[1] // HEAD_DIM
    scaling = jnp.where(image, head_ref[1, 1:2, :], head_ref[0, 1:2, :])
    inner = jnp.zeros((raw_ref.shape[0], 1), f32)
    for b in range(blocks):
        part = slice(b * HEAD_DIM, (b + 1) * HEAD_DIM)
        raw = raw_ref[:, part]
        upstream = grad_refs[0][:, part].astype(f32)
        for grad_ref in grad_refs[1:]:
            upstream += grad_ref[:, part].astype(f32)
        is_key = (rank_ref[0] * blocks + b) % 2 == 0
        normed_back = norm_back(raw, inverse_norm(raw), scaling, upstream)
        back = jnp.where(is_key, normed_back, upstream).astype(bf16)
        back_ref[:, part] = back
        inner += jnp.sum(back.astype(f32) * raw, axis=1, keepdims=True)
    inner_ref[...] = inner_in_ref[...] + row_of(inner)
    for start, size in chunks_of(out_ref.shape[1], HEAD_DIM):
        place = pl.ds(base + start, size)
        product = both_back(image, back_ref[...], weight_ref[:, place, :])
        out_ref[:, start : start + size] = (product + part_ref[:, place]).astype(bf16)


def key_back_stage(rank, modality, head_gain, raw, inner, part, weights, grads, split):
    _, depth, width = weights.shape
    rows = raw.shape[0]
    return pl.pallas_call(
        functools.partial(key_back_kernel, split),
        out_shape=[
            jax.ShapeDtypeStruct((rows, depth // 2 if split else depth), bf16),
            jax.ShapeDtypeStruct((rows, width), bf16),
            jax.ShapeDtypeStruct((1, rows), f32),
        ],
        in_specs=[SMEM] + [VMEM] * (6 + len(grads)),
        out_specs=[VMEM] * 3,
        compiler_params=params(6),
        cost_estimate=cost(2),
        name="key_back_stage",
    )(rank, modality, head_gain, raw, inner, part, weights, *grads)


def kept_kernel(rank_ref, modality_ref, part_ref, weight_ref, back_ref, out_ref):
    base = pl.multiple_of(rank_ref[0] * out_ref.shape[1], HEAD_DIM)
    image = column(modality_ref[...]) > 0.0
    for start, size in chunks_of(out_ref.shape[1], HEAD_DIM):
        place = pl.ds(base + start, size)
        product = both_back(image, back_ref[...], weight_ref[:, place, :])
        out_ref[:, start : start + size] = product + part_ref[:, place]


def kept_stage(rank, modality, part, weights, back):
    return pl.pallas_call(
        kept_kernel,
        out_shape=jax.ShapeDtypeStruct((back.shape[0], weights.shape[1] // 2), f32),
        in_specs=[SMEM] + [VMEM] * 4,
        out_specs=VMEM,
        compiler_params=params(6),
        cost_estimate=cost(2),
        name="kept_stage",
    )(rank, modality, part, weights, back)


def finish_kernel(backs, inners, total_width, *refs):
    rank_ref, modality_ref, gain_ref, factor_ref, inputs_ref = refs[:5]
    back_refs = refs[5 : 5 + backs]
    inner_refs = refs[5 + backs : 5 + backs + inners]
    rest = refs[5 + backs + inners :]
    width = inputs_ref.shape[1]
    copies = []

    def send(staged_ref, out_ref, sem, part):
        copy = pltpu.make_async_copy(staged_ref.at[:, part], out_ref.at[:, part], sem)
        copy.start()
        copies.append(copy)

    pieces = [slice(start, start + size) for start, size in chunks_of(width, 896)]
    if len(rest) == 7:
        kept_ref, other_ref, attention_ref, out_ref, staged, staged_attention, sems = rest
        for index, part in enumerate(pieces):
            whole = kept_ref[:, part] + other_ref[:, part].astype(f32)
            staged_attention[:, part] = whole.astype(bf16)
            send(staged_attention, attention_ref, sems.at[1, index], part)
    else:
        out_ref, staged, sems = rest
    image = column(modality_ref[...]) > 0.0
    factor = column(factor_ref[...])
    inner = inner_refs[0][...]
    for ref in inner_refs[1:]:
        inner += ref[...]
    inner_mean = factor * column(inner) * (1.0 / total_width)
    gathered = gain_ref.shape[1] != width
    for index, part in enumerate(pieces):
        columns = part
        if gathered:
            first = pl.multiple_of(rank_ref[0] * width, HEAD_DIM) + part.start
            columns = pl.ds(first, part.stop - part.start)
        back = back_refs[0][:, part].astype(f32)
        for ref in back_refs[1:]:
            back += ref[:, part].astype(f32)
        rows = inputs_ref[:, part].astype(f32)
        result = factor * (gain_of(image, gain_ref, columns) * back - rows * inner_mean)
        staged[:, part] = result.astype(bf16)
        send(staged, out_ref, sems.at[0, index], part)
    for copy in copies:
        copy.wait()


def finish(rank, total_width, modality, gain, factor, inputs, backs, inners, projected):
    shape = jax.ShapeDtypeStruct(inputs.shape, bf16)
    arrays = [modality, gain, factor, inputs, *backs, *inners, *projected]
    count = 2 if projected else 1
    pieces = len(chunks_of(inputs.shape[1], 896))
    return pl.pallas_call(
        functools.partial(finish_kernel, len(backs), len(inners), total_width),
        out_shape=[shape] * count,
        in_specs=[SMEM] + [VMEM] * len(arrays),
        out_specs=[ANY] * count,
        scratch_shapes=[pltpu.VMEM(inputs.shape, bf16)] * count
        + [pltpu.SemaphoreType.DMA((count, pieces))],
        compiler_params=params(6),
        cost_estimate=cost(1),
        name="finish",
    )(rank, *arrays)


def local(
    inputs,
    cotangent,
    norm_gain,
    head_gain,
    query_weight,
    key_weight,
    output_weight,
    modality,
    segments,
    block_order,
):
    tensor_rank = lax.axis_index("tensor")
    block_rank = lax.axis_index("seq")
    tensor_count = lax.axis_size("tensor")
    block_count = lax.axis_size("seq")
    local_rows, local_width = inputs.shape
    full_width = local_width * tensor_count
    split = tensor_count == 2
    swap = [(0, 1), (1, 0)]
    rank = tensor_rank.astype(jnp.int32).reshape(1)
    modality = modality.reshape(1, local_rows)
    segments = segments.reshape(block_count, local_rows)

    def spread(part):
        if split:
            return [part, lax.ppermute(part, "tensor", swap)]
        return [lax.all_gather(part, "tensor", axis=1, tiled=True)]

    def scatter_columns(part):
        return lax.psum_scatter(part, "tensor", scatter_dimension=1, tiled=True)

    if split:
        other = lax.ppermute(inputs, "tensor", swap)
        *early, key_held = early_stage(rank, modality, norm_gain, inputs, key_weight)
    else:
        other = lax.all_gather(inputs, "tensor", axis=1, tiled=True)
        early, key_held = [], key_weight
    memory, key_raw, scaled, row_factor = key_stage(
        rank, modality, norm_gain, head_gain, key_held, other, early
    )
    shared = tensor_count > KV_HEADS
    is_even = tensor_rank % 2 == 0
    pair_swap = [(i, i ^ 1) for i in range(tensor_count)]
    if shared:
        partner = lax.ppermute(memory, "tensor", pair_swap)
        memory = jnp.where(
            is_even,
            jnp.concatenate([memory, partner], 1),
            jnp.concatenate([partner, memory], 1),
        )
    memories = [memory]
    for step in seq_steps(block_count):
        memories.append(lax.ppermute(memory, "seq", seq_pairs(step, block_count)))

    query, query_raw, back_attended = middle_stage(
        rank,
        modality,
        head_gain,
        scaled,
        row_factor,
        output_weight,
        query_weight,
        spread(cotangent),
    )
    attended, query_back, inner, own_grad, *grads = attention_stage(
        block_rank.astype(jnp.int32).reshape(1),
        block_order,
        segments,
        modality,
        head_gain,
        query,
        query_raw,
        back_attended,
        memories,
    )
    incoming = [
        lax.ppermute(grad, "seq", inverted(seq_pairs(step, block_count)))
        for step, grad in zip(seq_steps(block_count), grads)
    ]

    projected, gradient_part = turn_stage(
        rank, modality, output_weight, attended, query_back, query_weight, split
    )
    if split:
        passed = tie(projected[0], incoming[0])
        projected = [projected[1], lax.ppermute(passed, "tensor", swap)]
    else:
        attention_out = scatter_columns(projected[0])
        projected = []

    if shared:
        total = own_grad + sum(grad.astype(f32) for grad in incoming)
        low, high = total[:, :HEAD_DIM], total[:, HEAD_DIM:]
        outgoing = jnp.where(is_even, high, low).astype(bf16)
        sums = [jnp.where(is_even, low, high), lax.ppermute(outgoing, "tensor", pair_swap)]
    else:
        sums = [own_grad, *incoming]
    sent, slice_back, inner = key_back_stage(
        rank,
        modality,
        head_gain,
        key_raw,
        inner,
        gradient_part,
        key_weight,
        sums,
        split,
    )
    if split:
        inners = [inner, lax.ppermute(inner, "tensor", swap)]
        other = lax.ppermute(sent, "tensor", swap)
        kept = kept_stage(rank, modality, gradient_part, key_weight, slice_back)
        backs = [kept, other]
        gain = norm_gain
    else:
        inners = [lax.psum(inner, "tensor")]
        backs = [scatter_columns(sent)]
        gain = lax.dynamic_slice_in_dim(norm_gain, tensor_rank * local_width, local_width, 1)
    results = finish(
        rank, full_width, modality, gain, row_factor, inputs, backs, inners, projected
    )
    if split:
        attention_out = results[0]
    return (attention_out, results[-1])


def solution(mesh):
    return jax.shard_map(
        local,
        mesh=mesh,
        in_specs=(
            P(("dp", "seq"), "tensor"),
            P(("dp", "seq"), "tensor"),
            P(),
            P(),
            P(None, None, "tensor"),
            P(None, None, "tensor"),
            P(None, "tensor", None),
            P(("dp", "seq")),
            P("dp"),
            P("dp"),
        ),
        out_specs=(P(("dp", "seq"), "tensor"), P(("dp", "seq"), "tensor")),
        check_vma=False,
    )
```

```python
import functools
import math

import jax
import jax.numpy as jnp
from jax import lax
from jax.experimental import pallas as pl
from jax.experimental.pallas import tpu as pltpu
from jax.sharding import PartitionSpec as P

KV_HEADS = 4
HEAD_DIM = 128
MIB = 1024 * 1024

epsilon = 1e-06
bf16 = jnp.bfloat16
f32 = jnp.float32
SMEM = pl.BlockSpec(memory_space=pltpu.SMEM)
VMEM = pl.BlockSpec(memory_space=pltpu.VMEM)
ANY = pl.BlockSpec(memory_space=pl.ANY)


def seq_pairs(step, count):
    if count & (count - 1) == 0:
        return [(i, i ^ step) for i in range(count)]
    return [(i, (i + step) % count) for i in range(count)]


def seq_steps(count):
    return sorted(range(1, count), key=lambda step: (step != count // 2, step))


def seq_source(rank, step, count):
    if count & (count - 1) == 0:
        return rank ^ step
    return (rank - step) % count


def inverted(pairs):
    return [(b, a) for a, b in pairs]


def tile_of(extent, most):
    best = HEAD_DIM
    for size in range(HEAD_DIM, min(extent, most) + 1, HEAD_DIM):
        if extent % size == 0:
            best = size
    return best


def dot_nt(a, b):
    return lax.dot_general(a, b, (((1,), (1,)), ((), ())), preferred_element_type=f32)


def dot_tn(a, b):
    return lax.dot_general(a, b, (((0,), (0,)), ((), ())), preferred_element_type=f32)


def column(row):
    count = row.shape[1]
    return jnp.broadcast_to(row.astype(f32), (count, count)).T[:, :1]


def row_of(col):
    count = col.shape[0]
    return jnp.broadcast_to(col, (count, count)).T[:1, :]


def inverse_norm(values):
    return lax.rsqrt(jnp.mean(values * values, axis=-1, keepdims=True) + epsilon)


def norm_back(values, factor, scaling, upstream):
    unit_rows = values * factor
    inner_mean = jnp.mean(scaling * upstream * unit_rows, axis=-1, keepdims=True)
    return factor * (scaling * upstream - unit_rows * inner_mean)


def streamed(weights):
    return pltpu.with_memory_space_constraint(weights, pltpu.HBM)


def params(mib):
    return pltpu.CompilerParams(vmem_limit_bytes=mib * MIB)


def cost(micros):
    return pl.CostEstimate(
        flops=int(micros * 1e9), bytes_accessed=int(micros * 2e6), transcendentals=0
    )


def in_order(rank, part_refs):
    if len(part_refs) == 1:
        return part_refs[0][...]
    own, other = part_refs[0][...], part_refs[1][...]
    first = rank == 0
    return jnp.concatenate([jnp.where(first, own, other), jnp.where(first, other, own)], axis=1)


def both_experts(image, rows, weights):
    zero = jnp.zeros_like(rows)
    masked = jnp.concatenate([jnp.where(image, zero, rows), jnp.where(image, rows, zero)], axis=1)
    flat = weights.reshape(2 * weights.shape[1], weights.shape[2])
    return jnp.dot(masked, flat, preferred_element_type=f32)


def both_back(image, rows, weights):
    return jnp.where(image, dot_nt(rows, weights[1]), dot_nt(rows, weights[0]))


def chunks_of(extent, most):
    size = tile_of(extent, most)
    return [(start, size) for start in range(0, extent, size)]


AHEAD = 4


def copies_of(source_ref, target_ref, sem_ref, pieces, base=0, slots=0):
    copies = []
    for index, (start, size) in enumerate(pieces):
        pair = []
        for e in range(2):
            if slots:
                target = target_ref.at[index % slots, e]
            else:
                target = target_ref.at[e, pl.ds(start, size), :]
            source = source_ref.at[e, pl.ds(base + start, size), :]
            pair.append(pltpu.make_async_copy(source, target, sem_ref.at[index, e]))
        copies.append(pair)
    return copies


def begin(copies, index):
    if index < len(copies):
        for copy in copies[index]:
            copy.start()


def begin_first(copies):
    for index in range(AHEAD):
        begin(copies, index)


def arrive(copies, index):
    for copy in copies[index]:
        copy.wait()


def ring(weights, pieces):
    return pltpu.VMEM((AHEAD, 2, pieces[0][1], weights.shape[2]), weights.dtype)


def resident(weights):
    return pltpu.VMEM(weights.shape, weights.dtype)


def fetch_kernel(pieces, weight_ref, held_ref, sem_ref):
    copies = copies_of(weight_ref, held_ref, sem_ref, pieces)
    for pair in copies:
        for copy in pair:
            copy.start()
    for pair in copies:
        for copy in pair:
            copy.wait()


def fetch(weights):
    pieces = chunks_of(weights.shape[1], 896)
    return pl.pallas_call(
        functools.partial(fetch_kernel, pieces),
        out_shape=resident(weights),
        in_specs=[ANY],
        out_specs=VMEM,
        scratch_shapes=[pltpu.SemaphoreType.DMA((len(pieces), 2))],
        compiler_params=params(1),
        cost_estimate=cost(0.2),
        name="fetch",
    )(streamed(weights))


def gain_of(image, gain_ref, columns):
    return jnp.where(image, gain_ref[1:2, columns], gain_ref[0:1, columns])


def key_kernel(count, *refs):
    rank_ref, modality_ref, gain_ref, head_ref, weight_ref = refs[:5]
    part_refs = refs[5 : 5 + count]
    memory_ref, raw_ref, normed_ref, factor_ref = refs[5 + count :]
    image = column(modality_ref[...]) > 0.0
    rows = in_order(rank_ref[0], part_refs).astype(f32)
    factor = inverse_norm(rows)
    scaling = jnp.where(image, gain_ref[1:2, :], gain_ref[0:1, :])
    normed_ref[...] = (rows * factor * scaling).astype(bf16)
    factor_ref[...] = row_of(factor)
    for index, (start, size) in enumerate(chunks_of(normed_ref.shape[1], 1792)):
        part = slice(start, start + size)
        product = both_experts(image, normed_ref[:, part], weight_ref[:, part, :])
        if index == 0:
            raw_ref[...] = product
        else:
            raw_ref[...] += product
    blocks = raw_ref.shape[1] // HEAD_DIM
    scaling = jnp.where(image, head_ref[1, 1:2, :], head_ref[0, 1:2, :])
    for b in range(blocks):
        part = slice(b * HEAD_DIM, (b + 1) * HEAD_DIM)
        raw = raw_ref[:, part]
        normed = raw * inverse_norm(raw) * scaling
        is_key = (rank_ref[0] * blocks + b) % 2 == 0
        memory_ref[:, part] = jnp.where(is_key, normed, raw).astype(bf16)


def key_stage(rank, modality, norm_gain, head_gain, weights, parts):
    _, depth, width = weights.shape
    rows = parts[0].shape[0]
    return pl.pallas_call(
        functools.partial(key_kernel, len(parts)),
        out_shape=[
            jax.ShapeDtypeStruct((rows, width), bf16),
            jax.ShapeDtypeStruct((rows, width), f32),
            jax.ShapeDtypeStruct((rows, depth), bf16),
            jax.ShapeDtypeStruct((1, rows), f32),
        ],
        in_specs=[SMEM] + [VMEM] * (4 + len(parts)),
        out_specs=[VMEM] * 4,
        compiler_params=params(8),
        cost_estimate=cost(10),
        name="key_stage",
    )(rank, modality, norm_gain, head_gain, weights, *parts)


def middle_kernel(count, pieces, *refs):
    rank_ref, modality_ref, head_ref, normed_ref, output_ref, query_weight_ref = refs[:6]
    part_refs = refs[6 : 6 + count]
    query_ref, raw_ref, back_ref, slots, sems = refs[6 + count :]
    copies = copies_of(query_weight_ref, slots, sems, pieces, slots=AHEAD)
    begin_first(copies)
    image = column(modality_ref[...]) > 0.0
    cotangent = in_order(rank_ref[0], part_refs)
    tiles = chunks_of(output_ref.shape[1], HEAD_DIM)
    done = 0
    for turn, (start, size) in enumerate(tiles, 1):
        part = slice(start, start + size)
        back_ref[:, part] = both_back(image, cotangent, output_ref[:, part, :]).astype(bf16)
        until = len(pieces) * turn // len(tiles)
        for index in range(done, until):
            arrive(copies, index)
            start, size = pieces[index]
            part = slice(start, start + size)
            product = both_experts(image, normed_ref[:, part], slots[index % AHEAD])
            if index == 0:
                raw_ref[...] = product
            else:
                raw_ref[...] += product
            begin(copies, index + AHEAD)
        done = until
    scaling = jnp.where(image, head_ref[1, 0:1, :], head_ref[0, 0:1, :])
    for h in range(raw_ref.shape[1] // HEAD_DIM):
        part = slice(h * HEAD_DIM, (h + 1) * HEAD_DIM)
        raw = raw_ref[:, part]
        query_ref[:, part] = (raw * inverse_norm(raw) * scaling).astype(bf16)


def middle_stage(rank, modality, head_gain, normed, output_weight, query_weight, parts):
    rows = normed.shape[0]
    width = query_weight.shape[2]
    pieces = chunks_of(query_weight.shape[1], 512)
    return pl.pallas_call(
        functools.partial(middle_kernel, len(parts), pieces),
        out_shape=[
            jax.ShapeDtypeStruct((rows, width), bf16),
            jax.ShapeDtypeStruct((rows, width), f32),
            jax.ShapeDtypeStruct((rows, width), bf16),
        ],
        in_specs=[SMEM, VMEM, VMEM, VMEM, VMEM, ANY] + [VMEM] * len(parts),
        out_specs=[VMEM] * 3,
        scratch_shapes=[
            ring(query_weight, pieces),
            pltpu.SemaphoreType.DMA((len(pieces), 2)),
        ],
        compiler_params=params(14),
        cost_estimate=cost(8),
        name="middle_stage",
    )(rank, modality, head_gain, normed, output_weight, streamed(query_weight), *parts)


def attention_kernel(blocks, pairs, per_group, *refs):
    place_ref, order_ref, segments_ref, query_ref, back_ref = refs[:5]
    memory_refs = refs[5 : 5 + blocks]
    attended_ref, upstream_ref = refs[5 + blocks : 7 + blocks]
    grad_refs = refs[7 + blocks :]
    rows = query_ref.shape[0]
    scale = 1.0 / math.sqrt(HEAD_DIM)
    lines = [
        segments_ref[pl.ds(order_ref[seq_source(place_ref[0], step, blocks)], 1), :]
        for step in [0, *seq_steps(blocks)]
    ]
    key_segments = jnp.concatenate(lines, axis=1).astype(f32)
    visible = key_segments <= column(lines[0])
    for pair in range(pairs):
        columns = [
            slice(h * HEAD_DIM, (h + 1) * HEAD_DIM)
            for h in range(pair * per_group, (pair + 1) * per_group)
        ]
        parts = [slice(h * rows, (h + 1) * rows) for h in range(per_group)]
        keys = slice(2 * pair * HEAD_DIM, (2 * pair + 1) * HEAD_DIM)
        values = slice((2 * pair + 1) * HEAD_DIM, (2 * pair + 2) * HEAD_DIM)
        query = jnp.concatenate([query_ref[:, c] for c in columns], axis=0)
        back = jnp.concatenate([back_ref[:, c] for c in columns], axis=0)
        key = jnp.concatenate([m[:, keys] for m in memory_refs], axis=0)
        value = jnp.concatenate([m[:, values] for m in memory_refs], axis=0)
        scores = dot_nt(query, key) * (scale * math.log2(math.e))
        weights = jnp.concatenate(
            [jnp.where(visible, jnp.exp2(scores[p]), 0.0).astype(bf16) for p in parts], axis=0
        )
        weights32 = weights.astype(f32)
        inverse = 1.0 / jnp.sum(weights32, axis=1, keepdims=True)
        numerator = jnp.dot(weights, value, preferred_element_type=f32)
        attended = (numerator * inverse).astype(bf16)
        offset = jnp.sum(back.astype(f32) * attended.astype(f32), axis=1, keepdims=True)
        probability = (weights32 * inverse).astype(bf16)
        back_prob = dot_nt(back, value)
        back_score = (probability.astype(f32) * (back_prob - offset)).astype(bf16)
        back_query = jnp.dot(back_score, key, preferred_element_type=f32) * scale
        back_key = dot_tn(back_score, query) * scale
        back_value = dot_tn(probability, back)
        for b, grad_ref in enumerate(grad_refs):
            part = slice(b * rows, (b + 1) * rows)
            grad_ref[:, keys] = back_key[part].astype(grad_ref.dtype)
            grad_ref[:, values] = back_value[part].astype(grad_ref.dtype)
        for part, place in zip(parts, columns):
            attended_ref[:, place] = attended[part]
            upstream_ref[:, place] = back_query[part]


def attention_stage(place, order, segments, query, back, memories):
    rows, width = query.shape
    blocks = len(memories)
    pairs = memories[0].shape[1] // (2 * HEAD_DIM)
    per_group = width // HEAD_DIM // pairs
    outs = [
        jax.ShapeDtypeStruct((rows, width), bf16),
        jax.ShapeDtypeStruct((rows, width), f32),
    ] + [
        jax.ShapeDtypeStruct((rows, pairs * 2 * HEAD_DIM), f32 if b == 0 else bf16)
        for b in range(blocks)
    ]
    return pl.pallas_call(
        functools.partial(attention_kernel, blocks, pairs, per_group),
        out_shape=outs,
        in_specs=[SMEM, SMEM] + [VMEM] * (3 + blocks),
        out_specs=[VMEM] * (2 + blocks),
        compiler_params=params(12),
        cost_estimate=cost(4),
        name="attention_stage",
    )(place, order, segments, query, back, *memories)


def turn_kernel(pieces, outputs, *refs):
    rank_ref, modality_ref, head_ref, output_ref, attended_ref = refs[:5]
    upstream_ref, raw_ref, query_ref = refs[5:8]
    out_refs = refs[8 : 8 + outputs]
    part_ref, inner_ref, back_ref, slots, sems = refs[8 + outputs :]
    copies = copies_of(query_ref, slots, sems, pieces, slots=AHEAD)
    begin_first(copies)
    image = column(modality_ref[...]) > 0.0
    scaling = jnp.where(image, head_ref[1, 0:1, :], head_ref[0, 0:1, :])
    inner = jnp.zeros((raw_ref.shape[0], 1), f32)
    for start, size in chunks_of(raw_ref.shape[1], HEAD_DIM):
        part = slice(start, start + size)
        raw = raw_ref[:, part]
        back = norm_back(raw, inverse_norm(raw), scaling, upstream_ref[:, part]).astype(bf16)
        back_ref[:, part] = back
        inner += jnp.sum(back.astype(f32) * raw, axis=1, keepdims=True)
    inner_ref[...] = row_of(inner)
    attended = attended_ref[...]
    extent = output_ref.shape[2] // 2

    def project(rank):
        sent_ref, kept_ref = out_refs
        for start, size in chunks_of(extent, 896):
            part = slice(start, start + size)
            first = (1 - rank) * extent + start
            product = both_experts(image, attended, output_ref[:, :, first : first + size])
            sent_ref[:, part] = product.astype(bf16)
            first = rank * extent + start
            product = both_experts(image, attended, output_ref[:, :, first : first + size])
            kept_ref[:, part] = product

    if outputs == 1:
        out_refs[0][...] = both_experts(image, attended, output_ref[...]).astype(bf16)
    else:
        for rank in range(2):
            pl.when(rank_ref[0] == rank)(functools.partial(project, rank))
    for index, (start, size) in enumerate(pieces):
        arrive(copies, index)
        for inside, tile in chunks_of(size, HEAD_DIM):
            weights = slots[index % AHEAD, :, inside : inside + tile, :]
            part = slice(start + inside, start + inside + tile)
            part_ref[:, part] = both_back(image, back_ref[...], weights)
        begin(copies, index + AHEAD)


def turn_stage(
    rank, modality, head_gain, output_weight, attended, upstream, raw, query_weight, split
):
    depth = query_weight.shape[1]
    width = output_weight.shape[2]
    rows = attended.shape[0]
    pieces = chunks_of(depth, 512)
    if split:
        outs = [
            jax.ShapeDtypeStruct((rows, width // 2), bf16),
            jax.ShapeDtypeStruct((rows, width // 2), f32),
        ]
    else:
        outs = [jax.ShapeDtypeStruct((rows, width), bf16)]
    *projected, part, inner = pl.pallas_call(
        functools.partial(turn_kernel, pieces, len(outs)),
        out_shape=outs
        + [jax.ShapeDtypeStruct((rows, depth), f32), jax.ShapeDtypeStruct((1, rows), f32)],
        in_specs=[SMEM] + [VMEM] * 6 + [ANY],
        out_specs=[VMEM] * (len(outs) + 2),
        scratch_shapes=[
            pltpu.VMEM(attended.shape, bf16),
            ring(query_weight, pieces),
            pltpu.SemaphoreType.DMA((len(pieces), 2)),
        ],
        compiler_params=params(16),
        cost_estimate=cost(10),
        name="turn_stage",
    )(rank, modality, head_gain, output_weight, attended, upstream, raw, streamed(query_weight))
    return projected, part, inner


def tie(passed, arrived):
    def kernel(passed_ref, arrived_ref, out_ref):
        del passed_ref, arrived_ref, out_ref

    return pl.pallas_call(
        kernel,
        out_shape=jax.ShapeDtypeStruct(passed.shape, passed.dtype),
        in_specs=[ANY, ANY],
        out_specs=ANY,
        input_output_aliases={0: 0},
        compiler_params=params(1),
        cost_estimate=cost(0.1),
        name="tie",
    )(passed, arrived)


def key_back_kernel(split, *refs):
    rank_ref, modality_ref, head_ref, raw_ref, inner_in_ref, part_ref, weight_ref = refs[:7]
    grad_refs = refs[7:-3]
    out_ref, back_ref, inner_ref = refs[-3:]
    base = pl.multiple_of((1 - rank_ref[0]) * out_ref.shape[1], HEAD_DIM) if split else 0
    image = column(modality_ref[...]) > 0.0
    blocks = raw_ref.shape[1] // HEAD_DIM
    scaling = jnp.where(image, head_ref[1, 1:2, :], head_ref[0, 1:2, :])
    inner = jnp.zeros((raw_ref.shape[0], 1), f32)
    for b in range(blocks):
        part = slice(b * HEAD_DIM, (b + 1) * HEAD_DIM)
        raw = raw_ref[:, part]
        upstream = grad_refs[0][:, part].astype(f32)
        for grad_ref in grad_refs[1:]:
            upstream += grad_ref[:, part].astype(f32)
        is_key = (rank_ref[0] * blocks + b) % 2 == 0
        normed_back = norm_back(raw, inverse_norm(raw), scaling, upstream)
        back = jnp.where(is_key, normed_back, upstream).astype(bf16)
        back_ref[:, part] = back
        inner += jnp.sum(back.astype(f32) * raw, axis=1, keepdims=True)
    inner_ref[...] = inner_in_ref[...] + row_of(inner)
    for start, size in chunks_of(out_ref.shape[1], HEAD_DIM):
        place = pl.ds(base + start, size)
        product = both_back(image, back_ref[...], weight_ref[:, place, :])
        out_ref[:, start : start + size] = (product + part_ref[:, place]).astype(bf16)


def key_back_stage(rank, modality, head_gain, raw, inner, part, weights, grads, split):
    _, depth, width = weights.shape
    rows = raw.shape[0]
    return pl.pallas_call(
        functools.partial(key_back_kernel, split),
        out_shape=[
            jax.ShapeDtypeStruct((rows, depth // 2 if split else depth), bf16),
            jax.ShapeDtypeStruct((rows, width), bf16),
            jax.ShapeDtypeStruct((1, rows), f32),
        ],
        in_specs=[SMEM] + [VMEM] * (6 + len(grads)),
        out_specs=[VMEM] * 3,
        compiler_params=params(6),
        cost_estimate=cost(2),
        name="key_back_stage",
    )(rank, modality, head_gain, raw, inner, part, weights, *grads)


def kept_kernel(rank_ref, modality_ref, part_ref, weight_ref, back_ref, out_ref):
    base = pl.multiple_of(rank_ref[0] * out_ref.shape[1], HEAD_DIM)
    image = column(modality_ref[...]) > 0.0
    for start, size in chunks_of(out_ref.shape[1], HEAD_DIM):
        place = pl.ds(base + start, size)
        product = both_back(image, back_ref[...], weight_ref[:, place, :])
        out_ref[:, start : start + size] = product + part_ref[:, place]


def kept_stage(rank, modality, part, weights, back):
    return pl.pallas_call(
        kept_kernel,
        out_shape=jax.ShapeDtypeStruct((back.shape[0], weights.shape[1] // 2), f32),
        in_specs=[SMEM] + [VMEM] * 4,
        out_specs=VMEM,
        compiler_params=params(6),
        cost_estimate=cost(2),
        name="kept_stage",
    )(rank, modality, part, weights, back)


def finish_kernel(backs, inners, total_width, *refs):
    rank_ref, modality_ref, gain_ref, factor_ref, inputs_ref = refs[:5]
    back_refs = refs[5 : 5 + backs]
    inner_refs = refs[5 + backs : 5 + backs + inners]
    rest = refs[5 + backs + inners :]
    width = inputs_ref.shape[1]
    copies = []

    def send(staged_ref, out_ref, sem, part):
        copy = pltpu.make_async_copy(staged_ref.at[:, part], out_ref.at[:, part], sem)
        copy.start()
        copies.append(copy)

    pieces = [slice(start, start + size) for start, size in chunks_of(width, 896)]
    if len(rest) == 7:
        kept_ref, other_ref, attention_ref, out_ref, staged, staged_attention, sems = rest
        for index, part in enumerate(pieces):
            whole = kept_ref[:, part] + other_ref[:, part].astype(f32)
            staged_attention[:, part] = whole.astype(bf16)
            send(staged_attention, attention_ref, sems.at[1, index], part)
    else:
        out_ref, staged, sems = rest
    image = column(modality_ref[...]) > 0.0
    factor = column(factor_ref[...])
    inner = inner_refs[0][...]
    for ref in inner_refs[1:]:
        inner += ref[...]
    inner_mean = factor * column(inner) * (1.0 / total_width)
    gathered = gain_ref.shape[1] != width
    for index, part in enumerate(pieces):
        columns = part
        if gathered:
            first = pl.multiple_of(rank_ref[0] * width, HEAD_DIM) + part.start
            columns = pl.ds(first, part.stop - part.start)
        back = back_refs[0][:, part].astype(f32)
        for ref in back_refs[1:]:
            back += ref[:, part].astype(f32)
        rows = inputs_ref[:, part].astype(f32)
        result = factor * (gain_of(image, gain_ref, columns) * back - rows * inner_mean)
        staged[:, part] = result.astype(bf16)
        send(staged, out_ref, sems.at[0, index], part)
    for copy in copies:
        copy.wait()


def finish(rank, total_width, modality, gain, factor, inputs, backs, inners, projected):
    shape = jax.ShapeDtypeStruct(inputs.shape, bf16)
    arrays = [modality, gain, factor, inputs, *backs, *inners, *projected]
    count = 2 if projected else 1
    pieces = len(chunks_of(inputs.shape[1], 896))
    return pl.pallas_call(
        functools.partial(finish_kernel, len(backs), len(inners), total_width),
        out_shape=[shape] * count,
        in_specs=[SMEM] + [VMEM] * len(arrays),
        out_specs=[ANY] * count,
        scratch_shapes=[pltpu.VMEM(inputs.shape, bf16)] * count
        + [pltpu.SemaphoreType.DMA((count, pieces))],
        compiler_params=params(6),
        cost_estimate=cost(1),
        name="finish",
    )(rank, *arrays)


def local(
    inputs,
    cotangent,
    norm_gain,
    head_gain,
    query_weight,
    key_weight,
    output_weight,
    modality,
    segments,
    block_order,
):
    tensor_rank = lax.axis_index("tensor")
    block_rank = lax.axis_index("seq")
    tensor_count = lax.axis_size("tensor")
    block_count = lax.axis_size("seq")
    local_rows, local_width = inputs.shape
    full_width = local_width * tensor_count
    split = tensor_count == 2
    swap = [(0, 1), (1, 0)]
    rank = tensor_rank.astype(jnp.int32).reshape(1)
    modality = modality.reshape(1, local_rows)
    segments = segments.reshape(block_count, local_rows)

    def spread(part):
        if split:
            return [part, lax.ppermute(part, "tensor", swap)]
        return [lax.all_gather(part, "tensor", axis=1, tiled=True)]

    def scatter_columns(part):
        return lax.psum_scatter(part, "tensor", scatter_dimension=1, tiled=True)

    memory, key_raw, normed, row_factor = key_stage(
        rank, modality, norm_gain, head_gain, fetch(key_weight), spread(inputs)
    )
    shared = tensor_count > KV_HEADS
    is_even = tensor_rank % 2 == 0
    pair_swap = [(i, i ^ 1) for i in range(tensor_count)]
    if shared:
        partner = lax.ppermute(memory, "tensor", pair_swap)
        memory = jnp.where(
            is_even,
            jnp.concatenate([memory, partner], 1),
            jnp.concatenate([partner, memory], 1),
        )
    memories = [memory]
    for step in seq_steps(block_count):
        memories.append(lax.ppermute(memory, "seq", seq_pairs(step, block_count)))

    query, query_raw, back_attended = middle_stage(
        rank, modality, head_gain, normed, output_weight, query_weight, spread(cotangent)
    )
    attended, upstream, own_grad, *grads = attention_stage(
        block_rank.astype(jnp.int32).reshape(1),
        block_order,
        segments,
        query,
        back_attended,
        memories,
    )
    incoming = [
        lax.ppermute(grad, "seq", inverted(seq_pairs(step, block_count)))
        for step, grad in zip(seq_steps(block_count), grads)
    ]

    projected, gradient_part, inner = turn_stage(
        rank,
        modality,
        head_gain,
        output_weight,
        attended,
        upstream,
        query_raw,
        query_weight,
        split,
    )
    if split:
        passed = tie(projected[0], incoming[0])
        projected = [projected[1], lax.ppermute(passed, "tensor", swap)]
    else:
        attention_out = scatter_columns(projected[0])
        projected = []

    if shared:
        total = own_grad + sum(grad.astype(f32) for grad in incoming)
        low, high = total[:, :HEAD_DIM], total[:, HEAD_DIM:]
        outgoing = jnp.where(is_even, high, low).astype(bf16)
        sums = [jnp.where(is_even, low, high), lax.ppermute(outgoing, "tensor", pair_swap)]
    else:
        sums = [own_grad, *incoming]
    sent, slice_back, inner = key_back_stage(
        rank,
        modality,
        head_gain,
        key_raw,
        inner,
        gradient_part,
        key_weight,
        sums,
        split,
    )
    if split:
        inners = [inner, lax.ppermute(inner, "tensor", swap)]
        other = lax.ppermute(sent, "tensor", swap)
        kept = kept_stage(rank, modality, gradient_part, key_weight, slice_back)
        backs = [kept, other]
        gain = norm_gain
    else:
        inners = [lax.psum(inner, "tensor")]
        backs = [scatter_columns(sent)]
        gain = lax.dynamic_slice_in_dim(norm_gain, tensor_rank * local_width, local_width, 1)
    results = finish(
        rank, full_width, modality, gain, row_factor, inputs, backs, inners, projected
    )
    if split:
        attention_out = results[0]
    return (attention_out, results[-1])


def solution(mesh):
    return jax.shard_map(
        local,
        mesh=mesh,
        in_specs=(
            P(("dp", "seq"), "tensor"),
            P(("dp", "seq"), "tensor"),
            P(),
            P(),
            P(None, None, "tensor"),
            P(None, None, "tensor"),
            P(None, "tensor", None),
            P(("dp", "seq")),
            P("dp"),
            P("dp"),
        ),
        out_specs=(P(("dp", "seq"), "tensor"), P(("dp", "seq"), "tensor")),
        check_vma=False,
    )
```

```python
import functools
import math

import jax
import jax.numpy as jnp
from jax import lax
from jax.experimental import pallas as pl
from jax.experimental.pallas import tpu as pltpu
from jax.sharding import PartitionSpec as P

KV_HEADS = 4
HEAD_DIM = 128
MIB = 1024 * 1024

epsilon = 1e-06
bf16 = jnp.bfloat16
f32 = jnp.float32
SMEM = pl.BlockSpec(memory_space=pltpu.SMEM)
VMEM = pl.BlockSpec(memory_space=pltpu.VMEM)
ANY = pl.BlockSpec(memory_space=pl.ANY)


def seq_pairs(step, count):
    if count & (count - 1) == 0:
        return [(i, i ^ step) for i in range(count)]
    return [(i, (i + step) % count) for i in range(count)]


def seq_steps(count):
    return sorted(range(1, count), key=lambda step: (step != count // 2, step))


def seq_source(rank, step, count):
    if count & (count - 1) == 0:
        return rank ^ step
    return (rank - step) % count


def inverted(pairs):
    return [(b, a) for a, b in pairs]


def tile_of(extent, most):
    best = HEAD_DIM
    for size in range(HEAD_DIM, min(extent, most) + 1, HEAD_DIM):
        if extent % size == 0:
            best = size
    return best


def dot_nt(a, b):
    return lax.dot_general(a, b, (((1,), (1,)), ((), ())), preferred_element_type=f32)


def dot_tn(a, b):
    return lax.dot_general(a, b, (((0,), (0,)), ((), ())), preferred_element_type=f32)


def column(row):
    count = row.shape[1]
    return jnp.broadcast_to(row.astype(f32), (count, count)).T[:, :1]


def row_of(col):
    count = col.shape[0]
    return jnp.broadcast_to(col, (count, count)).T[:1, :]


def inverse_norm(values):
    return lax.rsqrt(jnp.mean(values * values, axis=-1, keepdims=True) + epsilon)


def norm_back(values, factor, scaling, upstream):
    unit_rows = values * factor
    inner_mean = jnp.mean(scaling * upstream * unit_rows, axis=-1, keepdims=True)
    return factor * (scaling * upstream - unit_rows * inner_mean)


def streamed(weights):
    return pltpu.with_memory_space_constraint(weights, pltpu.HBM)


def params(mib):
    return pltpu.CompilerParams(vmem_limit_bytes=mib * MIB)


def cost(micros):
    return pl.CostEstimate(
        flops=int(micros * 1e9), bytes_accessed=int(micros * 2e6), transcendentals=0
    )


def in_order(rank, part_refs):
    if len(part_refs) == 1:
        return part_refs[0][...]
    own, other = part_refs[0][...], part_refs[1][...]
    first = rank == 0
    return jnp.concatenate([jnp.where(first, own, other), jnp.where(first, other, own)], axis=1)


def both_experts(image, rows, weights):
    zero = jnp.zeros_like(rows)
    masked = jnp.concatenate([jnp.where(image, zero, rows), jnp.where(image, rows, zero)], axis=1)
    flat = weights.reshape(2 * weights.shape[1], weights.shape[2])
    return jnp.dot(masked, flat, preferred_element_type=f32)


def both_back(image, rows, weights):
    return jnp.where(image, dot_nt(rows, weights[1]), dot_nt(rows, weights[0]))


def chunks_of(extent, most):
    size = tile_of(extent, most)
    return [(start, size) for start in range(0, extent, size)]


AHEAD = 4


def copies_of(source_ref, target_ref, sem_ref, pieces, base=0, slots=0):
    copies = []
    for index, (start, size) in enumerate(pieces):
        pair = []
        for e in range(2):
            if slots:
                target = target_ref.at[index % slots, e]
            else:
                target = target_ref.at[e, pl.ds(start, size), :]
            source = source_ref.at[e, pl.ds(base + start, size), :]
            pair.append(pltpu.make_async_copy(source, target, sem_ref.at[index, e]))
        copies.append(pair)
    return copies


def begin(copies, index):
    if index < len(copies):
        for copy in copies[index]:
            copy.start()


def begin_first(copies):
    for index in range(AHEAD):
        begin(copies, index)


def arrive(copies, index):
    for copy in copies[index]:
        copy.wait()


def ring(weights, pieces):
    return pltpu.VMEM((AHEAD, 2, pieces[0][1], weights.shape[2]), weights.dtype)


def resident(weights):
    return pltpu.VMEM(weights.shape, weights.dtype)


def fetch_kernel(pieces, weight_ref, held_ref, sem_ref):
    copies = copies_of(weight_ref, held_ref, sem_ref, pieces)
    for pair in copies:
        for copy in pair:
            copy.start()
    for pair in copies:
        for copy in pair:
            copy.wait()


def fetch(weights):
    pieces = chunks_of(weights.shape[1], 896)
    return pl.pallas_call(
        functools.partial(fetch_kernel, pieces),
        out_shape=resident(weights),
        in_specs=[ANY],
        out_specs=VMEM,
        scratch_shapes=[pltpu.SemaphoreType.DMA((len(pieces), 2))],
        compiler_params=params(1),
        cost_estimate=cost(0.2),
        name="fetch",
    )(streamed(weights))


def gain_of(image, gain_ref, columns):
    return jnp.where(image, gain_ref[1:2, columns], gain_ref[0:1, columns])


def key_kernel(count, *refs):
    rank_ref, modality_ref, gain_ref, head_ref, weight_ref = refs[:5]
    part_refs = refs[5 : 5 + count]
    memory_ref, raw_ref, normed_ref, factor_ref = refs[5 + count :]
    image = column(modality_ref[...]) > 0.0
    rows = in_order(rank_ref[0], part_refs).astype(f32)
    factor = inverse_norm(rows)
    scaling = jnp.where(image, gain_ref[1:2, :], gain_ref[0:1, :])
    normed_ref[...] = (rows * factor * scaling).astype(bf16)
    factor_ref[...] = row_of(factor)
    for index, (start, size) in enumerate(chunks_of(normed_ref.shape[1], 1792)):
        part = slice(start, start + size)
        product = both_experts(image, normed_ref[:, part], weight_ref[:, part, :])
        if index == 0:
            raw_ref[...] = product
        else:
            raw_ref[...] += product
    blocks = raw_ref.shape[1] // HEAD_DIM
    scaling = jnp.where(image, head_ref[1, 1:2, :], head_ref[0, 1:2, :])
    for b in range(blocks):
        part = slice(b * HEAD_DIM, (b + 1) * HEAD_DIM)
        raw = raw_ref[:, part]
        normed = raw * inverse_norm(raw) * scaling
        is_key = (rank_ref[0] * blocks + b) % 2 == 0
        memory_ref[:, part] = jnp.where(is_key, normed, raw).astype(bf16)


def key_stage(rank, modality, norm_gain, head_gain, weights, parts):
    _, depth, width = weights.shape
    rows = parts[0].shape[0]
    return pl.pallas_call(
        functools.partial(key_kernel, len(parts)),
        out_shape=[
            jax.ShapeDtypeStruct((rows, width), bf16),
            jax.ShapeDtypeStruct((rows, width), f32),
            jax.ShapeDtypeStruct((rows, depth), bf16),
            jax.ShapeDtypeStruct((1, rows), f32),
        ],
        in_specs=[SMEM] + [VMEM] * (4 + len(parts)),
        out_specs=[VMEM] * 4,
        compiler_params=params(8),
        cost_estimate=cost(10),
        name="key_stage",
    )(rank, modality, norm_gain, head_gain, weights, *parts)


def middle_kernel(count, pieces, *refs):
    rank_ref, modality_ref, head_ref, normed_ref, output_ref, query_weight_ref = refs[:6]
    part_refs = refs[6 : 6 + count]
    query_ref, raw_ref, back_ref, slots, sems = refs[6 + count :]
    copies = copies_of(query_weight_ref, slots, sems, pieces, slots=AHEAD)
    begin_first(copies)
    image = column(modality_ref[...]) > 0.0
    cotangent = in_order(rank_ref[0], part_refs)
    tiles = chunks_of(output_ref.shape[1], HEAD_DIM)
    done = 0
    for turn, (start, size) in enumerate(tiles, 1):
        part = slice(start, start + size)
        back_ref[:, part] = both_back(image, cotangent, output_ref[:, part, :]).astype(bf16)
        until = len(pieces) * turn // len(tiles)
        for index in range(done, until):
            arrive(copies, index)
            start, size = pieces[index]
            part = slice(start, start + size)
            product = both_experts(image, normed_ref[:, part], slots[index % AHEAD])
            if index == 0:
                raw_ref[...] = product
            else:
                raw_ref[...] += product
            begin(copies, index + AHEAD)
        done = until
    scaling = jnp.where(image, head_ref[1, 0:1, :], head_ref[0, 0:1, :])
    for h in range(raw_ref.shape[1] // HEAD_DIM):
        part = slice(h * HEAD_DIM, (h + 1) * HEAD_DIM)
        raw = raw_ref[:, part]
        query_ref[:, part] = (raw * inverse_norm(raw) * scaling).astype(bf16)


def middle_stage(rank, modality, head_gain, normed, output_weight, query_weight, parts):
    rows = normed.shape[0]
    width = query_weight.shape[2]
    pieces = chunks_of(query_weight.shape[1], 512)
    return pl.pallas_call(
        functools.partial(middle_kernel, len(parts), pieces),
        out_shape=[
            jax.ShapeDtypeStruct((rows, width), bf16),
            jax.ShapeDtypeStruct((rows, width), f32),
            jax.ShapeDtypeStruct((rows, width), bf16),
        ],
        in_specs=[SMEM, VMEM, VMEM, VMEM, VMEM, ANY] + [VMEM] * len(parts),
        out_specs=[VMEM] * 3,
        scratch_shapes=[
            ring(query_weight, pieces),
            pltpu.SemaphoreType.DMA((len(pieces), 2)),
        ],
        compiler_params=params(14),
        cost_estimate=cost(8),
        name="middle_stage",
    )(rank, modality, head_gain, normed, output_weight, streamed(query_weight), *parts)


def attention_kernel(blocks, pairs, per_group, *refs):
    place_ref, order_ref, segments_ref, query_ref, back_ref = refs[:5]
    memory_refs = refs[5 : 5 + blocks]
    attended_ref, upstream_ref = refs[5 + blocks : 7 + blocks]
    grad_refs = refs[7 + blocks :]
    rows = query_ref.shape[0]
    scale = 1.0 / math.sqrt(HEAD_DIM)
    lines = [
        segments_ref[pl.ds(order_ref[seq_source(place_ref[0], step, blocks)], 1), :]
        for step in [0, *seq_steps(blocks)]
    ]
    key_segments = jnp.concatenate(lines, axis=1).astype(f32)
    visible = key_segments <= column(lines[0])
    for pair in range(pairs):
        columns = [
            slice(h * HEAD_DIM, (h + 1) * HEAD_DIM)
            for h in range(pair * per_group, (pair + 1) * per_group)
        ]
        parts = [slice(h * rows, (h + 1) * rows) for h in range(per_group)]
        keys = slice(2 * pair * HEAD_DIM, (2 * pair + 1) * HEAD_DIM)
        values = slice((2 * pair + 1) * HEAD_DIM, (2 * pair + 2) * HEAD_DIM)
        query = jnp.concatenate([query_ref[:, c] for c in columns], axis=0)
        back = jnp.concatenate([back_ref[:, c] for c in columns], axis=0)
        key = jnp.concatenate([m[:, keys] for m in memory_refs], axis=0)
        value = jnp.concatenate([m[:, values] for m in memory_refs], axis=0)
        scores = dot_nt(query, key) * (scale * math.log2(math.e))
        weights = jnp.concatenate(
            [jnp.where(visible, jnp.exp2(scores[p]), 0.0).astype(bf16) for p in parts], axis=0
        )
        weights32 = weights.astype(f32)
        inverse = 1.0 / jnp.sum(weights32, axis=1, keepdims=True)
        numerator = jnp.dot(weights, value, preferred_element_type=f32)
        attended = (numerator * inverse).astype(bf16)
        offset = jnp.sum(back.astype(f32) * attended.astype(f32), axis=1, keepdims=True)
        probability = (weights32 * inverse).astype(bf16)
        back_prob = dot_nt(back, value)
        back_score = (probability.astype(f32) * (back_prob - offset)).astype(bf16)
        back_query = jnp.dot(back_score, key, preferred_element_type=f32) * scale
        back_key = dot_tn(back_score, query) * scale
        back_value = dot_tn(probability, back)
        for b, grad_ref in enumerate(grad_refs):
            part = slice(b * rows, (b + 1) * rows)
            grad_ref[:, keys] = back_key[part].astype(grad_ref.dtype)
            grad_ref[:, values] = back_value[part].astype(grad_ref.dtype)
        for part, place in zip(parts, columns):
            attended_ref[:, place] = attended[part]
            upstream_ref[:, place] = back_query[part]


def attention_stage(place, order, segments, query, back, memories):
    rows, width = query.shape
    blocks = len(memories)
    pairs = memories[0].shape[1] // (2 * HEAD_DIM)
    per_group = width // HEAD_DIM // pairs
    outs = [
        jax.ShapeDtypeStruct((rows, width), bf16),
        jax.ShapeDtypeStruct((rows, width), f32),
    ] + [
        jax.ShapeDtypeStruct((rows, pairs * 2 * HEAD_DIM), f32 if b == 0 else bf16)
        for b in range(blocks)
    ]
    return pl.pallas_call(
        functools.partial(attention_kernel, blocks, pairs, per_group),
        out_shape=outs,
        in_specs=[SMEM, SMEM] + [VMEM] * (3 + blocks),
        out_specs=[VMEM] * (2 + blocks),
        compiler_params=params(12),
        cost_estimate=cost(4),
        name="attention_stage",
    )(place, order, segments, query, back, *memories)


def turn_kernel(pieces, outputs, *refs):
    rank_ref, modality_ref, head_ref, output_ref, attended_ref = refs[:5]
    upstream_ref, raw_ref, query_ref = refs[5:8]
    out_refs = refs[8 : 8 + outputs]
    part_ref, inner_ref, back_ref, slots, sems = refs[8 + outputs :]
    copies = copies_of(query_ref, slots, sems, pieces, slots=AHEAD)
    begin_first(copies)
    image = column(modality_ref[...]) > 0.0
    scaling = jnp.where(image, head_ref[1, 0:1, :], head_ref[0, 0:1, :])
    inner = jnp.zeros((raw_ref.shape[0], 1), f32)
    for start, size in chunks_of(raw_ref.shape[1], HEAD_DIM):
        part = slice(start, start + size)
        raw = raw_ref[:, part]
        back = norm_back(raw, inverse_norm(raw), scaling, upstream_ref[:, part]).astype(bf16)
        back_ref[:, part] = back
        inner += jnp.sum(back.astype(f32) * raw, axis=1, keepdims=True)
    inner_ref[...] = row_of(inner)
    attended = attended_ref[...]
    extent = output_ref.shape[2] // 2

    def project(rank):
        sent_ref, kept_ref = out_refs
        for start, size in chunks_of(extent, 896):
            part = slice(start, start + size)
            first = (1 - rank) * extent + start
            product = both_experts(image, attended, output_ref[:, :, first : first + size])
            sent_ref[:, part] = product.astype(bf16)
            first = rank * extent + start
            product = both_experts(image, attended, output_ref[:, :, first : first + size])
            kept_ref[:, part] = product

    if outputs == 1:
        out_refs[0][...] = both_experts(image, attended, output_ref[...]).astype(bf16)
    else:
        for rank in range(2):
            pl.when(rank_ref[0] == rank)(functools.partial(project, rank))
    for index, (start, size) in enumerate(pieces):
        arrive(copies, index)
        for inside, tile in chunks_of(size, HEAD_DIM):
            weights = slots[index % AHEAD, :, inside : inside + tile, :]
            part = slice(start + inside, start + inside + tile)
            part_ref[:, part] = both_back(image, back_ref[...], weights)
        begin(copies, index + AHEAD)


def turn_stage(
    rank, modality, head_gain, output_weight, attended, upstream, raw, query_weight, split
):
    depth = query_weight.shape[1]
    width = output_weight.shape[2]
    rows = attended.shape[0]
    pieces = chunks_of(depth, 512)
    if split:
        outs = [
            jax.ShapeDtypeStruct((rows, width // 2), bf16),
            jax.ShapeDtypeStruct((rows, width // 2), f32),
        ]
    else:
        outs = [jax.ShapeDtypeStruct((rows, width), bf16)]
    *projected, part, inner = pl.pallas_call(
        functools.partial(turn_kernel, pieces, len(outs)),
        out_shape=outs
        + [jax.ShapeDtypeStruct((rows, depth), f32), jax.ShapeDtypeStruct((1, rows), f32)],
        in_specs=[SMEM] + [VMEM] * 6 + [ANY],
        out_specs=[VMEM] * (len(outs) + 2),
        scratch_shapes=[
            pltpu.VMEM(attended.shape, bf16),
            ring(query_weight, pieces),
            pltpu.SemaphoreType.DMA((len(pieces), 2)),
        ],
        compiler_params=params(16),
        cost_estimate=cost(10),
        name="turn_stage",
    )(rank, modality, head_gain, output_weight, attended, upstream, raw, streamed(query_weight))
    return projected, part, inner


def tie(passed, arrived):
    def kernel(passed_ref, arrived_ref, out_ref):
        del passed_ref, arrived_ref, out_ref

    return pl.pallas_call(
        kernel,
        out_shape=jax.ShapeDtypeStruct(passed.shape, passed.dtype),
        in_specs=[ANY, ANY],
        out_specs=ANY,
        input_output_aliases={0: 0},
        compiler_params=params(1),
        cost_estimate=cost(0.1),
        name="tie",
    )(passed, arrived)


def key_back_kernel(split, *refs):
    rank_ref, modality_ref, head_ref, raw_ref, inner_in_ref, part_ref, weight_ref = refs[:7]
    grad_refs = refs[7:-3]
    out_ref, back_ref, inner_ref = refs[-3:]
    base = pl.multiple_of((1 - rank_ref[0]) * out_ref.shape[1], HEAD_DIM) if split else 0
    image = column(modality_ref[...]) > 0.0
    blocks = raw_ref.shape[1] // HEAD_DIM
    scaling = jnp.where(image, head_ref[1, 1:2, :], head_ref[0, 1:2, :])
    inner = jnp.zeros((raw_ref.shape[0], 1), f32)
    for b in range(blocks):
        part = slice(b * HEAD_DIM, (b + 1) * HEAD_DIM)
        raw = raw_ref[:, part]
        upstream = grad_refs[0][:, part].astype(f32)
        for grad_ref in grad_refs[1:]:
            upstream += grad_ref[:, part].astype(f32)
        is_key = (rank_ref[0] * blocks + b) % 2 == 0
        normed_back = norm_back(raw, inverse_norm(raw), scaling, upstream)
        back = jnp.where(is_key, normed_back, upstream).astype(bf16)
        back_ref[:, part] = back
        inner += jnp.sum(back.astype(f32) * raw, axis=1, keepdims=True)
    inner_ref[...] = inner_in_ref[...] + row_of(inner)
    for start, size in chunks_of(out_ref.shape[1], HEAD_DIM):
        place = pl.ds(base + start, size)
        product = both_back(image, back_ref[...], weight_ref[:, place, :])
        out_ref[:, start : start + size] = (product + part_ref[:, place]).astype(bf16)


def key_back_stage(rank, modality, head_gain, raw, inner, part, weights, grads, split):
    _, depth, width = weights.shape
    rows = raw.shape[0]
    return pl.pallas_call(
        functools.partial(key_back_kernel, split),
        out_shape=[
            jax.ShapeDtypeStruct((rows, depth // 2 if split else depth), bf16),
            jax.ShapeDtypeStruct((rows, width), bf16),
            jax.ShapeDtypeStruct((1, rows), f32),
        ],
        in_specs=[SMEM] + [VMEM] * (6 + len(grads)),
        out_specs=[VMEM] * 3,
        compiler_params=params(6),
        cost_estimate=cost(2),
        name="key_back_stage",
    )(rank, modality, head_gain, raw, inner, part, weights, *grads)


def kept_kernel(
    rank_ref,
    modality_ref,
    part_ref,
    weight_ref,
    back_ref,
    mine_ref,
    other_ref,
    out_ref,
    attention_ref,
    staged,
    sem,
):
    staged[...] = (mine_ref[...] + other_ref[...].astype(f32)).astype(bf16)
    copy = pltpu.make_async_copy(staged, attention_ref, sem)
    copy.start()
    base = pl.multiple_of(rank_ref[0] * out_ref.shape[1], HEAD_DIM)
    image = column(modality_ref[...]) > 0.0
    for start, size in chunks_of(out_ref.shape[1], HEAD_DIM):
        place = pl.ds(base + start, size)
        product = both_back(image, back_ref[...], weight_ref[:, place, :])
        out_ref[:, start : start + size] = product + part_ref[:, place]
    copy.wait()


def kept_stage(rank, modality, part, weights, back, mine, other):
    return pl.pallas_call(
        kept_kernel,
        out_shape=[
            jax.ShapeDtypeStruct((back.shape[0], weights.shape[1] // 2), f32),
            jax.ShapeDtypeStruct(other.shape, bf16),
        ],
        in_specs=[SMEM] + [VMEM] * 6,
        out_specs=[VMEM, ANY],
        scratch_shapes=[pltpu.VMEM(other.shape, bf16), pltpu.SemaphoreType.DMA],
        compiler_params=params(6),
        cost_estimate=cost(2),
        name="kept_stage",
    )(rank, modality, part, weights, back, mine, other)


def finish_kernel(backs, inners, total_width, *refs):
    rank_ref, modality_ref, gain_ref, factor_ref, inputs_ref = refs[:5]
    back_refs = refs[5 : 5 + backs]
    inner_refs = refs[5 + backs : 5 + backs + inners]
    rest = refs[5 + backs + inners :]
    width = inputs_ref.shape[1]
    copies = []

    def send(staged_ref, out_ref, sem, part):
        copy = pltpu.make_async_copy(staged_ref.at[:, part], out_ref.at[:, part], sem)
        copy.start()
        copies.append(copy)

    pieces = [slice(start, start + size) for start, size in chunks_of(width, 896)]
    out_ref, staged, sems = rest
    image = column(modality_ref[...]) > 0.0
    factor = column(factor_ref[...])
    inner = inner_refs[0][...]
    for ref in inner_refs[1:]:
        inner += ref[...]
    inner_mean = factor * column(inner) * (1.0 / total_width)
    gathered = gain_ref.shape[1] != width
    for index, part in enumerate(pieces):
        columns = part
        if gathered:
            first = pl.multiple_of(rank_ref[0] * width, HEAD_DIM) + part.start
            columns = pl.ds(first, part.stop - part.start)
        back = back_refs[0][:, part].astype(f32)
        for ref in back_refs[1:]:
            back += ref[:, part].astype(f32)
        rows = inputs_ref[:, part].astype(f32)
        result = factor * (gain_of(image, gain_ref, columns) * back - rows * inner_mean)
        staged[:, part] = result.astype(bf16)
        send(staged, out_ref, sems.at[index], part)
    for copy in copies:
        copy.wait()


def finish(rank, total_width, modality, gain, factor, inputs, backs, inners):
    arrays = [modality, gain, factor, inputs, *backs, *inners]
    pieces = len(chunks_of(inputs.shape[1], 896))
    return pl.pallas_call(
        functools.partial(finish_kernel, len(backs), len(inners), total_width),
        out_shape=jax.ShapeDtypeStruct(inputs.shape, bf16),
        in_specs=[SMEM] + [VMEM] * len(arrays),
        out_specs=ANY,
        scratch_shapes=[pltpu.VMEM(inputs.shape, bf16), pltpu.SemaphoreType.DMA((pieces,))],
        compiler_params=params(6),
        cost_estimate=cost(1),
        name="finish",
    )(rank, *arrays)


def local(
    inputs,
    cotangent,
    norm_gain,
    head_gain,
    query_weight,
    key_weight,
    output_weight,
    modality,
    segments,
    block_order,
):
    tensor_rank = lax.axis_index("tensor")
    block_rank = lax.axis_index("seq")
    tensor_count = lax.axis_size("tensor")
    block_count = lax.axis_size("seq")
    local_rows, local_width = inputs.shape
    full_width = local_width * tensor_count
    split = tensor_count == 2
    swap = [(0, 1), (1, 0)]
    rank = tensor_rank.astype(jnp.int32).reshape(1)
    modality = modality.reshape(1, local_rows)
    segments = segments.reshape(block_count, local_rows)

    def spread(part):
        if split:
            return [part, lax.ppermute(part, "tensor", swap)]
        return [lax.all_gather(part, "tensor", axis=1, tiled=True)]

    def scatter_columns(part):
        return lax.psum_scatter(part, "tensor", scatter_dimension=1, tiled=True)

    memory, key_raw, normed, row_factor = key_stage(
        rank, modality, norm_gain, head_gain, fetch(key_weight), spread(inputs)
    )
    shared = tensor_count > KV_HEADS
    is_even = tensor_rank % 2 == 0
    pair_swap = [(i, i ^ 1) for i in range(tensor_count)]
    if shared:
        partner = lax.ppermute(memory, "tensor", pair_swap)
        memory = jnp.where(
            is_even,
            jnp.concatenate([memory, partner], 1),
            jnp.concatenate([partner, memory], 1),
        )
    memories = [memory]
    for step in seq_steps(block_count):
        memories.append(lax.ppermute(memory, "seq", seq_pairs(step, block_count)))

    query, query_raw, back_attended = middle_stage(
        rank, modality, head_gain, normed, output_weight, query_weight, spread(cotangent)
    )
    attended, upstream, own_grad, *grads = attention_stage(
        block_rank.astype(jnp.int32).reshape(1),
        block_order,
        segments,
        query,
        back_attended,
        memories,
    )
    incoming = [
        lax.ppermute(grad, "seq", inverted(seq_pairs(step, block_count)))
        for step, grad in zip(seq_steps(block_count), grads)
    ]

    projected, gradient_part, inner = turn_stage(
        rank,
        modality,
        head_gain,
        output_weight,
        attended,
        upstream,
        query_raw,
        query_weight,
        split,
    )
    if split:
        passed = tie(projected[0], incoming[0])
        projected = [projected[1], lax.ppermute(passed, "tensor", swap)]
    else:
        attention_out = scatter_columns(projected[0])

    if shared:
        total = own_grad + sum(grad.astype(f32) for grad in incoming)
        low, high = total[:, :HEAD_DIM], total[:, HEAD_DIM:]
        outgoing = jnp.where(is_even, high, low).astype(bf16)
        sums = [jnp.where(is_even, low, high), lax.ppermute(outgoing, "tensor", pair_swap)]
    else:
        sums = [own_grad, *incoming]
    sent, slice_back, inner = key_back_stage(
        rank,
        modality,
        head_gain,
        key_raw,
        inner,
        gradient_part,
        key_weight,
        sums,
        split,
    )
    if split:
        inners = [inner, lax.ppermute(inner, "tensor", swap)]
        other = lax.ppermute(sent, "tensor", swap)
        kept, attention_out = kept_stage(
            rank, modality, gradient_part, key_weight, slice_back, *projected
        )
        backs = [kept, other]
        gain = norm_gain
    else:
        inners = [lax.psum(inner, "tensor")]
        backs = [scatter_columns(sent)]
        gain = lax.dynamic_slice_in_dim(norm_gain, tensor_rank * local_width, local_width, 1)
    grad_input = finish(rank, full_width, modality, gain, row_factor, inputs, backs, inners)
    return (attention_out, grad_input)


def solution(mesh):
    return jax.shard_map(
        local,
        mesh=mesh,
        in_specs=(
            P(("dp", "seq"), "tensor"),
            P(("dp", "seq"), "tensor"),
            P(),
            P(),
            P(None, None, "tensor"),
            P(None, None, "tensor"),
            P(None, "tensor", None),
            P(("dp", "seq")),
            P("dp"),
            P("dp"),
        ),
        out_specs=(P(("dp", "seq"), "tensor"), P(("dp", "seq"), "tensor")),
        check_vma=False,
    )
```

```python
import functools
import math

import jax
import jax.numpy as jnp
from jax import lax
from jax.experimental import pallas as pl
from jax.experimental.pallas import tpu as pltpu
from jax.sharding import PartitionSpec as P

KV_HEADS = 4
HEAD_DIM = 128
MIB = 1024 * 1024

epsilon = 1e-06
bf16 = jnp.bfloat16
f32 = jnp.float32
SMEM = pl.BlockSpec(memory_space=pltpu.SMEM)
VMEM = pl.BlockSpec(memory_space=pltpu.VMEM)
ANY = pl.BlockSpec(memory_space=pl.ANY)


def seq_pairs(step, count):
    if count & (count - 1) == 0:
        return [(i, i ^ step) for i in range(count)]
    return [(i, (i + step) % count) for i in range(count)]


def seq_steps(count):
    return sorted(range(1, count), key=lambda step: (step != count // 2, step))


def seq_source(rank, step, count):
    if count & (count - 1) == 0:
        return rank ^ step
    return (rank - step) % count


def inverted(pairs):
    return [(b, a) for a, b in pairs]


def tile_of(extent, most):
    best = HEAD_DIM
    for size in range(HEAD_DIM, min(extent, most) + 1, HEAD_DIM):
        if extent % size == 0:
            best = size
    return best


def dot_nt(a, b):
    return lax.dot_general(a, b, (((1,), (1,)), ((), ())), preferred_element_type=f32)


def dot_tn(a, b):
    return lax.dot_general(a, b, (((0,), (0,)), ((), ())), preferred_element_type=f32)


def column(row):
    count = row.shape[1]
    return jnp.broadcast_to(row.astype(f32), (count, count)).T[:, :1]


def row_of(col):
    count = col.shape[0]
    return jnp.broadcast_to(col, (count, count)).T[:1, :]


def inverse_norm(values):
    return lax.rsqrt(jnp.mean(values * values, axis=-1, keepdims=True) + epsilon)


def norm_back(values, factor, scaling, upstream):
    unit_rows = values * factor
    inner_mean = jnp.mean(scaling * upstream * unit_rows, axis=-1, keepdims=True)
    return factor * (scaling * upstream - unit_rows * inner_mean)


def streamed(weights):
    return pltpu.with_memory_space_constraint(weights, pltpu.HBM)


def params(mib):
    return pltpu.CompilerParams(vmem_limit_bytes=mib * MIB)


def cost(micros):
    return pl.CostEstimate(
        flops=int(micros * 1e9), bytes_accessed=int(micros * 2e6), transcendentals=0
    )


def in_order(rank, part_refs):
    if len(part_refs) == 1:
        return part_refs[0][...]
    own, other = part_refs[0][...], part_refs[1][...]
    first = rank == 0
    return jnp.concatenate([jnp.where(first, own, other), jnp.where(first, other, own)], axis=1)


def both_experts(image, rows, weights):
    zero = jnp.zeros_like(rows)
    masked = jnp.concatenate([jnp.where(image, zero, rows), jnp.where(image, rows, zero)], axis=1)
    flat = weights.reshape(2 * weights.shape[1], weights.shape[2])
    return jnp.dot(masked, flat, preferred_element_type=f32)


def both_back(image, rows, weights):
    return jnp.where(image, dot_nt(rows, weights[1]), dot_nt(rows, weights[0]))


def chunks_of(extent, most):
    size = tile_of(extent, most)
    return [(start, size) for start in range(0, extent, size)]


AHEAD = 4


def copies_of(source_ref, target_ref, sem_ref, pieces, base=0, slots=0):
    copies = []
    for index, (start, size) in enumerate(pieces):
        pair = []
        for e in range(2):
            if slots:
                target = target_ref.at[index % slots, e]
            else:
                target = target_ref.at[e, pl.ds(start, size), :]
            source = source_ref.at[e, pl.ds(base + start, size), :]
            pair.append(pltpu.make_async_copy(source, target, sem_ref.at[index, e]))
        copies.append(pair)
    return copies


def begin(copies, index):
    if index < len(copies):
        for copy in copies[index]:
            copy.start()


def begin_first(copies):
    for index in range(AHEAD):
        begin(copies, index)


def arrive(copies, index):
    for copy in copies[index]:
        copy.wait()


def ring(weights, pieces):
    return pltpu.VMEM((AHEAD, 2, pieces[0][1], weights.shape[2]), weights.dtype)


def resident(weights):
    return pltpu.VMEM(weights.shape, weights.dtype)


def fetch_kernel(pieces, weight_ref, held_ref, sem_ref):
    copies = copies_of(weight_ref, held_ref, sem_ref, pieces)
    for pair in copies:
        for copy in pair:
            copy.start()
    for pair in copies:
        for copy in pair:
            copy.wait()


def fetch(weights):
    pieces = chunks_of(weights.shape[1], 448)
    return pl.pallas_call(
        functools.partial(fetch_kernel, pieces),
        out_shape=resident(weights),
        in_specs=[ANY],
        out_specs=VMEM,
        scratch_shapes=[pltpu.SemaphoreType.DMA((len(pieces), 2))],
        compiler_params=params(1),
        cost_estimate=cost(0.2),
        name="fetch",
    )(streamed(weights))


def gain_of(image, gain_ref, columns):
    return jnp.where(image, gain_ref[1:2, columns], gain_ref[0:1, columns])


def key_kernel(count, *refs):
    rank_ref, modality_ref, gain_ref, head_ref, weight_ref = refs[:5]
    part_refs = refs[5 : 5 + count]
    memory_ref, raw_ref, normed_ref, factor_ref = refs[5 + count :]
    image = column(modality_ref[...]) > 0.0
    rows = in_order(rank_ref[0], part_refs).astype(f32)
    factor = inverse_norm(rows)
    scaling = jnp.where(image, gain_ref[1:2, :], gain_ref[0:1, :])
    normed_ref[...] = (rows * factor * scaling).astype(bf16)
    factor_ref[...] = row_of(factor)
    for index, (start, size) in enumerate(chunks_of(normed_ref.shape[1], 1792)):
        part = slice(start, start + size)
        product = both_experts(image, normed_ref[:, part], weight_ref[:, part, :])
        if index == 0:
            raw_ref[...] = product
        else:
            raw_ref[...] += product
    blocks = raw_ref.shape[1] // HEAD_DIM
    scaling = jnp.where(image, head_ref[1, 1:2, :], head_ref[0, 1:2, :])
    for b in range(blocks):
        part = slice(b * HEAD_DIM, (b + 1) * HEAD_DIM)
        raw = raw_ref[:, part]
        normed = raw * inverse_norm(raw) * scaling
        is_key = (rank_ref[0] * blocks + b) % 2 == 0
        memory_ref[:, part] = jnp.where(is_key, normed, raw).astype(bf16)


def key_stage(rank, modality, norm_gain, head_gain, weights, parts):
    _, depth, width = weights.shape
    rows = parts[0].shape[0]
    return pl.pallas_call(
        functools.partial(key_kernel, len(parts)),
        out_shape=[
            jax.ShapeDtypeStruct((rows, width), bf16),
            jax.ShapeDtypeStruct((rows, width), f32),
            jax.ShapeDtypeStruct((rows, depth), bf16),
            jax.ShapeDtypeStruct((1, rows), f32),
        ],
        in_specs=[SMEM] + [VMEM] * (4 + len(parts)),
        out_specs=[VMEM] * 4,
        compiler_params=params(8),
        cost_estimate=cost(20),
        name="key_stage",
    )(rank, modality, norm_gain, head_gain, weights, *parts)


def middle_kernel(count, pieces, *refs):
    rank_ref, modality_ref, head_ref, normed_ref, output_ref, query_weight_ref = refs[:6]
    part_refs = refs[6 : 6 + count]
    query_ref, raw_ref, back_ref, slots, sems = refs[6 + count :]
    copies = copies_of(query_weight_ref, slots, sems, pieces, slots=AHEAD)
    begin_first(copies)
    image = column(modality_ref[...]) > 0.0
    cotangent = in_order(rank_ref[0], part_refs)
    tiles = chunks_of(output_ref.shape[1], HEAD_DIM)
    done = 0
    for turn, (start, size) in enumerate(tiles, 1):
        part = slice(start, start + size)
        back_ref[:, part] = both_back(image, cotangent, output_ref[:, part, :]).astype(bf16)
        until = len(pieces) * turn // len(tiles)
        for index in range(done, until):
            arrive(copies, index)
            start, size = pieces[index]
            part = slice(start, start + size)
            product = both_experts(image, normed_ref[:, part], slots[index % AHEAD])
            if index == 0:
                raw_ref[...] = product
            else:
                raw_ref[...] += product
            begin(copies, index + AHEAD)
        done = until
    scaling = jnp.where(image, head_ref[1, 0:1, :], head_ref[0, 0:1, :])
    for h in range(raw_ref.shape[1] // HEAD_DIM):
        part = slice(h * HEAD_DIM, (h + 1) * HEAD_DIM)
        raw = raw_ref[:, part]
        query_ref[:, part] = (raw * inverse_norm(raw) * scaling).astype(bf16)


def middle_stage(rank, modality, head_gain, normed, output_weight, query_weight, parts):
    rows = normed.shape[0]
    width = query_weight.shape[2]
    pieces = chunks_of(query_weight.shape[1], 512)
    return pl.pallas_call(
        functools.partial(middle_kernel, len(parts), pieces),
        out_shape=[
            jax.ShapeDtypeStruct((rows, width), bf16),
            jax.ShapeDtypeStruct((rows, width), f32),
            jax.ShapeDtypeStruct((rows, width), bf16),
        ],
        in_specs=[SMEM, VMEM, VMEM, VMEM, VMEM, ANY] + [VMEM] * len(parts),
        out_specs=[VMEM] * 3,
        scratch_shapes=[
            ring(query_weight, pieces),
            pltpu.SemaphoreType.DMA((len(pieces), 2)),
        ],
        compiler_params=params(14),
        cost_estimate=cost(8),
        name="middle_stage",
    )(rank, modality, head_gain, normed, output_weight, streamed(query_weight), *parts)


def attention_kernel(blocks, pairs, per_group, *refs):
    place_ref, order_ref, segments_ref, query_ref, back_ref = refs[:5]
    memory_refs = refs[5 : 5 + blocks]
    attended_ref, upstream_ref = refs[5 + blocks : 7 + blocks]
    grad_refs = refs[7 + blocks :]
    rows = query_ref.shape[0]
    scale = 1.0 / math.sqrt(HEAD_DIM)
    lines = [
        segments_ref[pl.ds(order_ref[seq_source(place_ref[0], step, blocks)], 1), :]
        for step in [0, *seq_steps(blocks)]
    ]
    key_segments = jnp.concatenate(lines, axis=1).astype(f32)
    visible = key_segments <= column(lines[0])
    for pair in range(pairs):
        columns = [
            slice(h * HEAD_DIM, (h + 1) * HEAD_DIM)
            for h in range(pair * per_group, (pair + 1) * per_group)
        ]
        parts = [slice(h * rows, (h + 1) * rows) for h in range(per_group)]
        keys = slice(2 * pair * HEAD_DIM, (2 * pair + 1) * HEAD_DIM)
        values = slice((2 * pair + 1) * HEAD_DIM, (2 * pair + 2) * HEAD_DIM)
        query = jnp.concatenate([query_ref[:, c] for c in columns], axis=0)
        back = jnp.concatenate([back_ref[:, c] for c in columns], axis=0)
        key = jnp.concatenate([m[:, keys] for m in memory_refs], axis=0)
        value = jnp.concatenate([m[:, values] for m in memory_refs], axis=0)
        scores = dot_nt(query, key) * (scale * math.log2(math.e))
        weights = jnp.concatenate(
            [jnp.where(visible, jnp.exp2(scores[p]), 0.0).astype(bf16) for p in parts], axis=0
        )
        weights32 = weights.astype(f32)
        inverse = 1.0 / jnp.sum(weights32, axis=1, keepdims=True)
        numerator = jnp.dot(weights, value, preferred_element_type=f32)
        attended = (numerator * inverse).astype(bf16)
        offset = jnp.sum(back.astype(f32) * attended.astype(f32), axis=1, keepdims=True)
        probability = (weights32 * inverse).astype(bf16)
        back_prob = dot_nt(back, value)
        back_score = (probability.astype(f32) * (back_prob - offset)).astype(bf16)
        back_query = jnp.dot(back_score, key, preferred_element_type=f32) * scale
        back_key = dot_tn(back_score, query) * scale
        back_value = dot_tn(probability, back)
        for b, grad_ref in enumerate(grad_refs):
            part = slice(b * rows, (b + 1) * rows)
            grad_ref[:, keys] = back_key[part].astype(grad_ref.dtype)
            grad_ref[:, values] = back_value[part].astype(grad_ref.dtype)
        for part, place in zip(parts, columns):
            attended_ref[:, place] = attended[part]
            upstream_ref[:, place] = back_query[part]


def attention_stage(place, order, segments, query, back, memories):
    rows, width = query.shape
    blocks = len(memories)
    pairs = memories[0].shape[1] // (2 * HEAD_DIM)
    per_group = width // HEAD_DIM // pairs
    outs = [
        jax.ShapeDtypeStruct((rows, width), bf16),
        jax.ShapeDtypeStruct((rows, width), f32),
    ] + [
        jax.ShapeDtypeStruct((rows, pairs * 2 * HEAD_DIM), f32 if b == 0 else bf16)
        for b in range(blocks)
    ]
    return pl.pallas_call(
        functools.partial(attention_kernel, blocks, pairs, per_group),
        out_shape=outs,
        in_specs=[SMEM, SMEM] + [VMEM] * (3 + blocks),
        out_specs=[VMEM] * (2 + blocks),
        compiler_params=params(12),
        cost_estimate=cost(4),
        name="attention_stage",
    )(place, order, segments, query, back, *memories)


def turn_kernel(pieces, outputs, *refs):
    rank_ref, modality_ref, head_ref, output_ref, attended_ref = refs[:5]
    upstream_ref, raw_ref, query_ref = refs[5:8]
    out_refs = refs[8 : 8 + outputs]
    part_ref, inner_ref, back_ref, slots, sems = refs[8 + outputs :]
    copies = copies_of(query_ref, slots, sems, pieces, slots=AHEAD)
    begin_first(copies)
    image = column(modality_ref[...]) > 0.0
    scaling = jnp.where(image, head_ref[1, 0:1, :], head_ref[0, 0:1, :])
    inner = jnp.zeros((raw_ref.shape[0], 1), f32)
    for start, size in chunks_of(raw_ref.shape[1], HEAD_DIM):
        part = slice(start, start + size)
        raw = raw_ref[:, part]
        back = norm_back(raw, inverse_norm(raw), scaling, upstream_ref[:, part]).astype(bf16)
        back_ref[:, part] = back
        inner += jnp.sum(back.astype(f32) * raw, axis=1, keepdims=True)
    inner_ref[...] = row_of(inner)
    attended = attended_ref[...]
    extent = output_ref.shape[2] // 2

    def project(rank):
        sent_ref, kept_ref = out_refs
        for start, size in chunks_of(extent, 896):
            part = slice(start, start + size)
            first = (1 - rank) * extent + start
            product = both_experts(image, attended, output_ref[:, :, first : first + size])
            sent_ref[:, part] = product.astype(bf16)
            first = rank * extent + start
            product = both_experts(image, attended, output_ref[:, :, first : first + size])
            kept_ref[:, part] = product

    if outputs == 1:
        out_refs[0][...] = both_experts(image, attended, output_ref[...]).astype(bf16)
    else:
        for rank in range(2):
            pl.when(rank_ref[0] == rank)(functools.partial(project, rank))
    for index, (start, size) in enumerate(pieces):
        arrive(copies, index)
        for inside, tile in chunks_of(size, HEAD_DIM):
            weights = slots[index % AHEAD, :, inside : inside + tile, :]
            part = slice(start + inside, start + inside + tile)
            part_ref[:, part] = both_back(image, back_ref[...], weights)
        begin(copies, index + AHEAD)


def turn_stage(
    rank, modality, head_gain, output_weight, attended, upstream, raw, query_weight, split
):
    depth = query_weight.shape[1]
    width = output_weight.shape[2]
    rows = attended.shape[0]
    pieces = chunks_of(depth, 512)
    if split:
        outs = [
            jax.ShapeDtypeStruct((rows, width // 2), bf16),
            jax.ShapeDtypeStruct((rows, width // 2), f32),
        ]
    else:
        outs = [jax.ShapeDtypeStruct((rows, width), bf16)]
    *projected, part, inner = pl.pallas_call(
        functools.partial(turn_kernel, pieces, len(outs)),
        out_shape=outs
        + [jax.ShapeDtypeStruct((rows, depth), f32), jax.ShapeDtypeStruct((1, rows), f32)],
        in_specs=[SMEM] + [VMEM] * 6 + [ANY],
        out_specs=[VMEM] * (len(outs) + 2),
        scratch_shapes=[
            pltpu.VMEM(attended.shape, bf16),
            ring(query_weight, pieces),
            pltpu.SemaphoreType.DMA((len(pieces), 2)),
        ],
        compiler_params=params(16),
        cost_estimate=cost(10),
        name="turn_stage",
    )(rank, modality, head_gain, output_weight, attended, upstream, raw, streamed(query_weight))
    return projected, part, inner


def tie(passed, arrived):
    def kernel(passed_ref, arrived_ref, out_ref):
        del passed_ref, arrived_ref, out_ref

    return pl.pallas_call(
        kernel,
        out_shape=jax.ShapeDtypeStruct(passed.shape, passed.dtype),
        in_specs=[ANY, ANY],
        out_specs=ANY,
        input_output_aliases={0: 0},
        compiler_params=params(1),
        cost_estimate=cost(0.1),
        name="tie",
    )(passed, arrived)


def key_back_kernel(split, *refs):
    rank_ref, modality_ref, head_ref, raw_ref, inner_in_ref, part_ref, weight_ref = refs[:7]
    grad_refs = refs[7:-3]
    out_ref, back_ref, inner_ref = refs[-3:]
    base = pl.multiple_of((1 - rank_ref[0]) * out_ref.shape[1], HEAD_DIM) if split else 0
    image = column(modality_ref[...]) > 0.0
    blocks = raw_ref.shape[1] // HEAD_DIM
    scaling = jnp.where(image, head_ref[1, 1:2, :], head_ref[0, 1:2, :])
    inner = jnp.zeros((raw_ref.shape[0], 1), f32)
    for b in range(blocks):
        part = slice(b * HEAD_DIM, (b + 1) * HEAD_DIM)
        raw = raw_ref[:, part]
        upstream = grad_refs[0][:, part].astype(f32)
        for grad_ref in grad_refs[1:]:
            upstream += grad_ref[:, part].astype(f32)
        is_key = (rank_ref[0] * blocks + b) % 2 == 0
        normed_back = norm_back(raw, inverse_norm(raw), scaling, upstream)
        back = jnp.where(is_key, normed_back, upstream).astype(bf16)
        back_ref[:, part] = back
        inner += jnp.sum(back.astype(f32) * raw, axis=1, keepdims=True)
    inner_ref[...] = inner_in_ref[...] + row_of(inner)
    for start, size in chunks_of(out_ref.shape[1], HEAD_DIM):
        place = pl.ds(base + start, size)
        product = both_back(image, back_ref[...], weight_ref[:, place, :])
        out_ref[:, start : start + size] = (product + part_ref[:, place]).astype(bf16)


def key_back_stage(rank, modality, head_gain, raw, inner, part, weights, grads, split):
    _, depth, width = weights.shape
    rows = raw.shape[0]
    return pl.pallas_call(
        functools.partial(key_back_kernel, split),
        out_shape=[
            jax.ShapeDtypeStruct((rows, depth // 2 if split else depth), bf16),
            jax.ShapeDtypeStruct((rows, width), bf16),
            jax.ShapeDtypeStruct((1, rows), f32),
        ],
        in_specs=[SMEM] + [VMEM] * (6 + len(grads)),
        out_specs=[VMEM] * 3,
        compiler_params=params(6),
        cost_estimate=cost(2),
        name="key_back_stage",
    )(rank, modality, head_gain, raw, inner, part, weights, *grads)


def kept_kernel(rank_ref, modality_ref, part_ref, weight_ref, back_ref, out_ref):
    base = pl.multiple_of(rank_ref[0] * out_ref.shape[1], HEAD_DIM)
    image = column(modality_ref[...]) > 0.0
    for start, size in chunks_of(out_ref.shape[1], HEAD_DIM):
        place = pl.ds(base + start, size)
        product = both_back(image, back_ref[...], weight_ref[:, place, :])
        out_ref[:, start : start + size] = product + part_ref[:, place]


def kept_stage(rank, modality, part, weights, back):
    return pl.pallas_call(
        kept_kernel,
        out_shape=jax.ShapeDtypeStruct((back.shape[0], weights.shape[1] // 2), f32),
        in_specs=[SMEM] + [VMEM] * 4,
        out_specs=VMEM,
        compiler_params=params(6),
        cost_estimate=cost(2),
        name="kept_stage",
    )(rank, modality, part, weights, back)


def finish_kernel(backs, inners, total_width, *refs):
    rank_ref, modality_ref, gain_ref, factor_ref, inputs_ref = refs[:5]
    back_refs = refs[5 : 5 + backs]
    inner_refs = refs[5 + backs : 5 + backs + inners]
    rest = refs[5 + backs + inners :]
    width = inputs_ref.shape[1]
    copies = []

    def send(staged_ref, out_ref, sem, part):
        copy = pltpu.make_async_copy(staged_ref.at[:, part], out_ref.at[:, part], sem)
        copy.start()
        copies.append(copy)

    pieces = [slice(start, start + size) for start, size in chunks_of(width, 896)]
    if len(rest) == 7:
        kept_ref, other_ref, attention_ref, out_ref, staged, staged_attention, sems = rest
        for index, part in enumerate(pieces):
            whole = kept_ref[:, part] + other_ref[:, part].astype(f32)
            staged_attention[:, part] = whole.astype(bf16)
            send(staged_attention, attention_ref, sems.at[1, index], part)
    else:
        out_ref, staged, sems = rest
    image = column(modality_ref[...]) > 0.0
    factor = column(factor_ref[...])
    inner = inner_refs[0][...]
    for ref in inner_refs[1:]:
        inner += ref[...]
    inner_mean = factor * column(inner) * (1.0 / total_width)
    gathered = gain_ref.shape[1] != width
    for index, part in enumerate(pieces):
        columns = part
        if gathered:
            first = pl.multiple_of(rank_ref[0] * width, HEAD_DIM) + part.start
            columns = pl.ds(first, part.stop - part.start)
        back = back_refs[0][:, part].astype(f32)
        for ref in back_refs[1:]:
            back += ref[:, part].astype(f32)
        rows = inputs_ref[:, part].astype(f32)
        result = factor * (gain_of(image, gain_ref, columns) * back - rows * inner_mean)
        staged[:, part] = result.astype(bf16)
        send(staged, out_ref, sems.at[0, index], part)
    for copy in copies:
        copy.wait()


def finish(rank, total_width, modality, gain, factor, inputs, backs, inners, projected):
    shape = jax.ShapeDtypeStruct(inputs.shape, bf16)
    arrays = [modality, gain, factor, inputs, *backs, *inners, *projected]
    count = 2 if projected else 1
    pieces = len(chunks_of(inputs.shape[1], 896))
    return pl.pallas_call(
        functools.partial(finish_kernel, len(backs), len(inners), total_width),
        out_shape=[shape] * count,
        in_specs=[SMEM] + [VMEM] * len(arrays),
        out_specs=[ANY] * count,
        scratch_shapes=[pltpu.VMEM(inputs.shape, bf16)] * count
        + [pltpu.SemaphoreType.DMA((count, pieces))],
        compiler_params=params(6),
        cost_estimate=cost(1),
        name="finish",
    )(rank, *arrays)


def local(
    inputs,
    cotangent,
    norm_gain,
    head_gain,
    query_weight,
    key_weight,
    output_weight,
    modality,
    segments,
    block_order,
):
    tensor_rank = lax.axis_index("tensor")
    block_rank = lax.axis_index("seq")
    tensor_count = lax.axis_size("tensor")
    block_count = lax.axis_size("seq")
    local_rows, local_width = inputs.shape
    full_width = local_width * tensor_count
    split = tensor_count == 2
    swap = [(0, 1), (1, 0)]
    rank = tensor_rank.astype(jnp.int32).reshape(1)
    modality = modality.reshape(1, local_rows)
    segments = segments.reshape(block_count, local_rows)

    def spread(part):
        if split:
            return [part, lax.ppermute(part, "tensor", swap)]
        return [lax.all_gather(part, "tensor", axis=1, tiled=True)]

    def scatter_columns(part):
        return lax.psum_scatter(part, "tensor", scatter_dimension=1, tiled=True)

    memory, key_raw, normed, row_factor = key_stage(
        rank, modality, norm_gain, head_gain, fetch(key_weight), spread(inputs)
    )
    shared = tensor_count > KV_HEADS
    is_even = tensor_rank % 2 == 0
    pair_swap = [(i, i ^ 1) for i in range(tensor_count)]
    if shared:
        partner = lax.ppermute(memory, "tensor", pair_swap)
        memory = jnp.where(
            is_even,
            jnp.concatenate([memory, partner], 1),
            jnp.concatenate([partner, memory], 1),
        )
    memories = [memory]
    for step in seq_steps(block_count):
        memories.append(lax.ppermute(memory, "seq", seq_pairs(step, block_count)))

    query, query_raw, back_attended = middle_stage(
        rank, modality, head_gain, normed, output_weight, query_weight, spread(cotangent)
    )
    attended, upstream, own_grad, *grads = attention_stage(
        block_rank.astype(jnp.int32).reshape(1),
        block_order,
        segments,
        query,
        back_attended,
        memories,
    )
    incoming = [
        lax.ppermute(grad, "seq", inverted(seq_pairs(step, block_count)))
        for step, grad in zip(seq_steps(block_count), grads)
    ]

    projected, gradient_part, inner = turn_stage(
        rank,
        modality,
        head_gain,
        output_weight,
        attended,
        upstream,
        query_raw,
        query_weight,
        split,
    )
    if split:
        passed = tie(projected[0], incoming[0])
        projected = [projected[1], lax.ppermute(passed, "tensor", swap)]
    else:
        attention_out = scatter_columns(projected[0])
        projected = []

    if shared:
        total = own_grad + sum(grad.astype(f32) for grad in incoming)
        low, high = total[:, :HEAD_DIM], total[:, HEAD_DIM:]
        outgoing = jnp.where(is_even, high, low).astype(bf16)
        sums = [jnp.where(is_even, low, high), lax.ppermute(outgoing, "tensor", pair_swap)]
    else:
        sums = [own_grad, *incoming]
    sent, slice_back, inner = key_back_stage(
        rank,
        modality,
        head_gain,
        key_raw,
        inner,
        gradient_part,
        key_weight,
        sums,
        split,
    )
    if split:
        inners = [inner, lax.ppermute(inner, "tensor", swap)]
        other = lax.ppermute(sent, "tensor", swap)
        kept = kept_stage(rank, modality, gradient_part, key_weight, slice_back)
        backs = [kept, other]
        gain = norm_gain
    else:
        inners = [lax.psum(inner, "tensor")]
        backs = [scatter_columns(sent)]
        gain = lax.dynamic_slice_in_dim(norm_gain, tensor_rank * local_width, local_width, 1)
    results = finish(
        rank, full_width, modality, gain, row_factor, inputs, backs, inners, projected
    )
    if split:
        attention_out = results[0]
    return (attention_out, results[-1])


def solution(mesh):
    return jax.shard_map(
        local,
        mesh=mesh,
        in_specs=(
            P(("dp", "seq"), "tensor"),
            P(("dp", "seq"), "tensor"),
            P(),
            P(),
            P(None, None, "tensor"),
            P(None, None, "tensor"),
            P(None, "tensor", None),
            P(("dp", "seq")),
            P("dp"),
            P("dp"),
        ),
        out_specs=(P(("dp", "seq"), "tensor"), P(("dp", "seq"), "tensor")),
        check_vma=False,
    )
```
